32 devices in a mesh: segment: 2 (over y), ctx: 4 (over z), tp: 4 (over x, core).
Axes of the slice: x: 2, y: 2, z: 4, core: 2. Of those that a mesh axis runs over, the one named last changes fastest.
Arguments:
- stash_inputs: bfloat16 [2, 4, 1024, 3840], P('segment', None, ('ctx', 'tp')), may hold values from -12 to 12
- stash_grads: bfloat16 [2, 4, 1024, 3840], P('segment', None, ('ctx', 'tp')), may hold values from -6 to 6
- plan: int32 [2, 4], P('segment'), may hold values from 0 to 3, each once within a row
- query_weight: bfloat16 [2, 2, 3840, 4096], P('segment', None, None, 'tp'), may hold values from -0.1 to 0.1
- key_weight: bfloat16 [2, 2, 3840, 2048], P('segment', None, None, 'tp'), may hold values from -0.1 to 0.1
- value_weight: bfloat16 [2, 2, 3840, 2048], P('segment', None, None, 'tp'), may hold values from -0.09375 to 0.09375
- out_weight: bfloat16 [2, 2, 4096, 3840], P('segment', None, 'tp'), may hold values from -0.09375 to 0.09375
- input_gain: float32 [2, 2, 3840], P('segment'), may hold values from 0.1 to 1.9
- output_gain: float32 [2, 2, 3840], P('segment'), may hold values from 0.1 to 1.9
- query_gain: float32 [2, 2, 256], P('segment'), may hold values from 0.5 to 6
- key_gain: float32 [2, 2, 256], P('segment'), may hold values from 0.5 to 6
Outputs:
- arrived_act: bfloat16 [2, 1024, 3840], P('segment', ('ctx', 'tp'))
- arrived_grad: bfloat16 [2, 1024, 3840], P('segment', ('ctx', 'tp'))
The draws below stay inside these ranges and needn't reach their ends.
Inputs may be any that keep to these rules, and one draw needn't show every extreme that they name: `plan`: row s names each of the 4 micro-batches once; its first entry is run forward and its second through its input gradient.
All inputs are finite; a program needn't handle non-finite values.
Results may differ from the reference program's by a relative error of at most 0.019.
The reference program's roundings to bfloat16 on the way count: a program that leaves them out, or rounds other values in their place, can miss the bound.
Values may be sent and summed in bfloat16 or wider, within the bound.
No kernel may reach another device: no remote copies, remote signals or barrier semaphores. Data moves between devices by JAX's collectives and lax.ppermute only.
A program may use at most 128 MiB of HBM per device.

```python
import math
import jax
import jax.numpy as jnp
from jax import lax

D = 3840
HEADS = 16
KV_HEADS = 8
HEAD_DIM = 256
WINDOW = 1024
TOK_DEV = 256
MICRO = 4
LEGS = 2
SEGMENTS = 2
TOKENS = 1024
N_CTX = 4
N_TP = 4


def draw_stash_inputs(key, part):
    base_key = jax.random.fold_in(key, 505)
    first_key, second_key = jax.random.split(base_key)
    shape = (SEGMENTS, MICRO, TOKENS, D)
    base = jax.random.normal(first_key, shape, jnp.float32)
    scales = 0.3 * jnp.exp(jax.random.uniform(second_key, (SEGMENTS, MICRO, TOKENS, 1), jnp.float32, 0.0, math.log(10.0)))
    return jnp.clip(base * scales, -12.0, 12.0).astype(jnp.bfloat16)


def query_base(key):
    base_key = jax.random.fold_in(key, 101)
    shape = (SEGMENTS, LEGS, D, HEADS * HEAD_DIM)
    base = jax.random.normal(base_key, shape, jnp.float32)
    return base * D ** (-0.5)


def draw_query_weight(key, part):
    return jnp.clip(query_base(key), -0.09, 0.09).astype(jnp.bfloat16)


def draw_key_weight(key, part):
    noise_key = jax.random.fold_in(key, 202)
    shape = (SEGMENTS, LEGS, D, KV_HEADS * HEAD_DIM)
    result = jax.random.normal(noise_key, shape, jnp.float32) * D ** (-0.5)
    return jnp.clip(result, -0.09, 0.09).astype(jnp.bfloat16)


def gain_values(key, salt):
    gain_key = jax.random.fold_in(key, salt)
    shape = (SEGMENTS, LEGS, HEAD_DIM)
    return jnp.exp(jax.random.uniform(gain_key, shape, jnp.float32, math.log(0.5), math.log(2.0)))


def draw_query_gain(key, part):
    return gain_values(key, 303)


def draw_key_gain(key, part):
    return gain_values(key, 404)


def shard_levels(rng, extent, shards, smallest, largest):
    def one(axis_at, parts):
        steps = jax.random.uniform(jax.random.fold_in(jax.random.fold_in(rng, 6), axis_at), (parts,), jnp.float32, smallest / len(shards), largest / len(shards))
        return jnp.repeat(jnp.exp(steps), extent[axis_at] // parts).reshape((-1,) + (1,) * (len(extent) - axis_at - 1))

    level = one(*shards[0])
    for cut in shards[1:]:
        level = level * one(*cut)
    return level


def normal_values(rng, dims, spread, limit, shards=(), kind=jnp.bfloat16):
    values = jax.random.normal(rng, dims, jnp.float32) * spread
    if len(shards) > 0:
        values = shard_levels(rng, dims, shards, -0.22, 0.18) * values
    return jnp.clip(values, min=-limit, max=limit).astype(kind)


def setup_inputs(seed: int = 0) -> dict:
    arg_keys = jax.random.split(jax.random.key(seed), 12)
    stash_inputs = draw_stash_inputs(jax.random.fold_in(arg_keys[11], 71), 0)
    stash_grads = normal_values(arg_keys[1], (SEGMENTS, MICRO, TOKENS, D), 1.0, 6.0, ((0, 2), (2, 16)))
    plan = jax.vmap(lambda own: jax.random.permutation(own, MICRO))(jax.random.split(arg_keys[2], SEGMENTS)).reshape((SEGMENTS, MICRO)).astype(jnp.int32)
    query_weight = draw_query_weight(jax.random.fold_in(arg_keys[11], 71), 0)
    key_weight = draw_key_weight(jax.random.fold_in(arg_keys[11], 71), 0)
    value_weight = normal_values(arg_keys[5], (SEGMENTS, LEGS, D, KV_HEADS * HEAD_DIM), D ** -0.5, 0.09375, ((0, 2), (3, 4)))
    out_weight = normal_values(arg_keys[6], (SEGMENTS, LEGS, HEADS * HEAD_DIM, D), (HEADS * HEAD_DIM) ** -0.5, 0.09375, ((0, 2), (2, 4)))
    input_gain = jnp.clip(1.0 + 0.18 * jax.random.normal(arg_keys[7], (SEGMENTS, LEGS, D), jnp.float32), 0.1, 1.9)
    output_gain = jnp.clip(1.0 + 0.18 * jax.random.normal(arg_keys[8], (SEGMENTS, LEGS, D), jnp.float32), 0.1, 1.9)
    query_gain = draw_query_gain(jax.random.fold_in(arg_keys[11], 71), 0)
    key_gain = draw_key_gain(jax.random.fold_in(arg_keys[11], 71), 0)
    return {"stash_inputs": stash_inputs, "stash_grads": stash_grads, "plan": plan, "query_weight": query_weight, "key_weight": key_weight, "value_weight": value_weight, "out_weight": out_weight, "input_gain": input_gain, "output_gain": output_gain, "query_gain": query_gain, "key_gain": key_gain}


epsilon = 1e-06
rope_base = 10000.0
masked_score = -1e+30

def rms_scale(operand, gain):
    return operand * lax.rsqrt(lax.optimization_barrier(jnp.mean(operand * operand, axis=-1, keepdims=True)) + epsilon) * gain

def rotate(normed, positions):
    half_width = normed.shape[-1] // 2
    frequency = rope_base ** (-(jnp.arange(half_width).astype(normed.dtype) * 2.0 / normed.shape[-1]))
    angles = positions.astype(normed.dtype)[:, None] * frequency[None, :]
    cosine = jnp.cos(angles)[:, None, :]
    sines = jnp.sin(angles)[:, None, :]
    front_half = normed[..., :half_width]
    back_half = normed[..., half_width:]
    return jnp.concatenate([front_half * cosine - back_half * sines, back_half * cosine + front_half * sines], axis=-1)

def head_norm(raw_heads, gain, positions):
    return rotate(rms_scale(raw_heads, gain), positions)

def block_probs(query_block, key_block, query_place, key_place):
    groups = HEADS // KV_HEADS
    grouped = query_block.reshape(query_block.shape[0], KV_HEADS, groups, HEAD_DIM).astype(jnp.float32)
    scores = jnp.einsum('tkgd,skd->kgts', grouped, key_block.astype(jnp.float32)) * HEAD_DIM ** (-0.5)
    visible = (key_place[None, :] >= 0) & (key_place[None, :] <= query_place[:, None]) & (key_place[None, :] > query_place[:, None] - WINDOW)
    scores = jnp.where(visible, scores, masked_score)
    highest = lax.optimization_barrier(jnp.max(scores, axis=-1, keepdims=True))
    raised = jnp.exp(scores - highest)
    return raised / lax.optimization_barrier(jnp.sum(raised, axis=-1, keepdims=True))

def padded(rows_in):
    return jnp.concatenate([jnp.zeros((WINDOW, KV_HEADS, HEAD_DIM), rows_in.dtype), rows_in], axis=0)

def block_slices(queries, key_pad, value_pad, start):
    query_block = lax.dynamic_slice_in_dim(queries, start, TOK_DEV, 0)
    key_block = lax.dynamic_slice_in_dim(key_pad, start, WINDOW + TOK_DEV, 0)
    value_block = lax.dynamic_slice_in_dim(value_pad, start, WINDOW + TOK_DEV, 0)
    query_place = start + jnp.arange(TOK_DEV, dtype=jnp.int32)
    key_place = start - WINDOW + jnp.arange(WINDOW + TOK_DEV, dtype=jnp.int32)
    return (query_block, key_block, value_block, query_place, key_place)

def attention_out(queries, keys, values):
    key_pad = padded(keys)
    value_pad = padded(values)
    starts = jnp.arange(N_CTX, dtype=jnp.int32) * TOK_DEV

    def per_block(start):
        query_block, key_block, value_block, query_place, key_place = block_slices(queries, key_pad, value_pad, start)
        probs = block_probs(query_block, key_block, query_place, key_place)
        weighting_low = lax.optimization_barrier(probs.astype(jnp.bfloat16)).astype(jnp.float32)
        context = jnp.einsum('kgts,skd->tkgd', weighting_low, value_block.astype(jnp.float32))
        return context.astype(jnp.bfloat16).reshape(TOK_DEV, HEADS * HEAD_DIM)
    blocks = lax.map(per_block, starts)
    return blocks.reshape(N_CTX * TOK_DEV, HEADS * HEAD_DIM)

def attention_back(queries, keys, values, context_grad):
    key_pad = padded(keys)
    value_pad = padded(values)
    groups = HEADS // KV_HEADS
    grad_grouped = context_grad.reshape(context_grad.shape[0], KV_HEADS, groups, HEAD_DIM)
    starts = jnp.arange(N_CTX, dtype=jnp.int32) * TOK_DEV

    def per_block(carried, start):
        key_acc, value_acc = carried
        query_block, key_block, value_block, query_place, key_place = block_slices(queries, key_pad, value_pad, start)
        grad_block = lax.dynamic_slice_in_dim(grad_grouped, start, TOK_DEV, 0).astype(jnp.float32)
        probs = block_probs(query_block, key_block, query_place, key_place)
        weighting_low = lax.optimization_barrier(probs.astype(jnp.bfloat16)).astype(jnp.float32)
        weight_grad = jnp.einsum('tkgd,skd->kgts', grad_block, value_block.astype(jnp.float32))
        score_grad = probs * (weight_grad - lax.optimization_barrier(jnp.sum(weight_grad * probs, axis=-1, keepdims=True))) * HEAD_DIM ** (-0.5)
        score_grad = lax.optimization_barrier(score_grad.astype(jnp.bfloat16)).astype(jnp.float32)
        grouped = query_block.reshape(TOK_DEV, KV_HEADS, groups, HEAD_DIM).astype(jnp.float32)
        query_grad = jnp.einsum('kgts,skd->tkgd', score_grad, key_block.astype(jnp.float32)).reshape(TOK_DEV, HEADS, HEAD_DIM)
        key_grad = jnp.einsum('kgts,tkgd->skd', score_grad, grouped)
        value_grad = jnp.einsum('kgts,tkgd->skd', weighting_low, grad_block)
        key_acc = lax.dynamic_update_slice_in_dim(key_acc, lax.dynamic_slice_in_dim(key_acc, start, WINDOW + TOK_DEV, 0) + key_grad, start, 0)
        value_acc = lax.dynamic_update_slice_in_dim(value_acc, lax.dynamic_slice_in_dim(value_acc, start, WINDOW + TOK_DEV, 0) + value_grad, start, 0)
        return ((key_acc, value_acc), query_grad)
    zeros_pad = jnp.zeros((WINDOW + N_CTX * TOK_DEV, KV_HEADS, HEAD_DIM), jnp.float32)
    (key_acc, value_acc), query_grad = lax.scan(per_block, (zeros_pad, zeros_pad), starts)
    return (query_grad.reshape(N_CTX * TOK_DEV, HEADS, HEAD_DIM), key_acc[WINDOW:], value_acc[WINDOW:])

def group_sum(group_term, token_count):

    def add_group(group, running):
        partial_term = group_term(group.astype(jnp.int32))
        return running + lax.optimization_barrier(partial_term.astype(jnp.bfloat16)).astype(jnp.float32)
    return lax.fori_loop(0, N_TP, add_group, jnp.zeros((token_count, D), jnp.float32))

def layer_front(layer_input, query_proj, key_proj, value_proj, in_gain, q_gain, k_gain):
    token_count = layer_input.shape[0]
    wide_input = layer_input.astype(jnp.float32)
    normed = rms_scale(wide_input, in_gain).astype(jnp.bfloat16)
    positions = jnp.arange(token_count, dtype=jnp.int32)
    query_raw = jnp.dot(normed, query_proj, preferred_element_type=jnp.float32).reshape(token_count, HEADS, HEAD_DIM)
    key_raw = jnp.dot(normed, key_proj, preferred_element_type=jnp.float32).reshape(token_count, KV_HEADS, HEAD_DIM)
    values = jnp.dot(normed, value_proj, preferred_element_type=jnp.float32).astype(jnp.bfloat16).reshape(token_count, KV_HEADS, HEAD_DIM)
    queries = head_norm(query_raw, q_gain, positions).astype(jnp.bfloat16)
    keys = head_norm(key_raw, k_gain, positions).astype(jnp.bfloat16)
    return (wide_input, positions, query_raw, key_raw, queries, keys, values)

def out_sum(context, out_proj):
    query_cols = HEADS * HEAD_DIM // N_TP

    def group_term(group):
        return jnp.dot(lax.dynamic_slice_in_dim(context, group * query_cols, query_cols, 1), lax.dynamic_slice_in_dim(out_proj, group * query_cols, query_cols, 0), preferred_element_type=jnp.float32)
    return group_sum(group_term, context.shape[0])

def forward_layer(layer_input, query_proj, key_proj, value_proj, out_proj, in_gain, post_gain, q_gain, k_gain):
    wide_input, positions, query_raw, key_raw, queries, keys, values = layer_front(layer_input, query_proj, key_proj, value_proj, in_gain, q_gain, k_gain)
    projected = out_sum(attention_out(queries, keys, values), out_proj)
    return (wide_input + rms_scale(projected, post_gain)).astype(jnp.bfloat16)

def backward_layer(layer_input, incoming, query_proj, key_proj, value_proj, out_proj, in_gain, post_gain, q_gain, k_gain):
    wide_input, positions, query_raw, key_raw, queries, keys, values = layer_front(layer_input, query_proj, key_proj, value_proj, in_gain, q_gain, k_gain)
    token_count = layer_input.shape[0]
    projected = out_sum(attention_out(queries, keys, values), out_proj)
    wide_grad = incoming.astype(jnp.float32)
    out_grad = jax.vjp(lambda operand: rms_scale(operand, post_gain), projected)[1](wide_grad)[0].astype(jnp.bfloat16)
    context_grad = jnp.dot(out_grad, out_proj.T, preferred_element_type=jnp.float32).astype(jnp.bfloat16)
    query_grad, key_grad, value_grad = attention_back(queries, keys, values, context_grad)
    query_low = jax.vjp(lambda operand: head_norm(operand, q_gain, positions), query_raw)[1](query_grad)[0].astype(jnp.bfloat16).reshape(token_count, HEADS * HEAD_DIM)
    key_low = jax.vjp(lambda operand: head_norm(operand, k_gain, positions), key_raw)[1](key_grad)[0].astype(jnp.bfloat16).reshape(token_count, KV_HEADS * HEAD_DIM)
    value_low = value_grad.astype(jnp.bfloat16).reshape(token_count, KV_HEADS * HEAD_DIM)
    query_cols = HEADS * HEAD_DIM // N_TP
    key_cols = KV_HEADS * HEAD_DIM // N_TP

    def group_term(group):
        summed = jnp.dot(lax.dynamic_slice_in_dim(query_low, group * query_cols, query_cols, 1), lax.dynamic_slice_in_dim(query_proj, group * query_cols, query_cols, 1).T, preferred_element_type=jnp.float32)
        summed = summed + jnp.dot(lax.dynamic_slice_in_dim(key_low, group * key_cols, key_cols, 1), lax.dynamic_slice_in_dim(key_proj, group * key_cols, key_cols, 1).T, preferred_element_type=jnp.float32)
        summed = summed + jnp.dot(lax.dynamic_slice_in_dim(value_low, group * key_cols, key_cols, 1), lax.dynamic_slice_in_dim(value_proj, group * key_cols, key_cols, 1).T, preferred_element_type=jnp.float32)
        return summed
    hidden_grad = group_sum(group_term, token_count)
    outgoing = wide_grad + jax.vjp(lambda operand: rms_scale(operand, in_gain), wide_input)[1](hidden_grad)[0]
    return outgoing.astype(jnp.bfloat16)

def reference(stash_inputs, stash_grads, plan, query_weight, key_weight, value_weight, out_weight, input_gain, output_gain, query_gain, key_gain):
    forward_rows = []
    backward_rows = []
    for segment_index in range(SEGMENTS):
        forward_batch = plan[segment_index, 0]
        backward_batch = plan[segment_index, 1]

        def layer_set(leg_index):
            return (query_weight[segment_index, leg_index], key_weight[segment_index, leg_index], value_weight[segment_index, leg_index], out_weight[segment_index, leg_index], input_gain[segment_index, leg_index], output_gain[segment_index, leg_index], query_gain[segment_index, leg_index], key_gain[segment_index, leg_index])
        forward_in = lax.dynamic_index_in_dim(stash_inputs[segment_index], forward_batch, 0, keepdims=False)
        backward_in = lax.dynamic_index_in_dim(stash_inputs[segment_index], backward_batch, 0, keepdims=False)
        incoming = lax.dynamic_index_in_dim(stash_grads[segment_index], backward_batch, 0, keepdims=False)
        forward_rows.append(forward_layer(forward_in, *layer_set(segment_index)))
        backward_rows.append(backward_layer(backward_in, incoming, *layer_set(1 - segment_index)))
    arrived_act = jnp.stack(forward_rows[::-1])
    arrived_grad = jnp.stack(backward_rows[::-1])
    return (arrived_act, arrived_grad)
```

```python
import functools

import jax
import jax.numpy as jnp
from jax import lax
from jax.experimental import pallas as pl
from jax.experimental.pallas import tpu as pltpu
from jax.sharding import PartitionSpec as P

WINDOW = 1024

epsilon = 1e-06
rope_base = 10000.0
masked_score = -1e30
mebibyte = 1024 * 1024
f32 = jnp.float32
bf16 = jnp.bfloat16

whole = pl.BlockSpec(memory_space=pltpu.VMEM)
scalars = pl.BlockSpec(memory_space=pltpu.SMEM)
anywhere = pl.BlockSpec(memory_space=pl.ANY)
far_memory = pl.BlockSpec(memory_space=pltpu.HBM)


def params(mebibytes):
    return pltpu.CompilerParams(vmem_limit_bytes=int(mebibytes * mebibyte))


class Stream:
    def __init__(self, copies):
        self.copies = copies
        for copy in copies[:2]:
            copy.start()

    def wait(self, at):
        self.copies[at].wait()
        if at + 2 < len(self.copies):
            self.copies[at + 2].start()


def cost(flops, bytes_accessed):
    return pl.CostEstimate(flops=int(flops), bytes_accessed=int(bytes_accessed), transcendentals=0)


def widest_tile(width, limit=1024):
    best = 128
    for tile in range(128, limit + 1, 128):
        if width % tile == 0:
            best = tile
    return best


def mean_square_scale(value):
    return lax.rsqrt(jnp.mean(value * value, axis=-1, keepdims=True) + epsilon)


def norm_back(value, gain, grad):
    scale = mean_square_scale(value)
    weighted = grad * gain
    inner = jnp.mean(value * weighted, axis=-1, keepdims=True)
    return scale * weighted - value * (scale * scale * scale * inner)


def norm_kernel(picks, rows, gain, out, held, sem):
    copy = pltpu.make_async_copy(rows.at[0, picks[0]], held, sem)
    copy.start()
    gain_row = gain[0, pl.ds(picks[1], 1), :]
    copy.wait()
    value = held[...].astype(f32)
    out[...] = (value * mean_square_scale(value) * gain_row).astype(bf16)


def norm_rows(picks, stash, gain):
    rows, width = stash.shape[-2:]
    return pl.pallas_call(
        norm_kernel,
        out_shape=jax.ShapeDtypeStruct((rows, width), bf16),
        in_specs=[scalars, far_memory, whole],
        out_specs=whole,
        scratch_shapes=[pltpu.VMEM((rows, width), bf16), pltpu.SemaphoreType.DMA],
        compiler_params=params(8),
        cost_estimate=cost(0, 4 * rows * width),
        name="norm_rows",
    )(picks, stash, gain)


def qkv_kernel(count, keep_raw, *refs):
    picks = refs[0]
    pieces = refs[1 : 1 + count]
    cosine, sine, q_gain, k_gain, wq, wk, wv = refs[1 + count : 8 + count]
    outs = refs[8 + count :]
    if keep_raw:
        q_out, kv_out, q_raw, k_raw, act, wbuf, act_sem, w_sem = outs
    else:
        q_out, kv_out, act, wbuf, act_sem, w_sem = outs
    leg = picks[1]
    head = q_gain.shape[-1]
    rows = pieces[0].shape[0]
    q_heads = wq.shape[-1] // head
    k_heads = wk.shape[-1] // head
    tiles = []
    for kind, weight, heads in (("k", wk, k_heads), ("v", wv, k_heads), ("q", wq, q_heads)):
        for at in range(heads):
            tiles.append((kind, weight, at))
    act_copies = []
    for at, piece in enumerate(pieces):
        copy = pltpu.make_async_copy(piece, act.at[pl.ds(at * rows, rows)], act_sem.at[at])
        copy.start()
        act_copies.append(copy)
    slots = wbuf.shape[0]
    stream = Stream(
        [
            pltpu.make_async_copy(
                weight.at[0, leg, :, pl.ds(h * head, head)], wbuf.at[at % slots], w_sem.at[at]
            )
            for at, (kind, weight, h) in enumerate(tiles)
        ]
    )
    for copy in act_copies:
        copy.wait()
    gains = {
        "q": q_gain[0, pl.ds(leg, 1), :],
        "k": k_gain[0, pl.ds(leg, 1), :],
    }
    cos = cosine[...]
    sin = sine[...]
    half = head // 2
    for at, (kind, weight, h) in enumerate(tiles):
        stream.wait(at)
        raw = jnp.dot(act[...], wbuf[at % slots], preferred_element_type=f32)
        cols = pl.ds(h * head, head)
        if kind == "v":
            kv_out[:, pl.ds((k_heads + h) * head, head)] = raw.astype(bf16)
            continue
        if keep_raw:
            (q_raw if kind == "q" else k_raw)[:, cols] = raw
        normed = raw * mean_square_scale(raw) * gains[kind]
        front = normed[:, :half]
        back = normed[:, half:]
        target = q_out if kind == "q" else kv_out
        target[:, pl.ds(h * head, half)] = (front * cos - back * sin).astype(bf16)
        target[:, pl.ds(h * head + half, half)] = (back * cos + front * sin).astype(bf16)


def project(picks, pieces, tables, q_gain, k_gain, wq, wk, wv, keep_raw):
    rows, width = pieces[0].shape
    total = rows * len(pieces)
    head = q_gain.shape[-1]
    q_cols, k_cols = wq.shape[-1], wk.shape[-1]
    count = (q_cols + 2 * k_cols) // head
    shapes = [
        jax.ShapeDtypeStruct((total, q_cols), bf16),
        jax.ShapeDtypeStruct((total, 2 * k_cols), bf16),
    ]
    if keep_raw:
        shapes += [
            jax.ShapeDtypeStruct((total, q_cols), f32),
            jax.ShapeDtypeStruct((total, k_cols), f32),
        ]
    return pl.pallas_call(
        functools.partial(qkv_kernel, len(pieces), keep_raw),
        out_shape=shapes,
        in_specs=[scalars] + [anywhere] * len(pieces) + [whole] * 4 + [far_memory] * 3,
        out_specs=[whole] * len(shapes),
        scratch_shapes=[
            pltpu.VMEM((total, width), bf16),
            pltpu.VMEM((3, width, head), bf16),
            pltpu.SemaphoreType.DMA((len(pieces),)),
            pltpu.SemaphoreType.DMA((count,)),
        ],
        compiler_params=params(57),
        cost_estimate=cost(2 * total * width * count * head, 2 * width * count * head),
        name="project_heads",
    )(picks, *pieces, *tables, q_gain, k_gain, wq, wk, wv)


def visibility(query_place, key_place):
    seen = (
        (key_place >= 0) & (key_place <= query_place) & (key_place > query_place - WINDOW)
    )
    return jnp.where(seen, 0.0, masked_score).astype(f32)


def weights_of(queries, chunks, key_at, head, bias, scores):
    start = 0
    for chunk in chunks:
        size = chunk.shape[0]
        scores[:, pl.ds(start, size)] = lax.dot_general(
            queries,
            chunk[:, pl.ds(key_at * head, head)],
            (((1,), (1,)), ((), ())),
            preferred_element_type=f32,
        )
        start += size
    value = scores[...] * head ** (-0.5) + bias
    raised = jnp.exp(value - jnp.max(value, axis=-1, keepdims=True))
    return raised * (1.0 / jnp.sum(raised, axis=-1, keepdims=True))


def write_split(out_pair, groups, cores, rows, at, tile, value):
    for g in range(groups):
        for k in range(cores):
            begin = (g * cores + k) * rows
            out_pair[k][pl.ds(g * rows, rows), pl.ds(at * tile, tile)] = value[
                begin : begin + rows
            ].astype(bf16)


def attend_kernel(count, cores, rows, with_weights, head, *refs):
    picks, queries = refs[:2]
    chunks = refs[2 : 2 + count]
    query_place, key_place, wo = refs[2 + count : 5 + count]
    outs = refs[5 + count : 5 + count + cores]
    rest = refs[5 + count + cores :]
    scores, context, wbuf, w_sem = rest[-4:]
    leg = picks[1]
    tile = wbuf.shape[-1]
    tiles = wbuf.shape[0]
    copies = []
    for at in range(tiles):
        copy = pltpu.make_async_copy(
            wo.at[0, leg, :, pl.ds(at * tile, tile)], wbuf.at[at], w_sem.at[at]
        )
        copy.start()
        copies.append(copy)
    k_heads = chunks[0].shape[-1] // (2 * head)
    q_heads = queries.shape[-1] // head
    bias = visibility(query_place[...], key_place[...])
    for h in range(q_heads):
        key_at = h * k_heads // q_heads
        weights = weights_of(
            queries[:, pl.ds(h * head, head)], chunks, key_at, head, bias, scores
        )
        low = weights.astype(bf16)
        start = 0
        total = None
        for chunk in chunks:
            size = chunk.shape[0]
            term = jnp.dot(
                low[:, start : start + size],
                chunk[:, pl.ds((k_heads + key_at) * head, head)],
                preferred_element_type=f32,
            )
            total = term if total is None else total + term
            start += size
        context[:, pl.ds(h * head, head)] = total.astype(bf16)
    groups = queries.shape[0] // (cores * rows)
    for at in range(tiles):
        copies[at].wait()
        value = jnp.dot(context[...], wbuf[at], preferred_element_type=f32)
        write_split(outs, groups, cores, rows, at, tile, value)


def attend(picks, queries, chunks, query_place, key_place, wo, head, rows, cores):
    total, q_cols = queries.shape
    keys = sum(chunk.shape[0] for chunk in chunks)
    width = wo.shape[-1]
    tile = widest_tile(width)
    shape = jax.ShapeDtypeStruct((total // cores, width), bf16)
    return pl.pallas_call(
        functools.partial(attend_kernel, len(chunks), cores, rows, False, head),
        out_shape=[shape] * cores,
        in_specs=[scalars] + [whole] * (len(chunks) + 3) + [far_memory],
        out_specs=[whole] * cores,
        scratch_shapes=[
            pltpu.VMEM((total, keys), f32),
            pltpu.VMEM((total, q_cols), bf16),
            pltpu.VMEM((width // tile, q_cols, tile), bf16),
            pltpu.SemaphoreType.DMA((width // tile,)),
        ],
        compiler_params=params(57),
        cost_estimate=cost(
            4 * total * keys * q_cols + 2 * total * q_cols * width, 2 * q_cols * width
        ),
        name="attend_and_project",
    )(picks, queries, *chunks, query_place, key_place, wo)


def summed(terms):
    total = terms[0][...].astype(f32)
    for term in terms[1:]:
        total = total + term[...].astype(f32)
    return total


def out_grad_kernel(count, picks, *refs):
    terms = refs[:count]
    grads, gain, out, held, sem = refs[count:]
    copy = pltpu.make_async_copy(grads.at[0, picks[0]], held, sem)
    copy.start()
    projected = summed(terms)
    gain_row = gain[0, pl.ds(picks[1], 1), :]
    copy.wait()
    out[...] = norm_back(projected, gain_row, held[...].astype(f32)).astype(bf16)


def forward_out_kernel(count, picks, *refs):
    terms = refs[:count]
    stash, gain, out, held, sem = refs[count:]
    copy = pltpu.make_async_copy(stash.at[0, picks[0]], held, sem)
    copy.start()
    projected = summed(terms)
    gain_row = gain[0, pl.ds(picks[1], 1), :]
    value = projected * mean_square_scale(projected) * gain_row
    copy.wait()
    out[...] = (held[...].astype(f32) + value).astype(bf16)


def row_call(body, picks, terms, stash, gain, name):
    rows, width = stash.shape[-2:]
    return pl.pallas_call(
        functools.partial(body, len(terms)),
        out_shape=jax.ShapeDtypeStruct((rows, width), bf16),
        in_specs=[scalars] + [whole] * len(terms) + [far_memory, whole],
        out_specs=whole,
        scratch_shapes=[pltpu.VMEM((rows, width), bf16), pltpu.SemaphoreType.DMA],
        compiler_params=params(8),
        cost_estimate=cost(0, 2 * rows * width * (len(terms) + 2)),
        name=name,
    )(picks, *terms, stash, gain)


def outgoing_kernel(count, picks, *refs):
    terms = refs[:count]
    stash, grads, gain, out, held, grad_held, sem = refs[count:]
    first = pltpu.make_async_copy(stash.at[0, picks[0]], held, sem.at[0])
    second = pltpu.make_async_copy(grads.at[0, picks[0]], grad_held, sem.at[1])
    first.start()
    second.start()
    hidden = summed(terms)
    gain_row = gain[0, pl.ds(picks[1], 1), :]
    first.wait()
    value = norm_back(held[...].astype(f32), gain_row, hidden)
    second.wait()
    out[...] = (grad_held[...].astype(f32) + value).astype(bf16)


def outgoing_rows(picks, terms, stash, grads, gain):
    rows, width = stash.shape[-2:]
    return pl.pallas_call(
        functools.partial(outgoing_kernel, len(terms)),
        out_shape=jax.ShapeDtypeStruct((rows, width), bf16),
        in_specs=[scalars] + [whole] * len(terms) + [far_memory, far_memory, whole],
        out_specs=whole,
        scratch_shapes=[
            pltpu.VMEM((rows, width), bf16),
            pltpu.VMEM((rows, width), bf16),
            pltpu.SemaphoreType.DMA((2,)),
        ],
        compiler_params=params(8),
        cost_estimate=cost(0, 2 * rows * width * (len(terms) + 3)),
        name="outgoing_rows",
    )(picks, *terms, stash, grads, gain)


def head_back(raw, gain_row, cos, sin, grad):
    half = grad.shape[-1] // 2
    front = grad[:, :half]
    back = grad[:, half:]
    turned = jnp.concatenate([front * cos + back * sin, back * cos - front * sin], axis=-1)
    return norm_back(raw, gain_row, turned)


def attend_back_kernel(pieces_count, count, head, *refs):
    picks = refs[0]
    pieces = refs[1 : 1 + pieces_count]
    queries, q_raw = refs[1 + pieces_count : 3 + pieces_count]
    chunks = refs[3 + pieces_count : 3 + pieces_count + count]
    (query_place, key_place, cosine, sine, q_gain, wo) = refs[
        3 + pieces_count + count : 9 + pieces_count + count
    ]
    outs = refs[9 + pieces_count + count :]
    query_low = outs[0]
    grads = outs[1 : 1 + count]
    scores, act, context_grad, wbuf, act_sem, w_sem = outs[1 + count :]
    leg = picks[1]
    rows = pieces[0].shape[0]
    act_copies = []
    for at, piece in enumerate(pieces):
        copy = pltpu.make_async_copy(piece, act.at[pl.ds(at * rows, rows)], act_sem.at[at])
        copy.start()
        act_copies.append(copy)
    k_heads = chunks[0].shape[-1] // (2 * head)
    q_heads = queries.shape[-1] // head
    stream = Stream(
        [
            pltpu.make_async_copy(
                wo.at[0, leg, pl.ds(at * head, head), :], wbuf.at[at], w_sem.at[at]
            )
            for at in range(q_heads)
        ]
    )
    bias = visibility(query_place[...], key_place[...])
    gain_row = q_gain[0, pl.ds(leg, 1), :]
    cos = cosine[...]
    sin = sine[...]
    for copy in act_copies:
        copy.wait()
    for h in range(q_heads):
        stream.wait(h)
        context_grad[:, pl.ds(h * head, head)] = lax.dot_general(
            act[...], wbuf[h], (((1,), (1,)), ((), ())), preferred_element_type=f32
        ).astype(bf16)
    for h in range(q_heads):
        key_at = h * k_heads // q_heads
        first = h == 0 or (h - 1) * k_heads // q_heads != key_at
        query = queries[:, pl.ds(h * head, head)]
        upper = context_grad[:, pl.ds(h * head, head)]
        weights = weights_of(query, chunks, key_at, head, bias, scores)
        start = 0
        for chunk in chunks:
            size = chunk.shape[0]
            scores[:, pl.ds(start, size)] = lax.dot_general(
                upper,
                chunk[:, pl.ds((k_heads + key_at) * head, head)],
                (((1,), (1,)), ((), ())),
                preferred_element_type=f32,
            )
            start += size
        weight_grad = scores[...]
        inner = jnp.sum(weight_grad * weights, axis=-1, keepdims=True)
        score_grad = (weights * (weight_grad - inner) * head ** (-0.5)).astype(bf16)
        low = weights.astype(bf16)
        query_grad = None
        start = 0
        for chunk, grad in zip(chunks, grads):
            size = chunk.shape[0]
            part = score_grad[:, start : start + size]
            term = jnp.dot(
                part, chunk[:, pl.ds(key_at * head, head)], preferred_element_type=f32
            )
            query_grad = term if query_grad is None else query_grad + term
            key_term = lax.dot_general(
                part, query, (((0,), (0,)), ((), ())), preferred_element_type=f32
            )
            value_term = lax.dot_general(
                low[:, start : start + size],
                upper,
                (((0,), (0,)), ((), ())),
                preferred_element_type=f32,
            )
            key_cols = pl.ds(key_at * head, head)
            value_cols = pl.ds((k_heads + key_at) * head, head)
            if first:
                grad[:, key_cols] = key_term
                grad[:, value_cols] = value_term
            else:
                grad[:, key_cols] += key_term
                grad[:, value_cols] += value_term
            start += size
        query_low[:, pl.ds(h * head, head)] = head_back(
            q_raw[:, pl.ds(h * head, head)], gain_row, cos, sin, query_grad
        ).astype(bf16)


def attend_back(
    picks, pieces, queries, q_raw, chunks, query_place, key_place, tables, q_gain, wo
):
    total, q_cols = queries.shape
    head = q_gain.shape[-1]
    keys = sum(chunk.shape[0] for chunk in chunks)
    width = wo.shape[-1]
    shapes = [jax.ShapeDtypeStruct((total, q_cols), bf16)] + [
        jax.ShapeDtypeStruct(chunk.shape, f32) for chunk in chunks
    ]
    return pl.pallas_call(
        functools.partial(attend_back_kernel, len(pieces), len(chunks), head),
        out_shape=shapes,
        in_specs=[scalars]
        + [anywhere] * len(pieces)
        + [whole] * (2 + len(chunks) + 5)
        + [far_memory],
        out_specs=[whole] * len(shapes),
        scratch_shapes=[
            pltpu.VMEM((total, keys), f32),
            pltpu.VMEM((total, width), bf16),
            pltpu.VMEM((total, q_cols), bf16),
            pltpu.VMEM((q_cols // head, head, width), bf16),
            pltpu.SemaphoreType.DMA((len(pieces),)),
            pltpu.SemaphoreType.DMA((q_cols // head,)),
        ],
        compiler_params=params(57),
        cost_estimate=cost(
            10 * total * keys * q_cols + 2 * total * q_cols * width, 2 * q_cols * width
        ),
        name="attend_back",
    )(picks, *pieces, queries, q_raw, *chunks, query_place, key_place, *tables, q_gain, wo)


def key_value_low(own, received, k_raw, gain_row, cos, sin, head, key_low, value_low):
    k_cols = k_raw.shape[-1]
    for h in range(k_cols // head):
        cols = pl.ds(h * head, head)
        grad = own[:, cols] + received[:, cols].astype(f32)
        key_low[:, cols] = head_back(k_raw[:, cols], gain_row, cos, sin, grad).astype(bf16)
    value_cols = pl.ds(k_cols, k_cols)
    value_low[...] = (own[:, value_cols] + received[:, value_cols].astype(f32)).astype(bf16)


def weight_rows(leg, pairs, sem, tile, tiles):
    streams = []
    for j, (weight, buffer) in enumerate(pairs):
        slots = buffer.shape[0]
        streams.append(
            Stream(
                [
                    pltpu.make_async_copy(
                        weight.at[0, leg, pl.ds(at * tile, tile), :],
                        buffer.at[at % slots],
                        sem.at[j, at],
                    )
                    for at in range(tiles)
                ]
            )
        )
    return streams


contract_last = (((1,), (1,)), ((), ()))


def hidden_kernel(cores, rows, head, near, *refs):
    picks, query_part, own, received, k_raw, cosine, sine, k_gain = refs[:8]
    rest = refs[8:]
    leg = picks[1]
    if near is None:
        wk, wv, wq, near_part = rest[:4]
        outs = rest[4 : 4 + cores]
        key_low, value_low, bk, bv, bq, sem = rest[4 + cores :]
        pairs = ((wk, bk), (wv, bv), (wq, bq))
    else:
        wk, wv = rest[:2]
        outs = rest[2 : 2 + cores]
        key_low, value_low, bk, bv, sem = rest[2 + cores :]
        pairs = ((wk, bk), (wv, bv))
    tile = bk.shape[1]
    tiles = wk.shape[-2] // tile
    streams = weight_rows(leg, pairs, sem, tile, tiles)
    gain_row = k_gain[0, pl.ds(leg, 1), :]
    key_value_low(
        own, received, k_raw, gain_row, cosine[...], sine[...], head, key_low, value_low
    )
    count = key_low.shape[0]
    groups = count // (cores * rows)
    for at in range(tiles):
        for stream in streams:
            stream.wait(at)
        slot = at % bk.shape[0]
        cols = pl.ds(at * tile, tile)
        value = lax.dot_general(key_low[...], bk[slot], contract_last, preferred_element_type=f32)
        value += lax.dot_general(
            value_low[...], bv[slot], contract_last, preferred_element_type=f32
        )
        if near is None:
            queried = lax.dot_general(
                query_part[...], bq[slot], contract_last, preferred_element_type=f32
            )
            begin = queried.shape[0] - count
            near_part[:, cols] = queried[:begin]
            value += queried[begin:]
        else:
            value += query_part[:, cols]
        write_split(outs, groups, cores, rows, at, tile, value)


def hidden(picks, query_part, own, received, k_raw, tables, k_gain, weights, rows, cores, near):
    count = own.shape[0]
    head = k_gain.shape[-1]
    width = weights[0].shape[-2]
    columns = [weight.shape[-1] for weight in weights]
    tile = widest_tile(width)
    tiles = width // tile
    shapes = [jax.ShapeDtypeStruct((count // cores, width), bf16)] * cores
    if near is None:
        weights = (weights[1], weights[2], weights[0])
        columns = columns[1:] + columns[:1]
        shapes = [jax.ShapeDtypeStruct((query_part.shape[0] - count, width), f32)] + shapes
    else:
        weights = weights[1:]
        columns = columns[1:]
    return pl.pallas_call(
        functools.partial(hidden_kernel, cores, rows, head, near),
        out_shape=shapes,
        in_specs=[scalars] + [whole] * 7 + [far_memory] * len(weights),
        out_specs=[whole] * len(shapes),
        scratch_shapes=[
            pltpu.VMEM((count, k_raw.shape[-1]), bf16),
            pltpu.VMEM((count, k_raw.shape[-1]), bf16),
        ]
        + [pltpu.VMEM((min(3, tiles), tile, cols), bf16) for cols in columns]
        + [pltpu.SemaphoreType.DMA((len(weights), tiles))],
        compiler_params=params(57),
        cost_estimate=cost(2 * count * width * sum(columns), 2 * width * sum(columns)),
        name="hidden_grad",
    )(picks, query_part, own, received, k_raw, *tables, k_gain, *weights)


class Group:
    def __init__(self):
        self.size = lax.axis_size("tp")
        self.cores = 2 if self.size % 2 == 0 else 1
        self.chips = self.size // self.cores
        index = lax.axis_index("tp")
        self.chip = index // self.cores
        self.core = index % self.cores

    def place(self, chip, core):
        return (chip % self.chips) * self.cores + core % self.cores

    def to_chip(self, value, ahead):
        pairs = [
            (self.place(chip, core), self.place(chip + ahead, core))
            for chip in range(self.chips)
            for core in range(self.cores)
        ]
        return lax.ppermute(value, "tp", pairs)

    def to_core(self, value, ahead):
        pairs = [
            (self.place(chip, core), self.place(chip, core + ahead))
            for chip in range(self.chips)
            for core in range(self.cores)
        ]
        return lax.ppermute(value, "tp", pairs)

    def spread(self, piece):
        return [piece] + [self.to_core(piece, -k) for k in range(1, self.cores)]

    def positions(self, groups, rows, block):
        inner = jnp.arange(rows, dtype=jnp.int32)
        parts = []
        for g in groups:
            for k in range(self.cores):
                owner = ((self.chip + g) % self.chips) * self.cores + (self.core + k) % self.cores
                parts.append((block * self.size + owner) * rows + inner)
        return jnp.concatenate(parts)


def after(value, *others):
    return lax.optimization_barrier((value,) + others)[0]


def shifted(value, by, first):
    size = lax.axis_size("ctx")
    pairs = [(i, i + by) for i in range(size) if 0 <= i + by < size and i >= first]
    return lax.ppermute(value, "ctx", pairs)


def swapped(value):
    pairs = [(source, source ^ 1) for source in range(lax.axis_size("segment"))]
    return lax.ppermute(value, "segment", pairs)


def rope_tables(positions, head):
    half = head // 2
    frequency = rope_base ** (-(jnp.arange(half).astype(f32) * 2.0 / head))
    angles = positions.astype(f32)[:, None] * frequency[None, :]
    return jnp.cos(angles), jnp.sin(angles)


def per_device(
    stash_inputs,
    stash_grads,
    plan,
    query_weight,
    key_weight,
    value_weight,
    out_weight,
    input_gain,
    output_gain,
    query_gain,
    key_gain,
):
    segment_index = lax.axis_index("segment")
    other_index = 1 - segment_index
    ahead = jnp.stack([plan[0, 0], segment_index]).astype(jnp.int32)
    behind = jnp.stack([plan[0, 1], other_index]).astype(jnp.int32)
    group = Group()
    cores, chips = group.cores, group.chips
    rows = stash_inputs.shape[2]
    head = query_gain.shape[-1]
    block_rows = rows * group.size
    ctx_size = lax.axis_size("ctx")
    block = lax.axis_index("ctx")
    reaches = min(WINDOW // block_rows, ctx_size - 1)

    near_place = group.positions([0], rows, block)
    far_place = group.positions(range(1, chips), rows, block)
    own_place = jnp.concatenate([near_place, far_place])
    near_tables = rope_tables(near_place, head)
    far_tables = rope_tables(far_place, head)
    all_tables = tuple(
        jnp.concatenate([near, far], axis=0) for near, far in zip(near_tables, far_tables)
    )
    weights = (query_weight, key_weight, value_weight)

    back_normed = norm_rows(behind, stash_inputs, input_gain)
    back_far = [group.to_chip(back_normed, -g) for g in range(1, chips)]
    back_near = group.spread(back_normed)
    q_near, kv_near, q_raw_near, k_raw_near = project(
        behind, back_near, near_tables, query_gain, key_gain, *weights, True
    )
    ahead_normed = norm_rows(ahead, stash_inputs, input_gain)

    near_chain = [kv_near]
    for step in range(1, reaches + 1):
        near_chain.append(shifted(near_chain[-1], 1, step - 1))
    far_pieces = []
    for piece in back_far:
        far_pieces += group.spread(piece)
    q_far, kv_far, q_raw_far, k_raw_far = project(
        behind, far_pieces, far_tables, query_gain, key_gain, *weights, True
    )
    far_chain = [kv_far]
    for step in range(1, reaches + 1):
        far_chain.append(shifted(far_chain[-1], 1, step - 1))

    ahead_normed = after(ahead_normed, *back_far)
    ahead_far = [group.to_chip(ahead_normed, -g) for g in range(1, chips)]
    ahead_pieces = group.spread(ahead_normed)
    for piece in ahead_far:
        ahead_pieces += group.spread(piece)
    q_ahead, kv_ahead = project(
        ahead, ahead_pieces, all_tables, query_gain, key_gain, *weights, False
    )

    back_chunks = []
    key_places = []
    for distance in range(reaches + 1):
        back_chunks += [near_chain[distance], far_chain[distance]]
        key_places += [near_place - distance * block_rows, far_place - distance * block_rows]
    key_place = jnp.concatenate(key_places)[None, :]
    far_keep, far_send = attend(
        behind, q_far, back_chunks, far_place[:, None], key_place, out_weight, head, rows, cores
    )
    near_keep, near_send = attend(
        behind, q_near, back_chunks, near_place[:, None], key_place, out_weight, head, rows, cores
    )
    back_terms = scattered(group, rows, near_keep, near_send, far_keep, far_send)
    out_grad = row_call(
        out_grad_kernel, behind, back_terms, stash_grads, output_gain, "out_grad_rows"
    )
    grad_far = [group.to_chip(out_grad, -g) for g in range(1, chips)]
    grad_pieces = group.spread(out_grad)
    for piece in grad_far:
        grad_pieces += group.spread(piece)

    kv_ahead = after(kv_ahead, *far_chain)
    ahead_chain = [kv_ahead]
    for step in range(1, reaches + 1):
        ahead_chain.append(shifted(ahead_chain[-1], 1, step - 1))
    ahead_keep, ahead_send = attend(
        ahead,
        q_ahead,
        ahead_chain,
        own_place[:, None],
        key_place,
        out_weight,
        head,
        rows,
        cores,
    )
    ahead_keep = after(ahead_keep, *grad_far)
    ahead_terms = scattered(
        group, rows, ahead_keep[:rows], ahead_send[:rows], ahead_keep[rows:], ahead_send[rows:]
    )
    forward_out = row_call(
        forward_out_kernel, ahead, ahead_terms, stash_inputs, output_gain, "forward_rows"
    )
    arrived_act = swapped(forward_out)

    q_all = jnp.concatenate([q_near, q_far], axis=0)
    q_raw_all = jnp.concatenate([q_raw_near, q_raw_far], axis=0)
    results = attend_back(
        behind,
        grad_pieces,
        q_all,
        q_raw_all,
        back_chunks,
        own_place[:, None],
        key_place,
        all_tables,
        query_gain,
        out_weight,
    )
    query_low = results[0]
    near_grads = results[1::2]
    far_grads = results[2::2]

    def returned(grads):
        message = grads[reaches].astype(bf16)
        for distance in range(reaches, 0, -1):
            message = shifted(message, -1, distance)
            if distance > 1:
                message = (message.astype(f32) + grads[distance - 1]).astype(bf16)
        return message

    near_rows = rows * cores
    far_back = returned(far_grads)
    near_back = returned(near_grads)
    near_part, far_keep, far_send = hidden(
        behind,
        query_low,
        far_grads[0],
        far_back,
        k_raw_far,
        far_tables,
        key_gain,
        weights,
        rows,
        cores,
        None,
    )
    near_keep, near_send = hidden(
        behind,
        near_part,
        near_grads[0],
        near_back,
        k_raw_near,
        near_tables,
        key_gain,
        weights,
        rows,
        cores,
        True,
    )
    hidden_terms = scattered(group, rows, near_keep, near_send, far_keep, far_send)
    outgoing = outgoing_rows(behind, hidden_terms, stash_inputs, stash_grads, input_gain)
    arrived_grad = swapped(outgoing)
    return (arrived_act[None], arrived_grad[None])


def scattered(group, rows, near_keep, near_send, far_keep, far_send):
    far = far_keep.astype(f32) + group.to_core(far_send, 1).astype(f32)
    far = far.astype(bf16)
    terms = [near_keep, group.to_core(near_send, 1)]
    for g in range(1, group.chips):
        terms.append(group.to_chip(far[(g - 1) * rows : g * rows], g))
    return terms


def solution(mesh):
    return jax.shard_map(
        per_device,
        mesh=mesh,
        in_specs=(
            P("segment", None, ("ctx", "tp"), None),
            P("segment", None, ("ctx", "tp"), None),
            P("segment", None),
            P("segment", None, None, "tp"),
            P("segment", None, None, "tp"),
            P("segment", None, None, "tp"),
            P("segment", None, "tp", None),
            P("segment", None, None),
            P("segment", None, None),
            P("segment", None, None),
            P("segment", None, None),
        ),
        out_specs=(P("segment", ("ctx", "tp"), None), P("segment", ("ctx", "tp"), None)),
        check_vma=False,
    )
```

```python
import functools
import math

import jax
import jax.numpy as jnp
from jax import lax
from jax.experimental import pallas as pl
from jax.experimental.pallas import tpu as pltpu
from jax.sharding import PartitionSpec as P

WINDOW = 1024

epsilon = 1e-06
rope_base = 10000.0
masked_score = -1e30
mebibyte = 1024 * 1024
f32 = jnp.float32
bf16 = jnp.bfloat16

whole = pl.BlockSpec(memory_space=pltpu.VMEM)
scalars = pl.BlockSpec(memory_space=pltpu.SMEM)
anywhere = pl.BlockSpec(memory_space=pl.ANY)


def params(mebibytes):
    return pltpu.CompilerParams(vmem_limit_bytes=int(mebibytes * mebibyte))


class Stream:
    def __init__(self, copies):
        self.copies = copies
        for copy in copies[:2]:
            copy.start()

    def wait(self, at):
        self.copies[at].wait()
        if at + 2 < len(self.copies):
            self.copies[at + 2].start()


def cost(covers):
    size = 64 * mebibyte if covers else 1
    return pl.CostEstimate(flops=1, bytes_accessed=size, transcendentals=0)


def widest_tile(width, limit=1024):
    best = 128
    for tile in range(128, limit + 1, 128):
        if width % tile == 0:
            best = tile
    return best


class Loads:
    def __init__(self, sem):
        self.sem = sem
        self.count = 0

    def start(self, source, target):
        copy = pltpu.make_async_copy(source, target, self.sem.at[self.count])
        copy.start()
        self.count += 1
        return copy


def own_leg(other):
    index = lax.axis_index("segment")
    return 1 - index if other else index


def piece_bases(groups, cores, chips, rows):
    index = lax.axis_index("tp")
    chip = index // cores
    core = index % cores
    begin = lax.axis_index("ctx") * (chips * cores * rows)
    return [
        begin + (((chip + g) % chips) * cores + (core + k) % cores) * rows
        for g in groups
        for k in range(cores)
    ]


def row_places(bases, rows, width):
    return jnp.concatenate(
        [lax.broadcasted_iota(jnp.int32, (rows, width), 0) + base for base in bases], axis=0
    )


def lane_places(bases, rows, back):
    shape = (1, len(bases) * rows)
    lane = lax.broadcasted_iota(jnp.int32, shape, 1)
    place = lane + (bases[0] - back)
    for at in range(1, len(bases)):
        place = jnp.where(lane >= at * rows, lane + (bases[at] - at * rows - back), place)
    return place


def rotation(places, head):
    lane = lax.broadcasted_iota(jnp.int32, places.shape, 1).astype(f32)
    angles = places.astype(f32) * jnp.exp(lane * (-2.0 / head * math.log(rope_base)))
    return jnp.cos(angles), jnp.sin(angles)


def mean_square_scale(value):
    return lax.rsqrt(jnp.mean(value * value, axis=-1, keepdims=True) + epsilon)


def norm_back(value, gain, grad):
    scale = mean_square_scale(value)
    weighted = grad * gain
    inner = jnp.mean(value * weighted, axis=-1, keepdims=True)
    return scale * weighted - value * (scale * scale * scale * inner)


def norm_kernel(plan, stash, gain, first, second, held, gain_held, picks, normed, sem, out_sem):
    loads = Loads(sem)
    waits = [
        loads.start(plan, picks),
        loads.start(stash.at[0], held),
        loads.start(gain, gain_held),
    ]
    for copy in waits:
        copy.wait()
    copies = []
    for which, out in ((1, first), (0, second)):
        value = held[picks[0, which]].astype(f32)
        scaled = value * mean_square_scale(value)
        normed[which] = (scaled * gain_held[0, pl.ds(own_leg(which), 1), :]).astype(bf16)
        copy = pltpu.make_async_copy(normed.at[which], out, out_sem.at[which])
        copy.start()
        copies.append(copy)
    for copy in copies:
        copy.wait()


def norm_rows(plan, stash, gain, covers=False):
    rows, width = stash.shape[-2:]
    shape = jax.ShapeDtypeStruct((rows, width), bf16)
    return pl.pallas_call(
        norm_kernel,
        out_shape=[shape, shape],
        in_specs=[anywhere] * 3,
        out_specs=[anywhere] * 2,
        scratch_shapes=[
            pltpu.VMEM(stash.shape[1:], bf16),
            pltpu.VMEM(gain.shape, f32),
            pltpu.SMEM(plan.shape, plan.dtype),
            pltpu.VMEM((2, rows, width), bf16),
            pltpu.SemaphoreType.DMA((3,)),
            pltpu.SemaphoreType.DMA((2,)),
        ],
        compiler_params=params(62.5),
        cost_estimate=cost(covers),
        name="norm_rows",
    )(plan, stash, gain)


def qkv_kernel(which, layout, keep_raw, *refs):
    groups, cores, chips = layout
    count = len(groups) * cores
    pieces, refs = refs[:count], refs[count:]
    (q_gain, k_gain, wk, wv, wq), refs = refs[:5], refs[5:]
    outs, refs = refs[: 2 + keep_raw], refs[2 + keep_raw :]
    results, refs = refs[: 2 + keep_raw], refs[2 + keep_raw :]
    act, gains, wbuf, in_sem, w_sem, out_sem = refs
    leg = own_leg(which)
    head = q_gain.shape[-1]
    rows = pieces[0].shape[0]
    k_heads = wk.shape[-1] // head
    tiles = []
    for kind, weight in (("k", wk), ("v", wv), ("q", wq)):
        for at in range(weight.shape[-1] // head):
            tiles.append((kind, weight, at))
    slots = wbuf.shape[0]
    stream = Stream(
        [
            pltpu.make_async_copy(
                weight.at[0, leg, :, pl.ds(h * head, head)], wbuf.at[at % slots], w_sem.at[at]
            )
            for at, (kind, weight, h) in enumerate(tiles)
        ]
    )
    loads = Loads(in_sem)
    waits = [
        loads.start(piece, act.at[pl.ds(at * rows, rows)]) for at, piece in enumerate(pieces)
    ]
    waits += [loads.start(gain, gains.at[at]) for at, gain in enumerate((q_gain, k_gain))]
    half = head // 2
    bases = piece_bases(groups, cores, chips, rows)
    cos, sin = rotation(row_places(bases, rows, half), head)
    for copy in waits:
        copy.wait()
    row_gains = {
        "q": gains[0, 0, pl.ds(leg, 1), :],
        "k": gains[1, 0, pl.ds(leg, 1), :],
    }
    copies = []

    def send(array, column, at):
        cols = pl.ds(column * head, head)
        copy = pltpu.make_async_copy(
            results[array].at[:, cols], outs[array].at[:, cols], out_sem.at[array // 2, at]
        )
        copy.start()
        copies.append(copy)

    for at, (kind, weight, h) in enumerate(tiles):
        stream.wait(at)
        raw = jnp.dot(act[...], wbuf[at % slots], preferred_element_type=f32)
        column = h if kind != "v" else k_heads + h
        array = 1 if kind == "q" else 0
        begin = column * head
        if kind == "v":
            results[array][:, pl.ds(begin, head)] = raw.astype(bf16)
        else:
            if keep_raw:
                raw_column = h if kind == "k" else k_heads + h
                results[2][:, pl.ds(raw_column * head, head)] = raw
                send(2, raw_column, at)
            normed = raw * mean_square_scale(raw) * row_gains[kind]
            front = normed[:, :half]
            back = normed[:, half:]
            results[array][:, pl.ds(begin, half)] = (front * cos - back * sin).astype(bf16)
            results[array][:, pl.ds(begin + half, half)] = (back * cos + front * sin).astype(bf16)
        send(array, column, at)
    for copy in copies:
        copy.wait()


def project(which, layout, pieces, q_gain, k_gain, wk, wv, wq, keep_raw, covers=False, first=False):
    rows, width = pieces[0].shape
    total = rows * len(pieces)
    head = q_gain.shape[-1]
    q_cols, k_cols = wq.shape[-1], wk.shape[-1]
    columns = q_cols + 2 * k_cols
    tiles = columns // head
    forms = [((total, 2 * k_cols), bf16), ((total, q_cols), bf16)]
    if keep_raw:
        forms.append(((total, k_cols + q_cols), f32))
    return pl.pallas_call(
        functools.partial(qkv_kernel, which, layout, keep_raw),
        out_shape=[jax.ShapeDtypeStruct(*form) for form in forms],
        in_specs=[anywhere] * (len(pieces) + 5),
        out_specs=[anywhere] * len(forms),
        scratch_shapes=[pltpu.VMEM(*form) for form in forms]
        + [
            pltpu.VMEM((total, width), bf16),
            pltpu.VMEM((2,) + q_gain.shape, f32),
            pltpu.VMEM((3, width, head), bf16),
            pltpu.SemaphoreType.DMA((len(pieces) + 2,)),
            pltpu.SemaphoreType.DMA((tiles,)),
            pltpu.SemaphoreType.DMA((2, tiles)),
        ],
        compiler_params=params(57 if first else 49),
        cost_estimate=cost(covers),
        name="project_heads",
    )(*pieces, q_gain, k_gain, wk, wv, wq)


def visibility(query_place, key_place):
    seen = (
        (key_place >= 0) & (key_place <= query_place) & (key_place > query_place - WINDOW)
    )
    return jnp.where(seen, 0.0, masked_score).astype(f32)


def mask_of(q_groups, key_layout, cores, chips, rows, reaches):
    block = chips * cores * rows
    query_place = row_places(piece_bases(q_groups, cores, chips, rows), rows, 1)
    parts = []
    for distance in range(reaches + 1):
        for groups in key_layout:
            bases = piece_bases(groups, cores, chips, rows)
            parts.append(
                visibility(query_place, lane_places(bases, rows, distance * block))
            )
    return jnp.concatenate(parts, axis=1)


def weights_of(queries, keys, bias):
    scores = lax.dot_general(queries, keys, contract_last, preferred_element_type=f32)
    value = scores * queries.shape[-1] ** (-0.5) + bias
    raised = jnp.exp(value - jnp.max(value, axis=-1, keepdims=True))
    return raised * (1.0 / jnp.sum(raised, axis=-1, keepdims=True))


def load_chunks(loads, sources, held):
    waits = []
    start = 0
    for source in sources:
        size = source.shape[0]
        waits.append(loads.start(source, held.at[pl.ds(start, size)]))
        start += size
    return waits


def split_rows(value, groups, cores, rows):
    parts = []
    for g in range(groups):
        for k in range(cores):
            begin = (g * cores + k) * rows
            parts.append((k, g * rows, value[begin : begin + rows]))
    return parts


class SplitOut:
    def __init__(self, held, outs, sem, groups, cores, rows, tile):
        self.held, self.outs, self.sem = held, outs, sem
        self.groups, self.cores, self.rows, self.tile = groups, cores, rows, tile
        self.copies = []

    def write(self, at, value):
        cols = pl.ds(at * self.tile, self.tile)
        for k, begin, part in split_rows(value, self.groups, self.cores, self.rows):
            self.held[k, pl.ds(begin, self.rows), cols] = part.astype(bf16)
        for k in range(self.cores):
            copy = pltpu.make_async_copy(
                self.held.at[k, :, cols], self.outs[k].at[:, cols], self.sem.at[k, at]
            )
            copy.start()
            self.copies.append(copy)

    def wait(self):
        for copy in self.copies:
            copy.wait()


def attend_kernel(which, layout, key_layout, reaches, rows, head, *refs):
    groups, cores, chips = layout
    count = len(key_layout) * (reaches + 1)
    queries_hbm = refs[0]
    chunks_hbm = refs[1 : 1 + count]
    wo = refs[1 + count]
    outs = refs[2 + count : 2 + count + cores]
    refs = refs[2 + count + cores :]
    queries, keys, context, wbuf, held, in_sem, w_sem, out_sem = refs
    leg = own_leg(which)
    loads = Loads(in_sem)
    waits = [loads.start(queries_hbm, queries)]
    waits += load_chunks(loads, chunks_hbm, keys)
    tile = wbuf.shape[-1]
    tiles = wbuf.shape[0]
    stream = Stream(
        [
            pltpu.make_async_copy(
                wo.at[0, leg, :, pl.ds(at * tile, tile)], wbuf.at[at], w_sem.at[at]
            )
            for at in range(tiles)
        ]
    )
    k_heads = keys.shape[-1] // (2 * head)
    q_heads = queries.shape[-1] // head
    bias = mask_of(groups, key_layout, cores, chips, rows, reaches)
    for copy in waits:
        copy.wait()
    for h in range(q_heads):
        key_at = h * k_heads // q_heads
        key_cols = pl.ds(key_at * head, head)
        value_cols = pl.ds((k_heads + key_at) * head, head)
        weights = weights_of(queries[:, pl.ds(h * head, head)], keys[:, key_cols], bias)
        context[:, pl.ds(h * head, head)] = jnp.dot(
            weights.astype(bf16), keys[:, value_cols], preferred_element_type=f32
        ).astype(bf16)
        stream.wait(h)
    split = SplitOut(held, outs, out_sem, len(groups), cores, rows, tile)
    for at in range(tiles):
        if at >= q_heads:
            stream.wait(at)
        split.write(at, jnp.dot(context[...], wbuf[at], preferred_element_type=f32))
    split.wait()


def attend(which, layout, key_layout, reaches, queries, chunks, wo, head, rows, covers=False):
    cores = layout[1]
    total, q_cols = queries.shape
    keys = sum(chunk.shape[0] for chunk in chunks)
    width = wo.shape[-1]
    tile = widest_tile(width)
    shape = jax.ShapeDtypeStruct((total // cores, width), bf16)
    return pl.pallas_call(
        functools.partial(attend_kernel, which, layout, key_layout, reaches, rows, head),
        out_shape=[shape] * cores,
        in_specs=[anywhere] * (len(chunks) + 2),
        out_specs=[anywhere] * cores,
        scratch_shapes=[
            pltpu.VMEM((total, q_cols), bf16),
            pltpu.VMEM((keys, chunks[0].shape[-1]), bf16),
            pltpu.VMEM((total, q_cols), bf16),
            pltpu.VMEM((width // tile, q_cols, tile), bf16),
            pltpu.VMEM((cores, total // cores, width), bf16),
            pltpu.SemaphoreType.DMA((len(chunks) + 1,)),
            pltpu.SemaphoreType.DMA((width // tile,)),
            pltpu.SemaphoreType.DMA((cores, width // tile)),
        ],
        compiler_params=params(49),
        cost_estimate=cost(covers),
        name="attend_and_project",
    )(queries, *chunks, wo)


def summed(terms):
    total = terms[0][...].astype(f32)
    for term in terms[1:]:
        total = total + term[...].astype(f32)
    return total


def row_kernel(kind, which, count, plan, *refs):
    terms = refs[:count]
    stash, grads, gain, out, held, grad_held, gain_held, sem = refs[count:]
    batch = plan[0, which]
    loads = Loads(sem)
    waits = [loads.start(gain, gain_held)]
    if kind != "grad":
        waits.append(loads.start(stash.at[0, batch], held))
    if kind != "forward":
        waits.append(loads.start(grads.at[0, batch], grad_held))
    total = summed(terms)
    for copy in waits:
        copy.wait()
    gain_row = gain_held[0, pl.ds(own_leg(which), 1), :]
    if kind == "grad":
        result = norm_back(total, gain_row, grad_held[...].astype(f32))
    elif kind == "forward":
        result = held[...].astype(f32) + total * mean_square_scale(total) * gain_row
    else:
        back = norm_back(held[...].astype(f32), gain_row, total)
        result = grad_held[...].astype(f32) + back
    out[...] = result.astype(bf16)


def finish_rows(kind, which, plan, terms, stash, grads, gain, covers=False):
    rows, width = stash.shape[-2:]
    return pl.pallas_call(
        functools.partial(row_kernel, kind, which, len(terms)),
        out_shape=jax.ShapeDtypeStruct((rows, width), bf16),
        in_specs=[scalars] + [whole] * len(terms) + [anywhere] * 3,
        out_specs=whole,
        scratch_shapes=[
            pltpu.VMEM((rows, width), bf16),
            pltpu.VMEM((rows, width), bf16),
            pltpu.VMEM(gain.shape, f32),
            pltpu.SemaphoreType.DMA((3,)),
        ],
        compiler_params=params(8),
        cost_estimate=cost(covers),
        name=kind + "_rows",
    )(plan, *terms, stash, grads, gain)


def head_back(raw, gain_row, cos, sin, grad):
    half = grad.shape[-1] // 2
    front = grad[:, :half]
    back = grad[:, half:]
    turned = jnp.concatenate([front * cos + back * sin, back * cos - front * sin], axis=-1)
    return norm_back(raw, gain_row, turned)


def attend_back_kernel(which, layout, key_layout, reaches, *refs):
    groups, cores, chips = layout
    pieces_count = len(groups) * cores
    halves = len(key_layout)
    count = halves * (reaches + 1)
    pieces, refs = refs[:pieces_count], refs[pieces_count:]
    queries_hbm, refs = refs[:halves], refs[halves:]
    raw_hbm, refs = refs[:halves], refs[halves:]
    chunks_hbm, refs = refs[:count], refs[count:]
    (q_gain, wo, low_hbm), refs = refs[:3], refs[3:]
    grads_hbm, refs = refs[:count], refs[count:]
    (queries, raw, keys, grads, sent), refs = refs[:5], refs[5:]
    (gain_held, query_low, act, context_grad, wbuf, in_sem, w_sem, out_sem) = refs
    leg = own_leg(which)
    rows = pieces[0].shape[0]
    head = q_gain.shape[-1]
    half = head // 2
    k_heads = keys.shape[-1] // (2 * head)
    q_heads = queries.shape[-1] // head
    q_cols = raw.shape[-1]
    loads = Loads(in_sem)
    early = [
        loads.start(piece, act.at[pl.ds(at * rows, rows)]) for at, piece in enumerate(pieces)
    ]
    stream = Stream(
        [
            pltpu.make_async_copy(
                wo.at[0, leg, pl.ds(at * head, head), :], wbuf.at[at], w_sem.at[at]
            )
            for at in range(q_heads)
        ]
    )
    waits = [loads.start(q_gain, gain_held)]
    waits += load_chunks(loads, queries_hbm, queries)
    waits += load_chunks(loads, chunks_hbm, keys)
    raw_cols = pl.ds(raw_hbm[0].shape[-1] - q_cols, q_cols)
    waits += load_chunks(loads, [part.at[:, raw_cols] for part in raw_hbm], raw)
    cos, sin = rotation(row_places(piece_bases(groups, cores, chips, rows), rows, half), head)
    bias = mask_of(groups, key_layout, cores, chips, rows, reaches)
    for copy in early:
        copy.wait()
    for h in range(q_heads):
        stream.wait(h)
        context_grad[:, pl.ds(h * head, head)] = lax.dot_general(
            act[...], wbuf[h], contract_last, preferred_element_type=f32
        ).astype(bf16)
    for copy in waits:
        copy.wait()
    gain_row = gain_held[0, pl.ds(leg, 1), :]
    outs = []

    def send(source, target):
        copy = pltpu.make_async_copy(source, target, out_sem.at[len(outs)])
        copy.start()
        outs.append(copy)

    own = grads.shape[0]
    for h in range(q_heads):
        key_at = h * k_heads // q_heads
        first = h == 0 or (h - 1) * k_heads // q_heads != key_at
        last = h == q_heads - 1 or (h + 1) * k_heads // q_heads != key_at
        key_cols = pl.ds(key_at * head, head)
        value_cols = pl.ds((k_heads + key_at) * head, head)
        query_cols = pl.ds(h * head, head)
        query = queries[:, query_cols]
        upper = context_grad[:, query_cols]
        weights = weights_of(query, keys[:, key_cols], bias)
        weight_grad = lax.dot_general(
            upper, keys[:, value_cols], contract_last, preferred_element_type=f32
        )
        inner = jnp.sum(weight_grad * weights, axis=-1, keepdims=True)
        score_grad = (weights * (weight_grad - inner) * head ** (-0.5)).astype(bf16)
        query_grad = jnp.dot(score_grad, keys[:, key_cols], preferred_element_type=f32)
        key_term = lax.dot_general(score_grad, query, contract_first, preferred_element_type=f32)
        value_term = lax.dot_general(
            weights.astype(bf16), upper, contract_first, preferred_element_type=f32
        )
        for cols, term in ((key_cols, key_term), (value_cols, value_term)):
            if not first:
                term = term + grads[:, cols]
            if not last:
                grads[:, cols] = term
                continue
            sent[:, cols] = term.astype(bf16)
            start = 0
            for at, target in enumerate(grads_hbm):
                size = target.shape[0]
                here = pl.ds(start, size)
                if at < halves:
                    grads[here, cols] = term[start : start + size]
                    send(grads.at[here, cols], target.at[:, cols])
                else:
                    send(sent.at[here, cols], target.at[:, cols])
                start += size
        query_low[:, query_cols] = head_back(
            raw[:, query_cols], gain_row, cos, sin, query_grad
        ).astype(bf16)
        send(query_low.at[:, query_cols], low_hbm.at[:, query_cols])
    for copy in outs:
        copy.wait()


def attend_back(which, layout, key_layout, reaches, pieces, queries, raw, chunks, q_gain, wo, covers=False):
    total = sum(part.shape[0] for part in queries)
    q_cols = queries[0].shape[-1]
    head = q_gain.shape[-1]
    keys = sum(chunk.shape[0] for chunk in chunks)
    cols = chunks[0].shape[-1]
    width = wo.shape[-1]
    k_heads = cols // (2 * head)
    q_heads = q_cols // head
    halves = len(key_layout)
    inputs = len(pieces) + 2 * halves + len(chunks) + 1
    return pl.pallas_call(
        functools.partial(attend_back_kernel, which, layout, key_layout, reaches),
        out_shape=[jax.ShapeDtypeStruct((total, q_cols), bf16)]
        + [
            jax.ShapeDtypeStruct(chunk.shape, f32 if at < halves else bf16)
            for at, chunk in enumerate(chunks)
        ],
        in_specs=[anywhere] * (inputs + 1),
        out_specs=[anywhere] * (1 + len(chunks)),
        scratch_shapes=[
            pltpu.VMEM((total, q_cols), bf16),
            pltpu.VMEM((total, q_cols), f32),
            pltpu.VMEM((keys, cols), bf16),
            pltpu.VMEM((keys, cols), f32),
            pltpu.VMEM((keys, cols), bf16),
            pltpu.VMEM(q_gain.shape, f32),
            pltpu.VMEM((total, q_cols), bf16),
            pltpu.VMEM((total, width), bf16),
            pltpu.VMEM((total, q_cols), bf16),
            pltpu.VMEM((q_heads, head, width), bf16),
            pltpu.SemaphoreType.DMA((inputs,)),
            pltpu.SemaphoreType.DMA((q_heads,)),
            pltpu.SemaphoreType.DMA((2 * k_heads * len(chunks) + q_heads,)),
        ],
        compiler_params=params(49),
        cost_estimate=cost(covers),
        name="attend_back",
    )(*pieces, *queries, *raw, *chunks, q_gain, wo)


contract_last = (((1,), (1,)), ((), ()))
contract_first = (((0,), (0,)), ((), ()))


def row_streams(leg, weights, buffers, sem):
    slots, tile = buffers[0].shape[:2]
    return [
        Stream(
            [
                pltpu.make_async_copy(
                    weight.at[0, leg, pl.ds(at * tile, tile), :],
                    buffer.at[at % slots],
                    sem.at[j, at],
                )
                for at in range(weight.shape[-2] // tile)
            ]
        )
        for j, (weight, buffer) in enumerate(zip(weights, buffers))
    ]


def query_hidden_kernel(which, parts, query_hbm, wq, *refs):
    outs, refs = refs[: len(parts)], refs[len(parts) :]
    query, buffer, held, in_sem, w_sem, out_sem = refs
    copy = pltpu.make_async_copy(query_hbm, query, in_sem)
    copy.start()
    (stream,) = row_streams(own_leg(which), [wq], [buffer], w_sem)
    slots, tile = buffer.shape[:2]
    copy.wait()
    copies = []
    for at in range(wq.shape[-2] // tile):
        stream.wait(at)
        cols = pl.ds(at * tile, tile)
        held[:, cols] = lax.dot_general(
            query[...], buffer[at % slots], contract_last, preferred_element_type=f32
        )
        start = 0
        for j, size in enumerate(parts):
            copy = pltpu.make_async_copy(
                held.at[pl.ds(start, size), cols], outs[j].at[:, cols], out_sem.at[j, at]
            )
            copy.start()
            copies.append(copy)
            start += size
    for copy in copies:
        copy.wait()


def query_hidden(which, parts, query_low, wq, covers=False):
    total, q_cols = query_low.shape
    width = wq.shape[-2]
    tile = widest_tile(width)
    tiles = width // tile
    return pl.pallas_call(
        functools.partial(query_hidden_kernel, which, parts),
        out_shape=[jax.ShapeDtypeStruct((size, width), f32) for size in parts],
        in_specs=[anywhere] * 2,
        out_specs=[anywhere] * len(parts),
        scratch_shapes=[
            pltpu.VMEM((total, q_cols), bf16),
            pltpu.VMEM((min(3, tiles), tile, q_cols), bf16),
            pltpu.VMEM((total, width), f32),
            pltpu.SemaphoreType.DMA,
            pltpu.SemaphoreType.DMA((1, tiles)),
            pltpu.SemaphoreType.DMA((len(parts), tiles)),
        ],
        compiler_params=params(49),
        cost_estimate=cost(covers),
        name="query_hidden",
    )(query_low, wq)


def hidden_kernel(which, layout, rows, *refs):
    groups, cores, chips = layout
    (part_hbm, own_hbm, received_hbm, raw_hbm, k_gain, wk, wv), refs = refs[:7], refs[7:]
    outs, refs = refs[:cores], refs[cores:]
    (part, own, received, raw, gain_held, key_low, value_low, bk, bv, held), refs = (
        refs[:10],
        refs[10:],
    )
    in_sem, w_sem, out_sem = refs
    leg = own_leg(which)
    slots, tile = bk.shape[:2]
    loads = Loads(in_sem)
    waits = [
        loads.start(received_hbm, received),
        loads.start(own_hbm, own),
        loads.start(raw_hbm.at[:, pl.ds(0, raw.shape[-1])], raw),
        loads.start(k_gain, gain_held),
    ]
    streams = row_streams(leg, (wk, wv), (bk, bv), w_sem)
    part_wait = loads.start(part_hbm, part)
    head = k_gain.shape[-1]
    k_cols = raw.shape[-1]
    cos, sin = rotation(
        row_places(piece_bases(groups, cores, chips, rows), rows, head // 2), head
    )
    for copy in waits:
        copy.wait()
    gain_row = gain_held[0, pl.ds(leg, 1), :]
    for h in range(k_cols // head):
        cols = pl.ds(h * head, head)
        grad = own[:, cols] + received[:, cols].astype(f32)
        key_low[:, cols] = head_back(raw[:, cols], gain_row, cos, sin, grad).astype(bf16)
    value_cols = pl.ds(k_cols, k_cols)
    value_low[...] = (own[:, value_cols] + received[:, value_cols].astype(f32)).astype(bf16)
    split = SplitOut(held, outs, out_sem, len(groups), cores, rows, tile)
    for at in range(wk.shape[-2] // tile):
        for stream in streams:
            stream.wait(at)
        slot = at % slots
        value = lax.dot_general(
            key_low[...], bk[slot], contract_last, preferred_element_type=f32
        )
        value += lax.dot_general(
            value_low[...], bv[slot], contract_last, preferred_element_type=f32
        )
        if at == 0:
            part_wait.wait()
        split.write(at, value + part[:, pl.ds(at * tile, tile)])
    split.wait()


def hidden(which, layout, rows, part, own, received, raw, k_gain, wk, wv, covers=False):
    cores = layout[1]
    count = own.shape[0]
    width = wk.shape[-2]
    k_cols = wk.shape[-1]
    tile = widest_tile(width)
    tiles = width // tile
    slots = min(3, tiles)
    return pl.pallas_call(
        functools.partial(hidden_kernel, which, layout, rows),
        out_shape=[jax.ShapeDtypeStruct((count // cores, width), bf16)] * cores,
        in_specs=[anywhere] * 7,
        out_specs=[anywhere] * cores,
        scratch_shapes=[
            pltpu.VMEM(part.shape, part.dtype),
            pltpu.VMEM(own.shape, own.dtype),
            pltpu.VMEM(received.shape, received.dtype),
            pltpu.VMEM((count, k_cols), f32),
            pltpu.VMEM(k_gain.shape, f32),
            pltpu.VMEM((count, k_cols), bf16),
            pltpu.VMEM((count, k_cols), bf16),
            pltpu.VMEM((slots, tile, k_cols), bf16),
            pltpu.VMEM((slots, tile, k_cols), bf16),
            pltpu.VMEM((cores, count // cores, width), bf16),
            pltpu.SemaphoreType.DMA((5,)),
            pltpu.SemaphoreType.DMA((2, tiles)),
            pltpu.SemaphoreType.DMA((cores, tiles)),
        ],
        compiler_params=params(49),
        cost_estimate=cost(covers),
        name="hidden_grad",
    )(part, own, received, raw, k_gain, wk, wv)


class Group:
    def __init__(self):
        self.size = lax.axis_size("tp")
        self.cores = 2 if self.size % 2 == 0 else 1
        self.chips = self.size // self.cores
        index = lax.axis_index("tp")
        self.chip = index // self.cores
        self.core = index % self.cores

    def place(self, chip, core):
        return (chip % self.chips) * self.cores + core % self.cores

    def to_chip(self, value, ahead):
        pairs = [
            (self.place(chip, core), self.place(chip + ahead, core))
            for chip in range(self.chips)
            for core in range(self.cores)
        ]
        return lax.ppermute(value, "tp", pairs)

    def to_core(self, value, ahead):
        pairs = [
            (self.place(chip, core), self.place(chip, core + ahead))
            for chip in range(self.chips)
            for core in range(self.cores)
        ]
        return lax.ppermute(value, "tp", pairs)

    def spread(self, piece):
        return [piece] + [self.to_core(piece, -k) for k in range(1, self.cores)]

    def positions(self, groups, rows, block):
        inner = jnp.arange(rows, dtype=jnp.int32)
        parts = []
        for g in groups:
            for k in range(self.cores):
                owner = ((self.chip + g) % self.chips) * self.cores + (self.core + k) % self.cores
                parts.append((block * self.size + owner) * rows + inner)
        return jnp.concatenate(parts)


def after(value, *others):
    return lax.optimization_barrier((value,) + others)[0]


def shifted(value, by, first):
    size = lax.axis_size("ctx")
    pairs = [(i, i + by) for i in range(size) if 0 <= i + by < size and i >= first]
    return lax.ppermute(value, "ctx", pairs)


def passed_along(value, by):
    size = lax.axis_size("ctx")
    return lax.ppermute(value, "ctx", [(i, i + by) for i in range(size - by)])


def swapped(value):
    pairs = [(source, source ^ 1) for source in range(lax.axis_size("segment"))]
    return lax.ppermute(value, "segment", pairs)


def per_device(
    stash_inputs,
    stash_grads,
    plan,
    query_weight,
    key_weight,
    value_weight,
    out_weight,
    input_gain,
    output_gain,
    query_gain,
    key_gain,
):
    ahead, behind = 0, 1
    group = Group()
    cores, chips = group.cores, group.chips
    rows = stash_inputs.shape[2]
    head = query_gain.shape[-1]
    block_rows = rows * group.size
    reaches = min(WINDOW // block_rows, lax.axis_size("ctx") - 1)
    near_groups = (0,)
    far_groups = tuple(range(1, chips))
    near = (near_groups, cores, chips)
    far = (far_groups, cores, chips)
    every = (near_groups + far_groups, cores, chips)
    everything = (key_weight, value_weight, query_weight)
    gains = (query_gain, key_gain)

    def chip_pieces(value):
        return [group.to_chip(value, -g) for g in far_groups]

    def all_pieces(pieces):
        spread = []
        for piece in pieces:
            spread += group.spread(piece)
        return spread

    back_normed, ahead_normed = norm_rows(plan, stash_inputs, input_gain)
    back_far = chip_pieces(back_normed)
    back_near = group.spread(back_normed)
    kv_near, q_near, raw_near = project(
        behind, near, back_near, *gains, *everything, True, covers=True, first=True
    )
    near_chain = [kv_near]
    back_far = [after(piece, q_near) for piece in back_far]
    ahead_far = chip_pieces(after(ahead_normed, *back_far))
    far_pieces = all_pieces(back_far)
    if reaches > 0:
        near_chain.append(shifted(kv_near, 1, 0))
        far_pieces[0] = after(far_pieces[0], near_chain[1])
    if reaches > 1:
        near_chain.append(shifted(near_chain[1], 1, 1))
    kv_far, q_far, raw_far = project(
        behind, far, far_pieces, *gains, *everything, True, covers=True
    )
    sent_kv = after(kv_far, *near_chain)
    for step in range(3, reaches + 1):
        near_chain.append(shifted(after(near_chain[-1], kv_far), 1, step - 1))
    far_chain = [kv_far] + [passed_along(sent_kv, d) for d in range(1, reaches + 1)]
    ahead_far = [after(piece, kv_far) for piece in ahead_far]
    ahead_pieces = group.spread(ahead_normed) + all_pieces(ahead_far)
    kv_ahead, q_ahead = project(
        ahead, every, ahead_pieces, *gains, *everything, False, covers=True
    )

    back_chunks = []
    for pair in zip(near_chain, far_chain):
        back_chunks += pair
    back_keys = (near_groups, far_groups)
    far_keep, far_send = attend(
        behind,
        far,
        back_keys,
        reaches,
        after(q_far, kv_ahead),
        back_chunks,
        out_weight,
        head,
        rows,
    )
    far_sums = far_parts(group, rows, far_keep, far_send)
    far_terms = [group.to_chip(part, g) for g, part in zip(far_groups, far_sums)]
    near_keep, near_send = attend(
        behind,
        near,
        back_keys,
        reaches,
        after(q_near, far_sums[0]),
        back_chunks,
        out_weight,
        head,
        rows,
        covers=True,
    )
    near_send = after(near_send, *far_terms)
    back_terms = [near_keep, group.to_core(near_send, 1)] + far_terms
    ahead_chain = [kv_ahead]
    if reaches > 0:
        ahead_chain.append(shifted(after(kv_ahead, far_sums[0]), 1, 0))
        back_terms[0] = after(near_keep, ahead_chain[1])
    out_grad = finish_rows(
        "grad", behind, plan, back_terms, stash_inputs, stash_grads, output_gain
    )
    grad_far = chip_pieces(out_grad)
    grad_near = group.spread(out_grad)
    for step in range(2, reaches + 1):
        ahead_chain.append(shifted(after(ahead_chain[-1], out_grad), 1, step - 1))
        if step == 2:
            grad_far = [after(piece, ahead_chain[-1]) for piece in grad_far]

    results = attend_back(
        behind,
        every,
        back_keys,
        reaches,
        grad_near + all_pieces(grad_far),
        (q_near, q_far),
        (raw_near, raw_far),
        back_chunks,
        query_gain,
        out_weight,
    )
    query_low = results[0]
    near_grads = results[1::2]
    far_grads = results[2::2]
    near_rows = near_grads[0].shape[0]
    near_part, far_part = query_hidden(
        behind, (near_rows, query_low.shape[0] - near_rows), query_low, query_weight, covers=True
    )

    def added(message, grads, distance):
        return (message.astype(f32) + grads[distance].astype(f32)).astype(bf16)

    far_back, near_back = far_grads[reaches], near_grads[reaches]
    beside = near_part
    ahead_keep = None
    for distance in range(reaches, 0, -1):
        far_back = shifted(far_back, -1, distance)
        near_back = shifted(near_back, -1, distance)
        if distance == 1:
            break
        far_back = added(after(far_back, beside), far_grads, distance - 1)
        near_back = added(after(near_back, beside), near_grads, distance - 1)
        if ahead_keep is None:
            ahead_keep, ahead_send = attend(
                ahead,
                every,
                (near_groups + far_groups,),
                reaches,
                after(q_ahead, far_back, near_back),
                ahead_chain,
                out_weight,
                head,
                rows,
                covers=True,
            )
            beside = ahead_keep
    if ahead_keep is None:
        ahead_keep, ahead_send = attend(
            ahead,
            every,
            (near_groups + far_groups,),
            reaches,
            after(q_ahead, near_part),
            ahead_chain,
            out_weight,
            head,
            rows,
        )
    ahead_sums = far_parts(group, rows, ahead_keep[rows:], ahead_send[rows:])
    ahead_terms = [ahead_keep[:rows], group.to_core(ahead_send[:rows], 1)] + [
        group.to_chip(part, g) for g, part in zip(far_groups, ahead_sums)
    ]

    kv_weights = (key_weight, value_weight)
    far_keep, far_send = hidden(
        behind, far, rows, far_part, far_grads[0], far_back, raw_far, key_gain, *kv_weights
    )
    far_sums = far_parts(group, rows, far_keep, far_send)
    far_terms = [group.to_chip(part, g) for g, part in zip(far_groups, far_sums)]
    forward_out = finish_rows(
        "forward",
        ahead,
        plan,
        [after(ahead_terms[0], far_sums[0])] + ahead_terms[1:],
        stash_inputs,
        stash_grads,
        output_gain,
    )
    arrived_act = swapped(forward_out)
    near_keep, near_send = hidden(
        behind,
        near,
        rows,
        after(near_part, forward_out),
        near_grads[0],
        after(near_back, far_sums[0]),
        raw_near,
        key_gain,
        *kv_weights,
        covers=True,
    )
    near_send = after(near_send, *far_terms)
    hidden_terms = [near_keep, group.to_core(near_send, 1)] + far_terms
    outgoing = finish_rows(
        "outgoing", behind, plan, hidden_terms, stash_inputs, stash_grads, input_gain
    )
    arrived_grad = swapped(outgoing)
    return (arrived_act[None], arrived_grad[None])


def far_parts(group, rows, far_keep, far_send):
    far = far_keep.astype(f32) + group.to_core(far_send, 1).astype(f32)
    far = far.astype(bf16)
    return [far[(g - 1) * rows : g * rows] for g in range(1, group.chips)]


def solution(mesh):
    return jax.shard_map(
        per_device,
        mesh=mesh,
        in_specs=(
            P("segment", None, ("ctx", "tp"), None),
            P("segment", None, ("ctx", "tp"), None),
            P("segment", None),
            P("segment", None, None, "tp"),
            P("segment", None, None, "tp"),
            P("segment", None, None, "tp"),
            P("segment", None, "tp", None),
            P("segment", None, None),
            P("segment", None, None),
            P("segment", None, None),
            P("segment", None, None),
        ),
        out_specs=(P("segment", ("ctx", "tp"), None), P("segment", ("ctx", "tp"), None)),
        check_vma=False,
    )
```

```python
import functools
import math

import jax
import jax.numpy as jnp
from jax import lax
from jax.experimental import pallas as pl
from jax.experimental.pallas import tpu as pltpu
from jax.sharding import PartitionSpec as P

WINDOW = 1024

epsilon = 1e-06
rope_base = 10000.0
masked_score = -1e30
mebibyte = 1024 * 1024
f32 = jnp.float32
bf16 = jnp.bfloat16

whole = pl.BlockSpec(memory_space=pltpu.VMEM)
scalars = pl.BlockSpec(memory_space=pltpu.SMEM)
anywhere = pl.BlockSpec(memory_space=pl.ANY)


def params(mebibytes):
    return pltpu.CompilerParams(vmem_limit_bytes=int(mebibytes * mebibyte))


class Stream:
    def __init__(self, copies):
        self.copies = copies
        for copy in copies[:2]:
            copy.start()

    def wait(self, at):
        self.copies[at].wait()
        if at + 2 < len(self.copies):
            self.copies[at + 2].start()


def cost(covers):
    size = 64 * mebibyte if covers else 1
    return pl.CostEstimate(flops=1, bytes_accessed=size, transcendentals=0)


def widest_tile(width, limit=1024):
    best = 128
    for tile in range(128, limit + 1, 128):
        if width % tile == 0:
            best = tile
    return best


class Loads:
    def __init__(self, sem):
        self.sem = sem
        self.count = 0

    def start(self, source, target):
        copy = pltpu.make_async_copy(source, target, self.sem.at[self.count])
        copy.start()
        self.count += 1
        return copy


def own_leg(other):
    index = lax.axis_index("segment")
    return 1 - index if other else index


def piece_bases(groups, cores, chips, rows):
    index = lax.axis_index("tp")
    chip = index // cores
    core = index % cores
    begin = lax.axis_index("ctx") * (chips * cores * rows)
    return [
        begin + (((chip + g) % chips) * cores + (core + k) % cores) * rows
        for g in groups
        for k in range(cores)
    ]


def row_places(bases, rows, width):
    return jnp.concatenate(
        [lax.broadcasted_iota(jnp.int32, (rows, width), 0) + base for base in bases], axis=0
    )


def lane_places(bases, rows, back):
    shape = (1, len(bases) * rows)
    lane = lax.broadcasted_iota(jnp.int32, shape, 1)
    place = lane + (bases[0] - back)
    for at in range(1, len(bases)):
        place = jnp.where(lane >= at * rows, lane + (bases[at] - at * rows - back), place)
    return place


def rotation(places, head):
    lane = lax.broadcasted_iota(jnp.int32, places.shape, 1).astype(f32)
    angles = places.astype(f32) * jnp.exp(lane * (-2.0 / head * math.log(rope_base)))
    return jnp.cos(angles), jnp.sin(angles)


def mean_square_scale(value):
    return lax.rsqrt(jnp.mean(value * value, axis=-1, keepdims=True) + epsilon)


def norm_back(value, gain, grad):
    scale = mean_square_scale(value)
    weighted = grad * gain
    inner = jnp.mean(value * weighted, axis=-1, keepdims=True)
    return scale * weighted - value * (scale * scale * scale * inner)


def norm_kernel(plan, stash, gain, first, second, held, gain_held, picks, normed, sem, out_sem):
    loads = Loads(sem)
    waits = [
        loads.start(plan, picks),
        loads.start(stash.at[0], held),
        loads.start(gain, gain_held),
    ]
    for copy in waits:
        copy.wait()
    copies = []
    for which, out in ((1, first), (0, second)):
        value = held[picks[0, which]].astype(f32)
        scaled = value * mean_square_scale(value)
        normed[which] = (scaled * gain_held[0, pl.ds(own_leg(which), 1), :]).astype(bf16)
        copy = pltpu.make_async_copy(normed.at[which], out, out_sem.at[which])
        copy.start()
        copies.append(copy)
    for copy in copies:
        copy.wait()


def norm_rows(plan, stash, gain, covers=False):
    rows, width = stash.shape[-2:]
    shape = jax.ShapeDtypeStruct((rows, width), bf16)
    return pl.pallas_call(
        norm_kernel,
        out_shape=[shape, shape],
        in_specs=[anywhere] * 3,
        out_specs=[anywhere] * 2,
        scratch_shapes=[
            pltpu.VMEM(stash.shape[1:], bf16),
            pltpu.VMEM(gain.shape, f32),
            pltpu.SMEM(plan.shape, plan.dtype),
            pltpu.VMEM((2, rows, width), bf16),
            pltpu.SemaphoreType.DMA((3,)),
            pltpu.SemaphoreType.DMA((2,)),
        ],
        compiler_params=params(62.5),
        cost_estimate=cost(covers),
        name="norm_rows",
    )(plan, stash, gain)


def qkv_kernel(which, layout, parts, keep_raw, *refs):
    groups, cores, chips = layout
    count = len(groups) * cores
    pieces, refs = refs[:count], refs[count:]
    (q_gain, k_gain, wk, wv, wq), refs = refs[:5], refs[5:]
    names = [name for name in ("kv", "q") if name in parts] + ["raw"] * keep_raw
    outs, refs = dict(zip(names, refs)), refs[len(names) :]
    results, refs = dict(zip(names, refs)), refs[len(names) :]
    act, gains, wbuf, in_sem, w_sem, out_sem = refs
    leg = own_leg(which)
    head = q_gain.shape[-1]
    rows = pieces[0].shape[0]
    k_heads = wk.shape[-1] // head
    tiles = []
    for kind, weight in (("k", wk), ("v", wv), ("q", wq)):
        if (kind == "q") != ("q" in parts) and len(parts) == 1:
            continue
        for at in range(weight.shape[-1] // head):
            tiles.append((kind, weight, at))
    slots = wbuf.shape[0]
    stream = Stream(
        [
            pltpu.make_async_copy(
                weight.at[0, leg, :, pl.ds(h * head, head)], wbuf.at[at % slots], w_sem.at[at]
            )
            for at, (kind, weight, h) in enumerate(tiles)
        ]
    )
    loads = Loads(in_sem)
    waits = [
        loads.start(piece, act.at[pl.ds(at * rows, rows)]) for at, piece in enumerate(pieces)
    ]
    waits += [loads.start(gain, gains.at[at]) for at, gain in enumerate((q_gain, k_gain))]
    half = head // 2
    bases = piece_bases(groups, cores, chips, rows)
    cos, sin = rotation(row_places(bases, rows, half), head)
    for copy in waits:
        copy.wait()
    row_gains = {
        "q": gains[0, 0, pl.ds(leg, 1), :],
        "k": gains[1, 0, pl.ds(leg, 1), :],
    }
    copies = []

    def send(array, column, at):
        cols = pl.ds(column * head, head)
        copy = pltpu.make_async_copy(
            results[array].at[:, cols], outs[array].at[:, cols], out_sem.at[int(array == "raw"), at]
        )
        copy.start()
        copies.append(copy)

    for at, (kind, weight, h) in enumerate(tiles):
        stream.wait(at)
        raw = jnp.dot(act[...], wbuf[at % slots], preferred_element_type=f32)
        column = h if kind != "v" else k_heads + h
        array = "q" if kind == "q" else "kv"
        begin = column * head
        if kind == "v":
            results[array][:, pl.ds(begin, head)] = raw.astype(bf16)
        else:
            if keep_raw:
                raw_column = h if kind == "k" else k_heads + h
                results["raw"][:, pl.ds(raw_column * head, head)] = raw
                send("raw", raw_column, at)
            normed = raw * mean_square_scale(raw) * row_gains[kind]
            front = normed[:, :half]
            back = normed[:, half:]
            results[array][:, pl.ds(begin, half)] = (front * cos - back * sin).astype(bf16)
            results[array][:, pl.ds(begin + half, half)] = (back * cos + front * sin).astype(bf16)
        send(array, column, at)
    for copy in copies:
        copy.wait()


def project(which, layout, pieces, q_gain, k_gain, wk, wv, wq, keep_raw, covers=False, first=False, parts=("kv", "q")):
    rows, width = pieces[0].shape
    total = rows * len(pieces)
    head = q_gain.shape[-1]
    q_cols, k_cols = wq.shape[-1], wk.shape[-1]
    forms = [((total, 2 * k_cols), bf16)] * ("kv" in parts)
    forms += [((total, q_cols), bf16)] * ("q" in parts)
    tiles = sum(form[0][1] for form in forms) // head
    if keep_raw:
        forms.append(((total, k_cols + q_cols), f32))
    return pl.pallas_call(
        functools.partial(qkv_kernel, which, layout, parts, keep_raw),
        out_shape=[jax.ShapeDtypeStruct(*form) for form in forms],
        in_specs=[anywhere] * (len(pieces) + 5),
        out_specs=[anywhere] * len(forms),
        scratch_shapes=[pltpu.VMEM(*form) for form in forms]
        + [
            pltpu.VMEM((total, width), bf16),
            pltpu.VMEM((2,) + q_gain.shape, f32),
            pltpu.VMEM((3, width, head), bf16),
            pltpu.SemaphoreType.DMA((len(pieces) + 2,)),
            pltpu.SemaphoreType.DMA((tiles,)),
            pltpu.SemaphoreType.DMA((2, tiles)),
        ],
        compiler_params=params(57 if first else 49),
        cost_estimate=cost(covers),
        name="project_heads",
    )(*pieces, q_gain, k_gain, wk, wv, wq)


def visibility(query_place, key_place):
    seen = (
        (key_place >= 0) & (key_place <= query_place) & (key_place > query_place - WINDOW)
    )
    return jnp.where(seen, 0.0, masked_score).astype(f32)


def mask_of(q_groups, key_layout, cores, chips, rows, reaches):
    block = chips * cores * rows
    query_place = row_places(piece_bases(q_groups, cores, chips, rows), rows, 1)
    parts = []
    for distance in range(reaches + 1):
        for groups in key_layout:
            bases = piece_bases(groups, cores, chips, rows)
            parts.append(
                visibility(query_place, lane_places(bases, rows, distance * block))
            )
    return jnp.concatenate(parts, axis=1)


def weights_of(queries, keys, bias):
    scores = lax.dot_general(queries, keys, contract_last, preferred_element_type=f32)
    value = scores * queries.shape[-1] ** (-0.5) + bias
    raised = jnp.exp(value - jnp.max(value, axis=-1, keepdims=True))
    return raised * (1.0 / jnp.sum(raised, axis=-1, keepdims=True))


def load_chunks(loads, sources, held):
    waits = []
    start = 0
    for source in sources:
        size = source.shape[0]
        waits.append(loads.start(source, held.at[pl.ds(start, size)]))
        start += size
    return waits


def split_rows(value, groups, cores, rows):
    parts = []
    for g in range(groups):
        for k in range(cores):
            begin = (g * cores + k) * rows
            parts.append((k, g * rows, value[begin : begin + rows]))
    return parts


class SplitOut:
    def __init__(self, held, outs, sem, groups, cores, rows, tile):
        self.held, self.outs, self.sem = held, outs, sem
        self.groups, self.cores, self.rows, self.tile = groups, cores, rows, tile
        self.copies = []

    def write(self, at, value):
        cols = pl.ds(at * self.tile, self.tile)
        for k, begin, part in split_rows(value, self.groups, self.cores, self.rows):
            self.held[k, pl.ds(begin, self.rows), cols] = part.astype(bf16)
        for k in range(self.cores):
            copy = pltpu.make_async_copy(
                self.held.at[k, :, cols], self.outs[k].at[:, cols], self.sem.at[k, at]
            )
            copy.start()
            self.copies.append(copy)

    def wait(self):
        for copy in self.copies:
            copy.wait()


def attend_kernel(which, layout, key_layout, reaches, rows, head, *refs):
    groups, cores, chips = layout
    count = len(key_layout) * (reaches + 1)
    queries_hbm = refs[0]
    chunks_hbm = refs[1 : 1 + count]
    wo = refs[1 + count]
    outs = refs[2 + count : 2 + count + cores]
    refs = refs[2 + count + cores :]
    if len(wo.shape) == 2:
        queries, keys, context, held, in_sem, out_sem = refs
        wbuf = None
    else:
        queries, keys, context, wbuf, held, in_sem, w_sem, out_sem = refs
    leg = own_leg(which)
    loads = Loads(in_sem)
    waits = [loads.start(queries_hbm, queries)]
    waits += load_chunks(loads, chunks_hbm, keys)
    tile = widest_tile(wo.shape[-1])
    tiles = wo.shape[-1] // tile
    stream = Stream(
        []
        if wbuf is None
        else [
            pltpu.make_async_copy(
                wo.at[0, leg, :, pl.ds(at * tile, tile)], wbuf.at[at], w_sem.at[at]
            )
            for at in range(tiles)
        ]
    )
    k_heads = keys.shape[-1] // (2 * head)
    q_heads = queries.shape[-1] // head
    bias = mask_of(groups, key_layout, cores, chips, rows, reaches)
    for copy in waits:
        copy.wait()
    for h in range(q_heads):
        key_at = h * k_heads // q_heads
        key_cols = pl.ds(key_at * head, head)
        value_cols = pl.ds((k_heads + key_at) * head, head)
        weights = weights_of(queries[:, pl.ds(h * head, head)], keys[:, key_cols], bias)
        context[:, pl.ds(h * head, head)] = jnp.dot(
            weights.astype(bf16), keys[:, value_cols], preferred_element_type=f32
        ).astype(bf16)
        if wbuf is not None:
            stream.wait(h)
    split = SplitOut(held, outs, out_sem, len(groups), cores, rows, tile)
    for at in range(tiles):
        if wbuf is None:
            tile_rows = wo[:, pl.ds(at * tile, tile)]
        else:
            if at >= q_heads:
                stream.wait(at)
            tile_rows = wbuf[at]
        split.write(at, jnp.dot(context[...], tile_rows, preferred_element_type=f32))
    split.wait()


def attend(which, layout, key_layout, reaches, queries, chunks, wo, head, rows, covers=False):
    cores = layout[1]
    total, q_cols = queries.shape
    keys = sum(chunk.shape[0] for chunk in chunks)
    width = wo.shape[-1]
    tile = widest_tile(width)
    resident = wo.ndim == 2
    shape = jax.ShapeDtypeStruct((total // cores, width), bf16)
    return pl.pallas_call(
        functools.partial(attend_kernel, which, layout, key_layout, reaches, rows, head),
        out_shape=[shape] * cores,
        in_specs=[anywhere] * (len(chunks) + 1) + [whole if resident else anywhere],
        out_specs=[anywhere] * cores,
        scratch_shapes=[
            pltpu.VMEM((total, q_cols), bf16),
            pltpu.VMEM((keys, chunks[0].shape[-1]), bf16),
            pltpu.VMEM((total, q_cols), bf16),
        ]
        + [pltpu.VMEM((width // tile, q_cols, tile), bf16)] * (not resident)
        + [
            pltpu.VMEM((cores, total // cores, width), bf16),
            pltpu.SemaphoreType.DMA((len(chunks) + 1,)),
        ]
        + [pltpu.SemaphoreType.DMA((width // tile,))] * (not resident)
        + [pltpu.SemaphoreType.DMA((cores, width // tile))],
        compiler_params=params(36 if resident else 49),
        cost_estimate=cost(covers),
        name="attend_and_project",
    )(queries, *chunks, wo)


def summed(terms):
    total = terms[0][...].astype(f32)
    for term in terms[1:]:
        total = total + term[...].astype(f32)
    return total


def row_kernel(kind, which, count, plan, *refs):
    terms = refs[:count]
    stash, grads, gain, out, held, grad_held, gain_held, sem = refs[count:]
    batch = plan[0, which]
    loads = Loads(sem)
    waits = [loads.start(gain, gain_held)]
    if kind != "grad":
        waits.append(loads.start(stash.at[0, batch], held))
    if kind != "forward":
        waits.append(loads.start(grads.at[0, batch], grad_held))
    total = summed(terms)
    for copy in waits:
        copy.wait()
    gain_row = gain_held[0, pl.ds(own_leg(which), 1), :]
    if kind == "grad":
        result = norm_back(total, gain_row, grad_held[...].astype(f32))
    elif kind == "forward":
        result = held[...].astype(f32) + total * mean_square_scale(total) * gain_row
    else:
        back = norm_back(held[...].astype(f32), gain_row, total)
        result = grad_held[...].astype(f32) + back
    out[...] = result.astype(bf16)


def finish_rows(kind, which, plan, terms, stash, grads, gain, covers=False):
    rows, width = stash.shape[-2:]
    return pl.pallas_call(
        functools.partial(row_kernel, kind, which, len(terms)),
        out_shape=jax.ShapeDtypeStruct((rows, width), bf16),
        in_specs=[scalars] + [whole] * len(terms) + [anywhere] * 3,
        out_specs=whole,
        scratch_shapes=[
            pltpu.VMEM((rows, width), bf16),
            pltpu.VMEM((rows, width), bf16),
            pltpu.VMEM(gain.shape, f32),
            pltpu.SemaphoreType.DMA((3,)),
        ],
        compiler_params=params(8),
        cost_estimate=cost(covers),
        name=kind + "_rows",
    )(plan, *terms, stash, grads, gain)


def copy_kernel(source, target, sem):
    copy = pltpu.make_async_copy(source, target, sem)
    copy.start()
    copy.wait()


def copied(value):
    return pl.pallas_call(
        copy_kernel,
        out_shape=jax.ShapeDtypeStruct(value.shape, value.dtype),
        in_specs=[anywhere],
        out_specs=anywhere,
        scratch_shapes=[pltpu.SemaphoreType.DMA],
        compiler_params=params(8),
        cost_estimate=cost(False),
        name="copied",
    )(value)


def head_back(raw, gain_row, cos, sin, grad):
    half = grad.shape[-1] // 2
    front = grad[:, :half]
    back = grad[:, half:]
    turned = jnp.concatenate([front * cos + back * sin, back * cos - front * sin], axis=-1)
    return norm_back(raw, gain_row, turned)


def attend_back_kernel(which, layout, key_layout, reaches, *refs):
    groups, cores, chips = layout
    pieces_count = len(groups) * cores
    halves = len(key_layout)
    count = halves * (reaches + 1)
    pieces, refs = refs[:pieces_count], refs[pieces_count:]
    queries_hbm, refs = refs[:halves], refs[halves:]
    raw_hbm, refs = refs[:halves], refs[halves:]
    chunks_hbm, refs = refs[:count], refs[count:]
    (q_gain, wo, low_hbm), refs = refs[:3], refs[3:]
    grads_hbm, refs = refs[:count], refs[count:]
    (queries, raw, keys, grads, sent), refs = refs[:5], refs[5:]
    resident = len(wo.shape) == 2
    if resident:
        (gain_held, query_low, act, context_grad, in_sem, out_sem) = refs
    else:
        (gain_held, query_low, act, context_grad, wbuf, in_sem, w_sem, out_sem) = refs
    leg = own_leg(which)
    rows = pieces[0].shape[0]
    head = q_gain.shape[-1]
    half = head // 2
    k_heads = keys.shape[-1] // (2 * head)
    q_heads = queries.shape[-1] // head
    q_cols = raw.shape[-1]
    loads = Loads(in_sem)
    early = [
        loads.start(piece, act.at[pl.ds(at * rows, rows)]) for at, piece in enumerate(pieces)
    ]
    stream = Stream(
        []
        if resident
        else [
            pltpu.make_async_copy(
                wo.at[0, leg, pl.ds(at * head, head), :], wbuf.at[at], w_sem.at[at]
            )
            for at in range(q_heads)
        ]
    )
    waits = [loads.start(q_gain, gain_held)]
    waits += load_chunks(loads, queries_hbm, queries)
    waits += load_chunks(loads, chunks_hbm, keys)
    raw_cols = pl.ds(raw_hbm[0].shape[-1] - q_cols, q_cols)
    waits += load_chunks(loads, [part.at[:, raw_cols] for part in raw_hbm], raw)
    cos, sin = rotation(row_places(piece_bases(groups, cores, chips, rows), rows, half), head)
    bias = mask_of(groups, key_layout, cores, chips, rows, reaches)
    for copy in early:
        copy.wait()
    for h in range(q_heads):
        if resident:
            head_rows = wo[pl.ds(h * head, head), :]
        else:
            stream.wait(h)
            head_rows = wbuf[h]
        context_grad[:, pl.ds(h * head, head)] = lax.dot_general(
            act[...], head_rows, contract_last, preferred_element_type=f32
        ).astype(bf16)
    for copy in waits:
        copy.wait()
    gain_row = gain_held[0, pl.ds(leg, 1), :]
    outs = []

    def send(source, target):
        copy = pltpu.make_async_copy(source, target, out_sem.at[len(outs)])
        copy.start()
        outs.append(copy)

    own = grads.shape[0]
    for h in range(q_heads):
        key_at = h * k_heads // q_heads
        first = h == 0 or (h - 1) * k_heads // q_heads != key_at
        last = h == q_heads - 1 or (h + 1) * k_heads // q_heads != key_at
        key_cols = pl.ds(key_at * head, head)
        value_cols = pl.ds((k_heads + key_at) * head, head)
        query_cols = pl.ds(h * head, head)
        query = queries[:, query_cols]
        upper = context_grad[:, query_cols]
        weights = weights_of(query, keys[:, key_cols], bias)
        weight_grad = lax.dot_general(
            upper, keys[:, value_cols], contract_last, preferred_element_type=f32
        )
        inner = jnp.sum(weight_grad * weights, axis=-1, keepdims=True)
        score_grad = (weights * (weight_grad - inner) * head ** (-0.5)).astype(bf16)
        query_grad = jnp.dot(score_grad, keys[:, key_cols], preferred_element_type=f32)
        key_term = lax.dot_general(score_grad, query, contract_first, preferred_element_type=f32)
        value_term = lax.dot_general(
            weights.astype(bf16), upper, contract_first, preferred_element_type=f32
        )
        for cols, term in ((key_cols, key_term), (value_cols, value_term)):
            if not first:
                term = term + grads[:, cols]
            if not last:
                grads[:, cols] = term
                continue
            sent[:, cols] = term.astype(bf16)
            start = 0
            for at, target in enumerate(grads_hbm):
                size = target.shape[0]
                here = pl.ds(start, size)
                if at < halves:
                    grads[here, cols] = term[start : start + size]
                    send(grads.at[here, cols], target.at[:, cols])
                else:
                    send(sent.at[here, cols], target.at[:, cols])
                start += size
        query_low[:, query_cols] = head_back(
            raw[:, query_cols], gain_row, cos, sin, query_grad
        ).astype(bf16)
        send(query_low.at[:, query_cols], low_hbm.at[:, query_cols])
    for copy in outs:
        copy.wait()


def attend_back(which, layout, key_layout, reaches, pieces, queries, raw, chunks, q_gain, wo, covers=False):
    total = sum(part.shape[0] for part in queries)
    q_cols = queries[0].shape[-1]
    head = q_gain.shape[-1]
    keys = sum(chunk.shape[0] for chunk in chunks)
    cols = chunks[0].shape[-1]
    width = wo.shape[-1]
    k_heads = cols // (2 * head)
    q_heads = q_cols // head
    halves = len(key_layout)
    inputs = len(pieces) + 2 * halves + len(chunks) + 1
    resident = wo.ndim == 2
    return pl.pallas_call(
        functools.partial(attend_back_kernel, which, layout, key_layout, reaches),
        out_shape=[jax.ShapeDtypeStruct((total, q_cols), bf16)]
        + [
            jax.ShapeDtypeStruct(chunk.shape, f32 if at < halves else bf16)
            for at, chunk in enumerate(chunks)
        ],
        in_specs=[anywhere] * inputs + [whole if resident else anywhere],
        out_specs=[anywhere] * (1 + len(chunks)),
        scratch_shapes=[
            pltpu.VMEM((total, q_cols), bf16),
            pltpu.VMEM((total, q_cols), f32),
            pltpu.VMEM((keys, cols), bf16),
            pltpu.VMEM((keys, cols), f32),
            pltpu.VMEM((keys, cols), bf16),
            pltpu.VMEM(q_gain.shape, f32),
            pltpu.VMEM((total, q_cols), bf16),
            pltpu.VMEM((total, width), bf16),
            pltpu.VMEM((total, q_cols), bf16),
        ]
        + [pltpu.VMEM((q_heads, head, width), bf16)] * (not resident)
        + [pltpu.SemaphoreType.DMA((inputs,))]
        + [pltpu.SemaphoreType.DMA((q_heads,))] * (not resident)
        + [pltpu.SemaphoreType.DMA((2 * k_heads * len(chunks) + q_heads,))],
        compiler_params=params(36 if resident else 49),
        cost_estimate=cost(covers),
        name="attend_back",
    )(*pieces, *queries, *raw, *chunks, q_gain, wo)


contract_last = (((1,), (1,)), ((), ()))
contract_first = (((0,), (0,)), ((), ()))


def row_streams(leg, weights, buffers, sem):
    slots, tile = buffers[0].shape[:2]
    return [
        Stream(
            [
                pltpu.make_async_copy(
                    weight.at[0, leg, pl.ds(at * tile, tile), :],
                    buffer.at[at % slots],
                    sem.at[j, at],
                )
                for at in range(weight.shape[-2] // tile)
            ]
        )
        for j, (weight, buffer) in enumerate(zip(weights, buffers))
    ]


def query_hidden_kernel(which, parts, query_hbm, wq, *refs):
    outs, refs = refs[: len(parts)], refs[len(parts) :]
    query, buffer, held, in_sem, w_sem, out_sem = refs
    copy = pltpu.make_async_copy(query_hbm, query, in_sem)
    copy.start()
    (stream,) = row_streams(own_leg(which), [wq], [buffer], w_sem)
    slots, tile = buffer.shape[:2]
    copy.wait()
    copies = []
    for at in range(wq.shape[-2] // tile):
        stream.wait(at)
        cols = pl.ds(at * tile, tile)
        held[:, cols] = lax.dot_general(
            query[...], buffer[at % slots], contract_last, preferred_element_type=f32
        )
        start = 0
        for j, size in enumerate(parts):
            copy = pltpu.make_async_copy(
                held.at[pl.ds(start, size), cols], outs[j].at[:, cols], out_sem.at[j, at]
            )
            copy.start()
            copies.append(copy)
            start += size
    for copy in copies:
        copy.wait()


def query_hidden(which, parts, query_low, wq, covers=False):
    total, q_cols = query_low.shape
    width = wq.shape[-2]
    tile = widest_tile(width)
    tiles = width // tile
    return pl.pallas_call(
        functools.partial(query_hidden_kernel, which, parts),
        out_shape=[jax.ShapeDtypeStruct((size, width), f32) for size in parts],
        in_specs=[anywhere] * 2,
        out_specs=[anywhere] * len(parts),
        scratch_shapes=[
            pltpu.VMEM((total, q_cols), bf16),
            pltpu.VMEM((min(3, tiles), tile, q_cols), bf16),
            pltpu.VMEM((total, width), f32),
            pltpu.SemaphoreType.DMA,
            pltpu.SemaphoreType.DMA((1, tiles)),
            pltpu.SemaphoreType.DMA((len(parts), tiles)),
        ],
        compiler_params=params(49),
        cost_estimate=cost(covers),
        name="query_hidden",
    )(query_low, wq)


def hidden_kernel(which, layout, rows, *refs):
    groups, cores, chips = layout
    (part_hbm, own_hbm, received_hbm, raw_hbm, k_gain, wk, wv), refs = refs[:7], refs[7:]
    outs, refs = refs[:cores], refs[cores:]
    (part, own, received, raw, gain_held, key_low, value_low, bk, bv, held), refs = (
        refs[:10],
        refs[10:],
    )
    in_sem, w_sem, out_sem = refs
    leg = own_leg(which)
    slots, tile = bk.shape[:2]
    loads = Loads(in_sem)
    waits = [
        loads.start(received_hbm, received),
        loads.start(own_hbm, own),
        loads.start(raw_hbm.at[:, pl.ds(0, raw.shape[-1])], raw),
        loads.start(k_gain, gain_held),
    ]
    streams = row_streams(leg, (wk, wv), (bk, bv), w_sem)
    part_wait = loads.start(part_hbm, part)
    head = k_gain.shape[-1]
    k_cols = raw.shape[-1]
    cos, sin = rotation(
        row_places(piece_bases(groups, cores, chips, rows), rows, head // 2), head
    )
    for copy in waits:
        copy.wait()
    gain_row = gain_held[0, pl.ds(leg, 1), :]
    for h in range(k_cols // head):
        cols = pl.ds(h * head, head)
        grad = own[:, cols] + received[:, cols].astype(f32)
        key_low[:, cols] = head_back(raw[:, cols], gain_row, cos, sin, grad).astype(bf16)
    value_cols = pl.ds(k_cols, k_cols)
    value_low[...] = (own[:, value_cols] + received[:, value_cols].astype(f32)).astype(bf16)
    split = SplitOut(held, outs, out_sem, len(groups), cores, rows, tile)
    for at in range(wk.shape[-2] // tile):
        for stream in streams:
            stream.wait(at)
        slot = at % slots
        value = lax.dot_general(
            key_low[...], bk[slot], contract_last, preferred_element_type=f32
        )
        value += lax.dot_general(
            value_low[...], bv[slot], contract_last, preferred_element_type=f32
        )
        if at == 0:
            part_wait.wait()
        split.write(at, value + part[:, pl.ds(at * tile, tile)])
    split.wait()


def hidden(which, layout, rows, part, own, received, raw, k_gain, wk, wv, covers=False):
    cores = layout[1]
    count = own.shape[0]
    width = wk.shape[-2]
    k_cols = wk.shape[-1]
    tile = widest_tile(width)
    tiles = width // tile
    slots = min(3, tiles)
    return pl.pallas_call(
        functools.partial(hidden_kernel, which, layout, rows),
        out_shape=[jax.ShapeDtypeStruct((count // cores, width), bf16)] * cores,
        in_specs=[anywhere] * 7,
        out_specs=[anywhere] * cores,
        scratch_shapes=[
            pltpu.VMEM(part.shape, part.dtype),
            pltpu.VMEM(own.shape, own.dtype),
            pltpu.VMEM(received.shape, received.dtype),
            pltpu.VMEM((count, k_cols), f32),
            pltpu.VMEM(k_gain.shape, f32),
            pltpu.VMEM((count, k_cols), bf16),
            pltpu.VMEM((count, k_cols), bf16),
            pltpu.VMEM((slots, tile, k_cols), bf16),
            pltpu.VMEM((slots, tile, k_cols), bf16),
            pltpu.VMEM((cores, count // cores, width), bf16),
            pltpu.SemaphoreType.DMA((5,)),
            pltpu.SemaphoreType.DMA((2, tiles)),
            pltpu.SemaphoreType.DMA((cores, tiles)),
        ],
        compiler_params=params(49),
        cost_estimate=cost(covers),
        name="hidden_grad",
    )(part, own, received, raw, k_gain, wk, wv)


class Group:
    def __init__(self):
        self.size = lax.axis_size("tp")
        self.cores = 2 if self.size % 2 == 0 else 1
        self.chips = self.size // self.cores
        index = lax.axis_index("tp")
        self.chip = index // self.cores
        self.core = index % self.cores

    def place(self, chip, core):
        return (chip % self.chips) * self.cores + core % self.cores

    def to_chip(self, value, ahead):
        pairs = [
            (self.place(chip, core), self.place(chip + ahead, core))
            for chip in range(self.chips)
            for core in range(self.cores)
        ]
        return lax.ppermute(value, "tp", pairs)

    def to_core(self, value, ahead):
        pairs = [
            (self.place(chip, core), self.place(chip, core + ahead))
            for chip in range(self.chips)
            for core in range(self.cores)
        ]
        return lax.ppermute(value, "tp", pairs)

    def spread(self, piece):
        return [piece] + [self.to_core(piece, -k) for k in range(1, self.cores)]

    def positions(self, groups, rows, block):
        inner = jnp.arange(rows, dtype=jnp.int32)
        parts = []
        for g in groups:
            for k in range(self.cores):
                owner = ((self.chip + g) % self.chips) * self.cores + (self.core + k) % self.cores
                parts.append((block * self.size + owner) * rows + inner)
        return jnp.concatenate(parts)


def after(value, *others):
    return lax.optimization_barrier((value,) + others)[0]


def shifted(value, by, first):
    size = lax.axis_size("ctx")
    pairs = [(i, i + by) for i in range(size) if 0 <= i + by < size and i >= first]
    return lax.ppermute(value, "ctx", pairs)


def passed_along(value, by):
    size = lax.axis_size("ctx")
    return lax.ppermute(value, "ctx", [(i, i + by) for i in range(size - by)])


def swapped(value):
    pairs = [(source, source ^ 1) for source in range(lax.axis_size("segment"))]
    return lax.ppermute(value, "segment", pairs)


def per_device(
    stash_inputs,
    stash_grads,
    plan,
    query_weight,
    key_weight,
    value_weight,
    out_weight,
    input_gain,
    output_gain,
    query_gain,
    key_gain,
):
    ahead, behind = 0, 1
    group = Group()
    cores, chips = group.cores, group.chips
    rows = stash_inputs.shape[2]
    head = query_gain.shape[-1]
    block_rows = rows * group.size
    reaches = min(WINDOW // block_rows, lax.axis_size("ctx") - 1)
    near_groups = (0,)
    far_groups = tuple(range(1, chips))
    near = (near_groups, cores, chips)
    far = (far_groups, cores, chips)
    every = (near_groups + far_groups, cores, chips)
    everything = (key_weight, value_weight, query_weight)
    gains = (query_gain, key_gain)

    def chip_pieces(value):
        return [group.to_chip(value, -g) for g in far_groups]

    def all_pieces(pieces):
        spread = []
        for piece in pieces:
            spread += group.spread(piece)
        return spread

    back_normed, ahead_normed = norm_rows(plan, stash_inputs, input_gain)
    back_far = chip_pieces(back_normed)
    back_near = group.spread(back_normed)
    kv_near, q_near, raw_near = project(
        behind, near, back_near, *gains, *everything, True, covers=True, first=True
    )
    near_chain = [kv_near]
    back_far = [after(piece, q_near) for piece in back_far]
    ahead_far = chip_pieces(after(ahead_normed, *back_far))
    far_pieces = all_pieces(back_far)
    if reaches > 0:
        near_chain.append(shifted(kv_near, 1, 0))
    kv_far, q_far, raw_far = project(
        behind, far, far_pieces, *gains, *everything, True, covers=True
    )
    kv_sent = after(kv_far, *near_chain)
    near_chain[-1] = after(near_chain[-1], *ahead_far)
    ahead_far = [after(piece, kv_far) for piece in ahead_far]
    ahead_pieces = group.spread(after(ahead_normed, kv_far)) + all_pieces(ahead_far)
    (kv_ahead,) = project(
        ahead, every, ahead_pieces, *gains, *everything, False, covers=True, parts=("kv",)
    )
    far_chain = [kv_far]
    q_ahead = None
    for step in range(1, reaches + 1):
        far_chain.append(shifted(kv_sent, 1, step - 1))
        if step < reaches:
            near_chain.append(shifted(after(near_chain[-1], kv_far), 1, step))
        if step == 2:
            (q_ahead,) = project(
                ahead,
                every,
                [after(ahead_pieces[0], kv_ahead, kv_sent)] + ahead_pieces[1:],
                *gains,
                *everything,
                False,
                covers=True,
                parts=("q",),
            )
        kv_sent = far_chain[-1]
        if step < reaches:
            beside = kv_ahead if q_ahead is None else q_ahead
            kv_sent = after(kv_sent, beside)
            near_chain[-1] = after(near_chain[-1], beside)
    if q_ahead is None:
        (q_ahead,) = project(
            ahead, every, ahead_pieces, *gains, *everything, False, parts=("q",)
        )
    out_rows = lax.dynamic_index_in_dim(
        after(out_weight, q_ahead, *far_chain[:-1])[0],
        1 - lax.axis_index("segment"),
        0,
        keepdims=False,
    )
    far_chain[-1] = after(far_chain[-1], out_rows)

    back_chunks = []
    for pair in zip(near_chain, far_chain):
        back_chunks += pair
    back_keys = (near_groups, far_groups)
    far_keep, far_send = attend(
        behind,
        far,
        back_keys,
        reaches,
        q_far,
        back_chunks,
        out_rows,
        head,
        rows,
    )
    far_sums = far_parts(group, rows, far_keep, far_send)
    far_terms = [group.to_chip(part, g) for g, part in zip(far_groups, far_sums)]
    near_keep, near_send = attend(
        behind,
        near,
        back_keys,
        reaches,
        after(q_near, far_sums[0]),
        back_chunks,
        out_rows,
        head,
        rows,
        covers=True,
    )
    ahead_chain = [kv_ahead]
    if reaches > 0:
        ahead_chain.append(shifted(after(kv_ahead, far_sums[0]), 1, 0))
    near_send = after(near_send, *far_terms, *ahead_chain)
    back_terms = [near_keep, group.to_core(near_send, 1)] + far_terms
    out_grad = finish_rows(
        "grad", behind, plan, back_terms, stash_inputs, stash_grads, output_gain
    )
    grad_far = chip_pieces(out_grad)
    grad_near = group.spread(out_grad)
    if reaches > 1:
        ahead_chain.append(shifted(after(ahead_chain[1], out_grad), 1, 1))
        grad_far = [after(piece, ahead_chain[2]) for piece in grad_far]
    for step in range(3, reaches + 1):
        ahead_chain.append(shifted(after(ahead_chain[-1], *grad_far), 1, step - 1))

    results = attend_back(
        behind,
        every,
        back_keys,
        reaches,
        grad_near + all_pieces(grad_far),
        (q_near, q_far),
        (raw_near, raw_far),
        back_chunks,
        query_gain,
        out_rows,
    )
    query_low = results[0]
    near_grads = results[1::2]
    far_grads = results[2::2]
    near_rows = near_grads[0].shape[0]
    near_part, far_part = query_hidden(
        behind, (near_rows, query_low.shape[0] - near_rows), query_low, query_weight, covers=True
    )

    def added(message, grads, distance):
        return (message.astype(f32) + grads[distance].astype(f32)).astype(bf16)

    far_back = after(far_grads[reaches], *ahead_chain)
    near_back = after(near_grads[reaches], *ahead_chain)
    near_sent = near_back
    beside = near_part
    ahead_keep = None
    for distance in range(reaches, 0, -1):
        near_sent = near_back
        far_back = shifted(far_back, -1, distance)
        near_back = shifted(near_back, -1, distance)
        if distance == 1:
            break
        far_back = added(after(far_back, beside), far_grads, distance - 1)
        near_back = added(after(near_back, beside), near_grads, distance - 1)
        if ahead_keep is None:
            ahead_keep, ahead_send = attend(
                ahead,
                every,
                (near_groups + far_groups,),
                reaches,
                after(q_ahead, far_back, near_back),
                ahead_chain,
                out_weight,
                head,
                rows,
                covers=True,
            )
            beside = ahead_keep
    if ahead_keep is None:
        ahead_keep, ahead_send = attend(
            ahead,
            every,
            (near_groups + far_groups,),
            reaches,
            after(q_ahead, near_part),
            ahead_chain,
            out_weight,
            head,
            rows,
        )
    ahead_sums = far_parts(group, rows, ahead_keep[rows:], ahead_send[rows:])
    ahead_terms = [ahead_keep[:rows], group.to_core(ahead_send[:rows], 1)] + [
        group.to_chip(part, g) for g, part in zip(far_groups, ahead_sums)
    ]

    kv_weights = (key_weight, value_weight)
    far_back = after(far_back, near_sent, *ahead_sums)
    far_keep, far_send = hidden(
        behind,
        far,
        rows,
        far_part,
        far_grads[0],
        far_back,
        raw_far,
        key_gain,
        *kv_weights,
        covers=True,
    )
    far_send = after(far_send, near_back, *ahead_terms[2:])
    far_sums = far_parts(group, rows, far_keep, far_send)
    far_terms = [group.to_chip(part, g) for g, part in zip(far_groups, far_sums)]
    forward_out = finish_rows(
        "forward",
        ahead,
        plan,
        [after(ahead_terms[0], far_sums[0])] + ahead_terms[1:],
        stash_inputs,
        stash_grads,
        output_gain,
    )
    arrived_act = swapped(forward_out)
    near_keep, near_send = hidden(
        behind,
        near,
        rows,
        after(near_part, forward_out),
        near_grads[0],
        after(near_back, far_sums[0]),
        raw_near,
        key_gain,
        *kv_weights,
        covers=True,
    )
    near_send = after(near_send, arrived_act, *far_terms)
    hidden_terms = [near_keep, group.to_core(near_send, 1)] + far_terms
    outgoing = finish_rows(
        "outgoing", behind, plan, hidden_terms, stash_inputs, stash_grads, input_gain
    )
    arrived_grad = swapped(after(outgoing, arrived_act))
    arrived_act = copied(arrived_act)
    return (arrived_act[None], arrived_grad[None])


def far_parts(group, rows, far_keep, far_send):
    far = far_keep.astype(f32) + group.to_core(far_send, 1).astype(f32)
    far = far.astype(bf16)
    return [far[(g - 1) * rows : g * rows] for g in range(1, group.chips)]


def solution(mesh):
    return jax.shard_map(
        per_device,
        mesh=mesh,
        in_specs=(
            P("segment", None, ("ctx", "tp"), None),
            P("segment", None, ("ctx", "tp"), None),
            P("segment", None),
            P("segment", None, None, "tp"),
            P("segment", None, None, "tp"),
            P("segment", None, None, "tp"),
            P("segment", None, "tp", None),
            P("segment", None, None),
            P("segment", None, None),
            P("segment", None, None),
            P("segment", None, None),
        ),
        out_specs=(P("segment", ("ctx", "tp"), None), P("segment", ("ctx", "tp"), None)),
        check_vma=False,
    )
```

```python
import functools
import math

import jax
import jax.numpy as jnp
from jax import lax
from jax.experimental import pallas as pl
from jax.experimental.pallas import tpu as pltpu
from jax.sharding import PartitionSpec as P

WINDOW = 1024

epsilon = 1e-06
rope_base = 10000.0
masked_score = -1e30
mebibyte = 1024 * 1024
f32 = jnp.float32
bf16 = jnp.bfloat16

whole = pl.BlockSpec(memory_space=pltpu.VMEM)
scalars = pl.BlockSpec(memory_space=pltpu.SMEM)
anywhere = pl.BlockSpec(memory_space=pl.ANY)


def params(mebibytes):
    return pltpu.CompilerParams(vmem_limit_bytes=int(mebibytes * mebibyte))


class Stream:
    def __init__(self, copies):
        self.copies = copies
        for copy in copies[:2]:
            copy.start()

    def wait(self, at):
        self.copies[at].wait()
        if at + 2 < len(self.copies):
            self.copies[at + 2].start()


def cost(covers):
    size = 64 * mebibyte if covers else 1
    return pl.CostEstimate(flops=1, bytes_accessed=size, transcendentals=0)


def widest_tile(width, limit=1024):
    best = 128
    for tile in range(128, limit + 1, 128):
        if width % tile == 0:
            best = tile
    return best


class Loads:
    def __init__(self, sem):
        self.sem = sem
        self.count = 0

    def start(self, source, target):
        copy = pltpu.make_async_copy(source, target, self.sem.at[self.count])
        copy.start()
        self.count += 1
        return copy


def own_leg(other):
    index = lax.axis_index("segment")
    return 1 - index if other else index


def piece_bases(groups, cores, chips, rows):
    index = lax.axis_index("tp")
    chip = index // cores
    core = index % cores
    begin = lax.axis_index("ctx") * (chips * cores * rows)
    return [
        begin + (((chip + g) % chips) * cores + (core + k) % cores) * rows
        for g in groups
        for k in range(cores)
    ]


def row_places(bases, rows, width):
    return jnp.concatenate(
        [lax.broadcasted_iota(jnp.int32, (rows, width), 0) + base for base in bases], axis=0
    )


def lane_places(bases, rows, back):
    shape = (1, len(bases) * rows)
    lane = lax.broadcasted_iota(jnp.int32, shape, 1)
    place = lane + (bases[0] - back)
    for at in range(1, len(bases)):
        place = jnp.where(lane >= at * rows, lane + (bases[at] - at * rows - back), place)
    return place


def rotation(places, head):
    lane = lax.broadcasted_iota(jnp.int32, places.shape, 1).astype(f32)
    angles = places.astype(f32) * jnp.exp(lane * (-2.0 / head * math.log(rope_base)))
    return jnp.cos(angles), jnp.sin(angles)


def mean_square_scale(value):
    return lax.rsqrt(jnp.mean(value * value, axis=-1, keepdims=True) + epsilon)


def norm_back(value, gain, grad):
    scale = mean_square_scale(value)
    weighted = grad * gain
    inner = jnp.mean(value * weighted, axis=-1, keepdims=True)
    return scale * weighted - value * (scale * scale * scale * inner)


def norm_kernel(plan, stash, gain, first, second, held, gain_held, picks, normed, sem, out_sem):
    loads = Loads(sem)
    waits = [
        loads.start(plan, picks),
        loads.start(stash.at[0], held),
        loads.start(gain, gain_held),
    ]
    for copy in waits:
        copy.wait()
    copies = []
    for which, out in ((1, first), (0, second)):
        value = held[picks[0, which]].astype(f32)
        scaled = value * mean_square_scale(value)
        normed[which] = (scaled * gain_held[0, pl.ds(own_leg(which), 1), :]).astype(bf16)
        copy = pltpu.make_async_copy(normed.at[which], out, out_sem.at[which])
        copy.start()
        copies.append(copy)
    for copy in copies:
        copy.wait()


def norm_rows(plan, stash, gain, covers=False):
    rows, width = stash.shape[-2:]
    shape = jax.ShapeDtypeStruct((rows, width), bf16)
    return pl.pallas_call(
        norm_kernel,
        out_shape=[shape, shape],
        in_specs=[anywhere] * 3,
        out_specs=[anywhere] * 2,
        scratch_shapes=[
            pltpu.VMEM(stash.shape[1:], bf16),
            pltpu.VMEM(gain.shape, f32),
            pltpu.SMEM(plan.shape, plan.dtype),
            pltpu.VMEM((2, rows, width), bf16),
            pltpu.SemaphoreType.DMA((3,)),
            pltpu.SemaphoreType.DMA((2,)),
        ],
        compiler_params=params(62.5),
        cost_estimate=cost(covers),
        name="norm_rows",
    )(plan, stash, gain)


def qkv_kernel(which, layout, parts, keep_raw, *refs):
    groups, cores, chips = layout
    count = len(groups) * cores
    pieces, refs = refs[:count], refs[count:]
    (q_gain, k_gain, wk, wv, wq), refs = refs[:5], refs[5:]
    names = [name for name in ("kv", "q") if name in parts] + ["raw"] * keep_raw
    outs, refs = dict(zip(names, refs)), refs[len(names) :]
    results, refs = dict(zip(names, refs)), refs[len(names) :]
    act, gains, wbuf, in_sem, w_sem, out_sem = refs
    leg = own_leg(which)
    head = q_gain.shape[-1]
    rows = pieces[0].shape[0]
    k_heads = wk.shape[-1] // head
    tiles = []
    for kind, weight in (("k", wk), ("v", wv), ("q", wq)):
        if (kind == "q") != ("q" in parts) and len(parts) == 1:
            continue
        for at in range(weight.shape[-1] // head):
            tiles.append((kind, weight, at))
    slots = wbuf.shape[0]
    stream = Stream(
        [
            pltpu.make_async_copy(
                weight.at[0, leg, :, pl.ds(h * head, head)], wbuf.at[at % slots], w_sem.at[at]
            )
            for at, (kind, weight, h) in enumerate(tiles)
        ]
    )
    loads = Loads(in_sem)
    waits = [
        loads.start(piece, act.at[pl.ds(at * rows, rows)]) for at, piece in enumerate(pieces)
    ]
    waits += [loads.start(gain, gains.at[at]) for at, gain in enumerate((q_gain, k_gain))]
    half = head // 2
    bases = piece_bases(groups, cores, chips, rows)
    cos, sin = rotation(row_places(bases, rows, half), head)
    for copy in waits:
        copy.wait()
    row_gains = {
        "q": gains[0, 0, pl.ds(leg, 1), :],
        "k": gains[1, 0, pl.ds(leg, 1), :],
    }
    copies = []

    def send(array, column, at):
        cols = pl.ds(column * head, head)
        copy = pltpu.make_async_copy(
            results[array].at[:, cols], outs[array].at[:, cols], out_sem.at[int(array == "raw"), at]
        )
        copy.start()
        copies.append(copy)

    for at, (kind, weight, h) in enumerate(tiles):
        stream.wait(at)
        raw = jnp.dot(act[...], wbuf[at % slots], preferred_element_type=f32)
        column = h if kind != "v" else k_heads + h
        array = "q" if kind == "q" else "kv"
        begin = column * head
        if kind == "v":
            results[array][:, pl.ds(begin, head)] = raw.astype(bf16)
        else:
            if keep_raw:
                raw_column = h if kind == "k" else k_heads + h
                results["raw"][:, pl.ds(raw_column * head, head)] = raw
                send("raw", raw_column, at)
            normed = raw * mean_square_scale(raw) * row_gains[kind]
            front = normed[:, :half]
            back = normed[:, half:]
            results[array][:, pl.ds(begin, half)] = (front * cos - back * sin).astype(bf16)
            results[array][:, pl.ds(begin + half, half)] = (back * cos + front * sin).astype(bf16)
        send(array, column, at)
    for copy in copies:
        copy.wait()


def project(which, layout, pieces, q_gain, k_gain, wk, wv, wq, keep_raw, covers=False, first=False, parts=("kv", "q")):
    rows, width = pieces[0].shape
    total = rows * len(pieces)
    head = q_gain.shape[-1]
    q_cols, k_cols = wq.shape[-1], wk.shape[-1]
    forms = [((total, 2 * k_cols), bf16)] * ("kv" in parts)
    forms += [((total, q_cols), bf16)] * ("q" in parts)
    tiles = sum(form[0][1] for form in forms) // head
    if keep_raw:
        forms.append(((total, k_cols + q_cols), f32))
    return pl.pallas_call(
        functools.partial(qkv_kernel, which, layout, parts, keep_raw),
        out_shape=[jax.ShapeDtypeStruct(*form) for form in forms],
        in_specs=[anywhere] * (len(pieces) + 5),
        out_specs=[anywhere] * len(forms),
        scratch_shapes=[pltpu.VMEM(*form) for form in forms]
        + [
            pltpu.VMEM((total, width), bf16),
            pltpu.VMEM((2,) + q_gain.shape, f32),
            pltpu.VMEM((3, width, head), bf16),
            pltpu.SemaphoreType.DMA((len(pieces) + 2,)),
            pltpu.SemaphoreType.DMA((tiles,)),
            pltpu.SemaphoreType.DMA((2, tiles)),
        ],
        compiler_params=params(57 if first else 49),
        cost_estimate=cost(covers),
        name="project_heads",
    )(*pieces, q_gain, k_gain, wk, wv, wq)


def visibility(query_place, key_place):
    seen = (
        (key_place >= 0) & (key_place <= query_place) & (key_place > query_place - WINDOW)
    )
    return jnp.where(seen, 0.0, masked_score).astype(f32)


def mask_of(q_groups, key_layout, cores, chips, rows, reaches):
    block = chips * cores * rows
    query_place = row_places(piece_bases(q_groups, cores, chips, rows), rows, 1)
    parts = []
    for distance in range(reaches + 1):
        for groups in key_layout:
            bases = piece_bases(groups, cores, chips, rows)
            parts.append(
                visibility(query_place, lane_places(bases, rows, distance * block))
            )
    return jnp.concatenate(parts, axis=1)


def weights_of(queries, keys, bias):
    scores = lax.dot_general(queries, keys, contract_last, preferred_element_type=f32)
    value = scores * queries.shape[-1] ** (-0.5) + bias
    raised = jnp.exp(value - jnp.max(value, axis=-1, keepdims=True))
    return raised * (1.0 / jnp.sum(raised, axis=-1, keepdims=True))


def load_chunks(loads, sources, held):
    waits = []
    start = 0
    for source in sources:
        size = source.shape[0]
        waits.append(loads.start(source, held.at[pl.ds(start, size)]))
        start += size
    return waits


def split_rows(value, groups, cores, rows):
    parts = []
    for g in range(groups):
        for k in range(cores):
            begin = (g * cores + k) * rows
            parts.append((k, g * rows, value[begin : begin + rows]))
    return parts


class SplitOut:
    def __init__(self, held, outs, sem, groups, cores, rows, tile):
        self.held, self.outs, self.sem = held, outs, sem
        self.groups, self.cores, self.rows, self.tile = groups, cores, rows, tile
        self.copies = []

    def write(self, at, value):
        cols = pl.ds(at * self.tile, self.tile)
        for k, begin, part in split_rows(value, self.groups, self.cores, self.rows):
            self.held[k, pl.ds(begin, self.rows), cols] = part.astype(bf16)
        for k in range(self.cores):
            copy = pltpu.make_async_copy(
                self.held.at[k, :, cols], self.outs[k].at[:, cols], self.sem.at[k, at]
            )
            copy.start()
            self.copies.append(copy)

    def wait(self):
        for copy in self.copies:
            copy.wait()


def attend_kernel(which, layout, key_layout, reaches, rows, head, *refs):
    groups, cores, chips = layout
    count = len(key_layout) * (reaches + 1)
    queries_hbm = refs[0]
    chunks_hbm = refs[1 : 1 + count]
    wo = refs[1 + count]
    outs = refs[2 + count : 2 + count + cores]
    refs = refs[2 + count + cores :]
    if len(wo.shape) == 2:
        queries, keys, context, held, in_sem, out_sem = refs
        wbuf = None
    else:
        queries, keys, context, wbuf, held, in_sem, w_sem, out_sem = refs
    leg = own_leg(which)
    loads = Loads(in_sem)
    waits = [loads.start(queries_hbm, queries)]
    waits += load_chunks(loads, chunks_hbm, keys)
    tile = widest_tile(wo.shape[-1])
    tiles = wo.shape[-1] // tile
    stream = Stream(
        []
        if wbuf is None
        else [
            pltpu.make_async_copy(
                wo.at[0, leg, :, pl.ds(at * tile, tile)], wbuf.at[at], w_sem.at[at]
            )
            for at in range(tiles)
        ]
    )
    k_heads = keys.shape[-1] // (2 * head)
    q_heads = queries.shape[-1] // head
    bias = mask_of(groups, key_layout, cores, chips, rows, reaches)
    for copy in waits:
        copy.wait()
    for h in range(q_heads):
        key_at = h * k_heads // q_heads
        key_cols = pl.ds(key_at * head, head)
        value_cols = pl.ds((k_heads + key_at) * head, head)
        weights = weights_of(queries[:, pl.ds(h * head, head)], keys[:, key_cols], bias)
        context[:, pl.ds(h * head, head)] = jnp.dot(
            weights.astype(bf16), keys[:, value_cols], preferred_element_type=f32
        ).astype(bf16)
        if wbuf is not None:
            stream.wait(h)
    split = SplitOut(held, outs, out_sem, len(groups), cores, rows, tile)
    for at in range(tiles):
        if wbuf is None:
            tile_rows = wo[:, pl.ds(at * tile, tile)]
        else:
            if at >= q_heads:
                stream.wait(at)
            tile_rows = wbuf[at]
        split.write(at, jnp.dot(context[...], tile_rows, preferred_element_type=f32))
    split.wait()


def attend(which, layout, key_layout, reaches, queries, chunks, wo, head, rows, covers=False):
    cores = layout[1]
    total, q_cols = queries.shape
    keys = sum(chunk.shape[0] for chunk in chunks)
    width = wo.shape[-1]
    tile = widest_tile(width)
    resident = wo.ndim == 2
    shape = jax.ShapeDtypeStruct((total // cores, width), bf16)
    return pl.pallas_call(
        functools.partial(attend_kernel, which, layout, key_layout, reaches, rows, head),
        out_shape=[shape] * cores,
        in_specs=[anywhere] * (len(chunks) + 1) + [whole if resident else anywhere],
        out_specs=[anywhere] * cores,
        scratch_shapes=[
            pltpu.VMEM((total, q_cols), bf16),
            pltpu.VMEM((keys, chunks[0].shape[-1]), bf16),
            pltpu.VMEM((total, q_cols), bf16),
        ]
        + [pltpu.VMEM((width // tile, q_cols, tile), bf16)] * (not resident)
        + [
            pltpu.VMEM((cores, total // cores, width), bf16),
            pltpu.SemaphoreType.DMA((len(chunks) + 1,)),
        ]
        + [pltpu.SemaphoreType.DMA((width // tile,))] * (not resident)
        + [pltpu.SemaphoreType.DMA((cores, width // tile))],
        compiler_params=params(36 if resident else 49),
        cost_estimate=cost(covers),
        name="attend_and_project",
    )(queries, *chunks, wo)


def summed(terms, begin, count):
    total = None
    for term in terms:
        at = begin if term.shape[0] > count else 0
        value = term[pl.ds(at, count), :].astype(f32)
        total = value if total is None else total + value
    return total


def row_kernel(kind, which, number, begin, plan, *refs):
    terms = refs[:number]
    stash, grads, gain, out, held, grad_held, gain_held, sem = refs[number:]
    batch = plan[0, which]
    count = out.shape[0]
    here = pl.ds(begin, count)
    loads = Loads(sem)
    waits = [loads.start(gain, gain_held)]
    if kind != "grad":
        waits.append(loads.start(stash.at[0, batch, here], held))
    if kind != "forward":
        waits.append(loads.start(grads.at[0, batch, here], grad_held))
    total = summed(terms, begin, count)
    for copy in waits:
        copy.wait()
    gain_row = gain_held[0, pl.ds(own_leg(which), 1), :]
    if kind == "grad":
        result = norm_back(total, gain_row, grad_held[...].astype(f32))
    elif kind == "forward":
        result = held[...].astype(f32) + total * mean_square_scale(total) * gain_row
    else:
        back = norm_back(held[...].astype(f32), gain_row, total)
        result = grad_held[...].astype(f32) + back
    out[...] = result.astype(bf16)


def finish_rows(kind, which, plan, terms, stash, grads, gain, half=None, covers=False):
    rows, width = stash.shape[-2:]
    begin, count = (0, rows) if half is None else half
    return pl.pallas_call(
        functools.partial(row_kernel, kind, which, len(terms), begin),
        out_shape=jax.ShapeDtypeStruct((count, width), bf16),
        in_specs=[scalars] + [whole] * len(terms) + [anywhere] * 3,
        out_specs=whole,
        scratch_shapes=[
            pltpu.VMEM((count, width), bf16),
            pltpu.VMEM((count, width), bf16),
            pltpu.VMEM(gain.shape, f32),
            pltpu.SemaphoreType.DMA((3,)),
        ],
        compiler_params=params(8),
        cost_estimate=cost(covers),
        name=kind + "_rows",
    )(plan, *terms, stash, grads, gain)


def copy_kernel(source, target, sem):
    copy = pltpu.make_async_copy(source, target, sem)
    copy.start()
    copy.wait()


def copied(value):
    return pl.pallas_call(
        copy_kernel,
        out_shape=jax.ShapeDtypeStruct(value.shape, value.dtype),
        in_specs=[anywhere],
        out_specs=anywhere,
        scratch_shapes=[pltpu.SemaphoreType.DMA],
        compiler_params=params(8),
        cost_estimate=cost(False),
        name="copied",
    )(value)


def head_back(raw, gain_row, cos, sin, grad):
    half = grad.shape[-1] // 2
    front = grad[:, :half]
    back = grad[:, half:]
    turned = jnp.concatenate([front * cos + back * sin, back * cos - front * sin], axis=-1)
    return norm_back(raw, gain_row, turned)


def attend_back_kernel(which, layout, key_layout, reaches, *refs):
    groups, cores, chips = layout
    pieces_count = len(groups) * cores
    halves = len(key_layout)
    count = halves * (reaches + 1)
    pieces, refs = refs[:pieces_count], refs[pieces_count:]
    queries_hbm, refs = refs[:halves], refs[halves:]
    raw_hbm, refs = refs[:halves], refs[halves:]
    chunks_hbm, refs = refs[:count], refs[count:]
    (q_gain, wo, low_hbm), refs = refs[:3], refs[3:]
    grads_hbm, refs = refs[:count], refs[count:]
    (queries, raw, keys, grads, sent), refs = refs[:5], refs[5:]
    resident = len(wo.shape) == 2
    if resident:
        (gain_held, query_low, act, context_grad, in_sem, out_sem) = refs
    else:
        (gain_held, query_low, act, context_grad, wbuf, in_sem, w_sem, out_sem) = refs
    leg = own_leg(which)
    rows = pieces[0].shape[0]
    head = q_gain.shape[-1]
    half = head // 2
    k_heads = keys.shape[-1] // (2 * head)
    q_heads = queries.shape[-1] // head
    q_cols = raw.shape[-1]
    loads = Loads(in_sem)
    early = [
        loads.start(piece, act.at[pl.ds(at * rows, rows)]) for at, piece in enumerate(pieces)
    ]
    stream = Stream(
        []
        if resident
        else [
            pltpu.make_async_copy(
                wo.at[0, leg, pl.ds(at * head, head), :], wbuf.at[at], w_sem.at[at]
            )
            for at in range(q_heads)
        ]
    )
    waits = [loads.start(q_gain, gain_held)]
    waits += load_chunks(loads, queries_hbm, queries)
    waits += load_chunks(loads, chunks_hbm, keys)
    raw_cols = pl.ds(raw_hbm[0].shape[-1] - q_cols, q_cols)
    waits += load_chunks(loads, [part.at[:, raw_cols] for part in raw_hbm], raw)
    cos, sin = rotation(row_places(piece_bases(groups, cores, chips, rows), rows, half), head)
    bias = mask_of(groups, key_layout, cores, chips, rows, reaches)
    for copy in early:
        copy.wait()
    for h in range(q_heads):
        if resident:
            head_rows = wo[pl.ds(h * head, head), :]
        else:
            stream.wait(h)
            head_rows = wbuf[h]
        context_grad[:, pl.ds(h * head, head)] = lax.dot_general(
            act[...], head_rows, contract_last, preferred_element_type=f32
        ).astype(bf16)
    for copy in waits:
        copy.wait()
    gain_row = gain_held[0, pl.ds(leg, 1), :]
    outs = []

    def send(source, target):
        copy = pltpu.make_async_copy(source, target, out_sem.at[len(outs)])
        copy.start()
        outs.append(copy)

    own = grads.shape[0]
    for h in range(q_heads):
        key_at = h * k_heads // q_heads
        first = h == 0 or (h - 1) * k_heads // q_heads != key_at
        last = h == q_heads - 1 or (h + 1) * k_heads // q_heads != key_at
        key_cols = pl.ds(key_at * head, head)
        value_cols = pl.ds((k_heads + key_at) * head, head)
        query_cols = pl.ds(h * head, head)
        query = queries[:, query_cols]
        upper = context_grad[:, query_cols]
        weights = weights_of(query, keys[:, key_cols], bias)
        weight_grad = lax.dot_general(
            upper, keys[:, value_cols], contract_last, preferred_element_type=f32
        )
        inner = jnp.sum(weight_grad * weights, axis=-1, keepdims=True)
        score_grad = (weights * (weight_grad - inner) * head ** (-0.5)).astype(bf16)
        query_grad = jnp.dot(score_grad, keys[:, key_cols], preferred_element_type=f32)
        key_term = lax.dot_general(score_grad, query, contract_first, preferred_element_type=f32)
        value_term = lax.dot_general(
            weights.astype(bf16), upper, contract_first, preferred_element_type=f32
        )
        for cols, term in ((key_cols, key_term), (value_cols, value_term)):
            if not first:
                term = term + grads[:, cols]
            if not last:
                grads[:, cols] = term
                continue
            sent[:, cols] = term.astype(bf16)
            start = 0
            for at, target in enumerate(grads_hbm):
                size = target.shape[0]
                here = pl.ds(start, size)
                if at < halves:
                    grads[here, cols] = term[start : start + size]
                    send(grads.at[here, cols], target.at[:, cols])
                else:
                    send(sent.at[here, cols], target.at[:, cols])
                start += size
        query_low[:, query_cols] = head_back(
            raw[:, query_cols], gain_row, cos, sin, query_grad
        ).astype(bf16)
        send(query_low.at[:, query_cols], low_hbm.at[:, query_cols])
    for copy in outs:
        copy.wait()


def attend_back(which, layout, key_layout, reaches, pieces, queries, raw, chunks, q_gain, wo, covers=False):
    total = sum(part.shape[0] for part in queries)
    q_cols = queries[0].shape[-1]
    head = q_gain.shape[-1]
    keys = sum(chunk.shape[0] for chunk in chunks)
    cols = chunks[0].shape[-1]
    width = wo.shape[-1]
    k_heads = cols // (2 * head)
    q_heads = q_cols // head
    halves = len(key_layout)
    inputs = len(pieces) + 2 * halves + len(chunks) + 1
    resident = wo.ndim == 2
    return pl.pallas_call(
        functools.partial(attend_back_kernel, which, layout, key_layout, reaches),
        out_shape=[jax.ShapeDtypeStruct((total, q_cols), bf16)]
        + [
            jax.ShapeDtypeStruct(chunk.shape, f32 if at < halves else bf16)
            for at, chunk in enumerate(chunks)
        ],
        in_specs=[anywhere] * inputs + [whole if resident else anywhere],
        out_specs=[anywhere] * (1 + len(chunks)),
        scratch_shapes=[
            pltpu.VMEM((total, q_cols), bf16),
            pltpu.VMEM((total, q_cols), f32),
            pltpu.VMEM((keys, cols), bf16),
            pltpu.VMEM((keys, cols), f32),
            pltpu.VMEM((keys, cols), bf16),
            pltpu.VMEM(q_gain.shape, f32),
            pltpu.VMEM((total, q_cols), bf16),
            pltpu.VMEM((total, width), bf16),
            pltpu.VMEM((total, q_cols), bf16),
        ]
        + [pltpu.VMEM((q_heads, head, width), bf16)] * (not resident)
        + [pltpu.SemaphoreType.DMA((inputs,))]
        + [pltpu.SemaphoreType.DMA((q_heads,))] * (not resident)
        + [pltpu.SemaphoreType.DMA((2 * k_heads * len(chunks) + q_heads,))],
        compiler_params=params(36 if resident else 49),
        cost_estimate=cost(covers),
        name="attend_back",
    )(*pieces, *queries, *raw, *chunks, q_gain, wo)


contract_last = (((1,), (1,)), ((), ()))
contract_first = (((0,), (0,)), ((), ()))


def row_streams(leg, weights, buffers, sem):
    slots, tile = buffers[0].shape[:2]
    return [
        Stream(
            [
                pltpu.make_async_copy(
                    weight.at[0, leg, pl.ds(at * tile, tile), :],
                    buffer.at[at % slots],
                    sem.at[j, at],
                )
                for at in range(weight.shape[-2] // tile)
            ]
        )
        for j, (weight, buffer) in enumerate(zip(weights, buffers))
    ]


def query_hidden_kernel(which, parts, query_hbm, wq, *refs):
    outs, refs = refs[: len(parts)], refs[len(parts) :]
    query, buffer, held, in_sem, w_sem, out_sem = refs
    copy = pltpu.make_async_copy(query_hbm, query, in_sem)
    copy.start()
    (stream,) = row_streams(own_leg(which), [wq], [buffer], w_sem)
    slots, tile = buffer.shape[:2]
    copy.wait()
    copies = []
    for at in range(wq.shape[-2] // tile):
        stream.wait(at)
        cols = pl.ds(at * tile, tile)
        held[:, cols] = lax.dot_general(
            query[...], buffer[at % slots], contract_last, preferred_element_type=f32
        )
        start = 0
        for j, size in enumerate(parts):
            copy = pltpu.make_async_copy(
                held.at[pl.ds(start, size), cols], outs[j].at[:, cols], out_sem.at[j, at]
            )
            copy.start()
            copies.append(copy)
            start += size
    for copy in copies:
        copy.wait()


def query_hidden(which, parts, query_low, wq, covers=False):
    total, q_cols = query_low.shape
    width = wq.shape[-2]
    tile = widest_tile(width)
    tiles = width // tile
    return pl.pallas_call(
        functools.partial(query_hidden_kernel, which, parts),
        out_shape=[jax.ShapeDtypeStruct((size, width), f32) for size in parts],
        in_specs=[anywhere] * 2,
        out_specs=[anywhere] * len(parts),
        scratch_shapes=[
            pltpu.VMEM((total, q_cols), bf16),
            pltpu.VMEM((min(3, tiles), tile, q_cols), bf16),
            pltpu.VMEM((total, width), f32),
            pltpu.SemaphoreType.DMA,
            pltpu.SemaphoreType.DMA((1, tiles)),
            pltpu.SemaphoreType.DMA((len(parts), tiles)),
        ],
        compiler_params=params(49),
        cost_estimate=cost(covers),
        name="query_hidden",
    )(query_low, wq)


def hidden_kernel(which, layout, rows, *refs):
    groups, cores, chips = layout
    (part_hbm, own_hbm, received_hbm, raw_hbm, k_gain, wk, wv), refs = refs[:7], refs[7:]
    outs, refs = refs[:cores], refs[cores:]
    (part, own, received, raw, gain_held, key_low, value_low, bk, bv, held), refs = (
        refs[:10],
        refs[10:],
    )
    in_sem, w_sem, out_sem = refs
    leg = own_leg(which)
    slots, tile = bk.shape[:2]
    loads = Loads(in_sem)
    waits = [
        loads.start(received_hbm, received),
        loads.start(own_hbm, own),
        loads.start(raw_hbm.at[:, pl.ds(0, raw.shape[-1])], raw),
        loads.start(k_gain, gain_held),
    ]
    streams = row_streams(leg, (wk, wv), (bk, bv), w_sem)
    part_wait = loads.start(part_hbm, part)
    head = k_gain.shape[-1]
    k_cols = raw.shape[-1]
    cos, sin = rotation(
        row_places(piece_bases(groups, cores, chips, rows), rows, head // 2), head
    )
    for copy in waits:
        copy.wait()
    gain_row = gain_held[0, pl.ds(leg, 1), :]
    for h in range(k_cols // head):
        cols = pl.ds(h * head, head)
        grad = own[:, cols] + received[:, cols].astype(f32)
        key_low[:, cols] = head_back(raw[:, cols], gain_row, cos, sin, grad).astype(bf16)
    value_cols = pl.ds(k_cols, k_cols)
    value_low[...] = (own[:, value_cols] + received[:, value_cols].astype(f32)).astype(bf16)
    split = SplitOut(held, outs, out_sem, len(groups), cores, rows, tile)
    for at in range(wk.shape[-2] // tile):
        for stream in streams:
            stream.wait(at)
        slot = at % slots
        value = lax.dot_general(
            key_low[...], bk[slot], contract_last, preferred_element_type=f32
        )
        value += lax.dot_general(
            value_low[...], bv[slot], contract_last, preferred_element_type=f32
        )
        if at == 0:
            part_wait.wait()
        split.write(at, value + part[:, pl.ds(at * tile, tile)])
    split.wait()


def hidden(which, layout, rows, part, own, received, raw, k_gain, wk, wv, covers=False):
    cores = layout[1]
    count = own.shape[0]
    width = wk.shape[-2]
    k_cols = wk.shape[-1]
    tile = widest_tile(width)
    tiles = width // tile
    slots = min(3, tiles)
    return pl.pallas_call(
        functools.partial(hidden_kernel, which, layout, rows),
        out_shape=[jax.ShapeDtypeStruct((count // cores, width), bf16)] * cores,
        in_specs=[anywhere] * 7,
        out_specs=[anywhere] * cores,
        scratch_shapes=[
            pltpu.VMEM(part.shape, part.dtype),
            pltpu.VMEM(own.shape, own.dtype),
            pltpu.VMEM(received.shape, received.dtype),
            pltpu.VMEM((count, k_cols), f32),
            pltpu.VMEM(k_gain.shape, f32),
            pltpu.VMEM((count, k_cols), bf16),
            pltpu.VMEM((count, k_cols), bf16),
            pltpu.VMEM((slots, tile, k_cols), bf16),
            pltpu.VMEM((slots, tile, k_cols), bf16),
            pltpu.VMEM((cores, count // cores, width), bf16),
            pltpu.SemaphoreType.DMA((5,)),
            pltpu.SemaphoreType.DMA((2, tiles)),
            pltpu.SemaphoreType.DMA((cores, tiles)),
        ],
        compiler_params=params(49),
        cost_estimate=cost(covers),
        name="hidden_grad",
    )(part, own, received, raw, k_gain, wk, wv)


class Group:
    def __init__(self):
        self.size = lax.axis_size("tp")
        self.cores = 2 if self.size % 2 == 0 else 1
        self.chips = self.size // self.cores
        index = lax.axis_index("tp")
        self.chip = index // self.cores
        self.core = index % self.cores

    def place(self, chip, core):
        return (chip % self.chips) * self.cores + core % self.cores

    def to_chip(self, value, ahead):
        pairs = [
            (self.place(chip, core), self.place(chip + ahead, core))
            for chip in range(self.chips)
            for core in range(self.cores)
        ]
        return lax.ppermute(value, "tp", pairs)

    def to_core(self, value, ahead):
        pairs = [
            (self.place(chip, core), self.place(chip, core + ahead))
            for chip in range(self.chips)
            for core in range(self.cores)
        ]
        return lax.ppermute(value, "tp", pairs)

    def spread(self, piece):
        return [piece] + [self.to_core(piece, -k) for k in range(1, self.cores)]

    def positions(self, groups, rows, block):
        inner = jnp.arange(rows, dtype=jnp.int32)
        parts = []
        for g in groups:
            for k in range(self.cores):
                owner = ((self.chip + g) % self.chips) * self.cores + (self.core + k) % self.cores
                parts.append((block * self.size + owner) * rows + inner)
        return jnp.concatenate(parts)


def after(value, *others):
    return lax.optimization_barrier((value,) + others)[0]


def shifted(value, by, first):
    size = lax.axis_size("ctx")
    pairs = [(i, i + by) for i in range(size) if 0 <= i + by < size and i >= first]
    return lax.ppermute(value, "ctx", pairs)


def passed_along(value, by):
    size = lax.axis_size("ctx")
    return lax.ppermute(value, "ctx", [(i, i + by) for i in range(size - by)])


def swapped(value):
    pairs = [(source, source ^ 1) for source in range(lax.axis_size("segment"))]
    return lax.ppermute(value, "segment", pairs)


def per_device(
    stash_inputs,
    stash_grads,
    plan,
    query_weight,
    key_weight,
    value_weight,
    out_weight,
    input_gain,
    output_gain,
    query_gain,
    key_gain,
):
    ahead, behind = 0, 1
    group = Group()
    cores, chips = group.cores, group.chips
    rows = stash_inputs.shape[2]
    head = query_gain.shape[-1]
    block_rows = rows * group.size
    reaches = min(WINDOW // block_rows, lax.axis_size("ctx") - 1)
    near_groups = (0,)
    far_groups = tuple(range(1, chips))
    near = (near_groups, cores, chips)
    far = (far_groups, cores, chips)
    every = (near_groups + far_groups, cores, chips)
    everything = (key_weight, value_weight, query_weight)
    gains = (query_gain, key_gain)

    def chip_pieces(value):
        return [group.to_chip(value, -g) for g in far_groups]

    def all_pieces(pieces):
        spread = []
        for piece in pieces:
            spread += group.spread(piece)
        return spread

    back_normed, ahead_normed = norm_rows(plan, stash_inputs, input_gain)
    back_far = chip_pieces(back_normed)
    back_near = group.spread(back_normed)
    kv_near, q_near, raw_near = project(
        behind, near, back_near, *gains, *everything, True, covers=True, first=True
    )
    near_chain = [kv_near]
    back_far = [after(piece, q_near) for piece in back_far]
    ahead_far = chip_pieces(after(ahead_normed, *back_far))
    far_pieces = all_pieces(back_far)
    if reaches > 0:
        near_chain.append(shifted(kv_near, 1, 0))
    kv_far, q_far, raw_far = project(
        behind, far, far_pieces, *gains, *everything, True, covers=True
    )
    kv_sent = after(kv_far, *near_chain)
    near_chain[-1] = after(near_chain[-1], *ahead_far)
    ahead_far = [after(piece, kv_far) for piece in ahead_far]
    ahead_pieces = group.spread(after(ahead_normed, kv_far)) + all_pieces(ahead_far)
    (kv_ahead,) = project(
        ahead, every, ahead_pieces, *gains, *everything, False, covers=True, parts=("kv",)
    )
    far_chain = [kv_far]
    q_ahead = None
    for step in range(1, reaches + 1):
        far_chain.append(shifted(kv_sent, 1, step - 1))
        if step < reaches:
            near_chain.append(shifted(after(near_chain[-1], kv_far), 1, step))
        if step == 2:
            (q_ahead,) = project(
                ahead,
                every,
                [after(ahead_pieces[0], kv_ahead, kv_sent)] + ahead_pieces[1:],
                *gains,
                *everything,
                False,
                covers=True,
                parts=("q",),
            )
        kv_sent = far_chain[-1]
        if step < reaches:
            beside = kv_ahead if q_ahead is None else q_ahead
            kv_sent = after(kv_sent, beside)
            near_chain[-1] = after(near_chain[-1], beside)
    if q_ahead is None:
        (q_ahead,) = project(
            ahead, every, ahead_pieces, *gains, *everything, False, parts=("q",)
        )
    out_rows = lax.dynamic_index_in_dim(
        after(out_weight, q_ahead, *far_chain[:-1])[0],
        1 - lax.axis_index("segment"),
        0,
        keepdims=False,
    )
    far_chain[-1] = after(far_chain[-1], out_rows)

    back_chunks = []
    for pair in zip(near_chain, far_chain):
        back_chunks += pair
    back_keys = (near_groups, far_groups)
    far_keep, far_send = attend(
        behind,
        far,
        back_keys,
        reaches,
        q_far,
        back_chunks,
        out_rows,
        head,
        rows,
    )
    far_sums = far_parts(group, rows, far_keep, far_send)
    far_terms = [group.to_chip(part, g) for g, part in zip(far_groups, far_sums)]
    near_keep, near_send = attend(
        behind,
        near,
        back_keys,
        reaches,
        after(q_near, far_sums[0]),
        back_chunks,
        out_rows,
        head,
        rows,
        covers=True,
    )
    ahead_chain = [kv_ahead]
    if reaches > 0:
        ahead_chain.append(shifted(after(kv_ahead, far_sums[0]), 1, 0))
    near_send = after(near_send, *far_terms, *ahead_chain)
    back_terms = [near_keep, group.to_core(near_send, 1)] + far_terms
    out_grad = finish_rows(
        "grad", behind, plan, back_terms, stash_inputs, stash_grads, output_gain
    )
    grad_far = chip_pieces(out_grad)
    grad_near = group.spread(out_grad)
    if reaches > 1:
        ahead_chain.append(shifted(after(ahead_chain[1], out_grad), 1, 1))
        grad_far = [after(piece, ahead_chain[2]) for piece in grad_far]
    for step in range(3, reaches + 1):
        ahead_chain.append(shifted(after(ahead_chain[-1], *grad_far), 1, step - 1))

    results = attend_back(
        behind,
        every,
        back_keys,
        reaches,
        grad_near + all_pieces(grad_far),
        (q_near, q_far),
        (raw_near, raw_far),
        back_chunks,
        query_gain,
        out_rows,
    )
    query_low = results[0]
    near_grads = results[1::2]
    far_grads = results[2::2]
    near_rows = near_grads[0].shape[0]
    near_part, far_part = query_hidden(
        behind, (near_rows, query_low.shape[0] - near_rows), query_low, query_weight, covers=True
    )

    def added(message, grads, distance):
        return (message.astype(f32) + grads[distance].astype(f32)).astype(bf16)

    far_back = after(far_grads[reaches], *ahead_chain)
    near_back = after(near_grads[reaches], *ahead_chain)
    near_sent = near_back
    beside = near_part
    near_hops = {}
    ahead_keep = None
    for distance in range(reaches, 0, -1):
        near_sent = near_back
        far_back = shifted(far_back, -1, distance)
        if distance in near_hops:
            near_back = near_hops[distance]
        else:
            near_back = shifted(near_back, -1, distance)
        if distance == 1:
            break
        far_back = added(after(far_back, beside), far_grads, distance - 1)
        near_back = added(after(near_back, beside), near_grads, distance - 1)
        if ahead_keep is None:
            ahead_keep, ahead_send = attend(
                ahead,
                every,
                (near_groups + far_groups,),
                reaches,
                after(q_ahead, far_back, near_back),
                ahead_chain,
                out_weight,
                head,
                rows,
                covers=True,
            )
            beside = ahead_keep
            late_near = shifted(near_back, -1, distance - 1)
            ahead_send = after(ahead_send, late_near)
            near_hops[distance - 1] = late_near
    if ahead_keep is None:
        ahead_keep, ahead_send = attend(
            ahead,
            every,
            (near_groups + far_groups,),
            reaches,
            after(q_ahead, near_part),
            ahead_chain,
            out_weight,
            head,
            rows,
        )
    ahead_sums = far_parts(group, rows, ahead_keep[rows:], ahead_send[rows:])
    ahead_terms = [ahead_keep[:rows], group.to_core(ahead_send[:rows], 1)] + [
        group.to_chip(part, g) for g, part in zip(far_groups, ahead_sums)
    ]

    kv_weights = (key_weight, value_weight)
    far_back = after(far_back, near_sent, *ahead_sums)
    far_keep, far_send = hidden(
        behind,
        far,
        rows,
        far_part,
        far_grads[0],
        far_back,
        raw_far,
        key_gain,
        *kv_weights,
        covers=True,
    )
    far_send = after(far_send, near_back, *ahead_terms[2:])
    far_sums = far_parts(group, rows, far_keep, far_send)
    halves = ((0, rows // 2), (rows // 2, rows // 2))
    half_terms = [
        [
            group.to_chip(part[begin : begin + count], g)
            for g, part in zip(far_groups, far_sums)
        ]
        for begin, count in halves
    ]
    forward_out = finish_rows(
        "forward",
        ahead,
        plan,
        [after(ahead_terms[0], far_sums[0])] + ahead_terms[1:],
        stash_inputs,
        stash_grads,
        output_gain,
    )
    arrived_act = swapped(forward_out)
    near_keep, near_send = hidden(
        behind,
        near,
        rows,
        after(near_part, forward_out),
        near_grads[0],
        after(near_back, far_sums[0]),
        raw_near,
        key_gain,
        *kv_weights,
        covers=True,
    )
    near_send = after(near_send, arrived_act, *half_terms[0], *half_terms[1])
    near_terms = [near_keep, group.to_core(near_send, 1)]
    arrived_halves = []
    for half, terms in zip(halves, half_terms):
        outgoing = finish_rows(
            "outgoing",
            behind,
            plan,
            near_terms + terms,
            stash_inputs,
            stash_grads,
            input_gain,
            half=half,
        )
        arrived_halves.append(swapped(outgoing))
    arrived_grad = jnp.concatenate(arrived_halves, axis=0)
    arrived_act = copied(arrived_act)
    return (arrived_act[None], arrived_grad[None])


def far_parts(group, rows, far_keep, far_send):
    far = far_keep.astype(f32) + group.to_core(far_send, 1).astype(f32)
    far = far.astype(bf16)
    return [far[(g - 1) * rows : g * rows] for g in range(1, group.chips)]


def solution(mesh):
    return jax.shard_map(
        per_device,
        mesh=mesh,
        in_specs=(
            P("segment", None, ("ctx", "tp"), None),
            P("segment", None, ("ctx", "tp"), None),
            P("segment", None),
            P("segment", None, None, "tp"),
            P("segment", None, None, "tp"),
            P("segment", None, None, "tp"),
            P("segment", None, "tp", None),
            P("segment", None, None),
            P("segment", None, None),
            P("segment", None, None),
            P("segment", None, None),
        ),
        out_specs=(P("segment", ("ctx", "tp"), None), P("segment", ("ctx", "tp"), None)),
        check_vma=False,
    )
```

```python
import functools
import math

import jax
import jax.numpy as jnp
from jax import lax
from jax.experimental import pallas as pl
from jax.experimental.pallas import tpu as pltpu
from jax.sharding import PartitionSpec as P

WINDOW = 1024

epsilon = 1e-06
rope_base = 10000.0
masked_score = -1e30
mebibyte = 1024 * 1024
f32 = jnp.float32
bf16 = jnp.bfloat16

whole = pl.BlockSpec(memory_space=pltpu.VMEM)
scalars = pl.BlockSpec(memory_space=pltpu.SMEM)
anywhere = pl.BlockSpec(memory_space=pl.ANY)


def params(mebibytes):
    return pltpu.CompilerParams(vmem_limit_bytes=int(mebibytes * mebibyte))


class Stream:
    def __init__(self, copies):
        self.copies = copies
        for copy in copies[:2]:
            copy.start()

    def wait(self, at):
        self.copies[at].wait()
        if at + 2 < len(self.copies):
            self.copies[at + 2].start()


def cost(covers):
    size = 64 * mebibyte if covers else 1
    return pl.CostEstimate(flops=1, bytes_accessed=size, transcendentals=0)


def widest_tile(width, limit=1024):
    best = 128
    for tile in range(128, limit + 1, 128):
        if width % tile == 0:
            best = tile
    return best


class Loads:
    def __init__(self, sem):
        self.sem = sem
        self.count = 0

    def start(self, source, target):
        copy = pltpu.make_async_copy(source, target, self.sem.at[self.count])
        copy.start()
        self.count += 1
        return copy


def own_leg(other):
    index = lax.axis_index("segment")
    return 1 - index if other else index


def piece_bases(groups, cores, chips, rows):
    index = lax.axis_index("tp")
    chip = index // cores
    core = index % cores
    begin = lax.axis_index("ctx") * (chips * cores * rows)
    return [
        begin + (((chip + g) % chips) * cores + (core + k) % cores) * rows
        for g in groups
        for k in range(cores)
    ]


def row_places(bases, rows, width):
    return jnp.concatenate(
        [lax.broadcasted_iota(jnp.int32, (rows, width), 0) + base for base in bases], axis=0
    )


def lane_places(bases, rows, back):
    shape = (1, len(bases) * rows)
    lane = lax.broadcasted_iota(jnp.int32, shape, 1)
    place = lane + (bases[0] - back)
    for at in range(1, len(bases)):
        place = jnp.where(lane >= at * rows, lane + (bases[at] - at * rows - back), place)
    return place


def rotation(places, head):
    lane = lax.broadcasted_iota(jnp.int32, places.shape, 1).astype(f32)
    angles = places.astype(f32) * jnp.exp(lane * (-2.0 / head * math.log(rope_base)))
    return jnp.cos(angles), jnp.sin(angles)


def mean_square_scale(value):
    return lax.rsqrt(jnp.mean(value * value, axis=-1, keepdims=True) + epsilon)


def norm_back(value, gain, grad):
    scale = mean_square_scale(value)
    weighted = grad * gain
    inner = jnp.mean(value * weighted, axis=-1, keepdims=True)
    return scale * weighted - value * (scale * scale * scale * inner)


def norm_kernel(plan, stash, gain, first, second, held, gain_held, picks, normed, sem, out_sem):
    loads = Loads(sem)
    waits = [
        loads.start(plan, picks),
        loads.start(stash.at[0], held),
        loads.start(gain, gain_held),
    ]
    for copy in waits:
        copy.wait()
    copies = []
    for which, out in ((1, first), (0, second)):
        value = held[picks[0, which]].astype(f32)
        scaled = value * mean_square_scale(value)
        normed[which] = (scaled * gain_held[0, pl.ds(own_leg(which), 1), :]).astype(bf16)
        copy = pltpu.make_async_copy(normed.at[which], out, out_sem.at[which])
        copy.start()
        copies.append(copy)
    for copy in copies:
        copy.wait()


def norm_rows(plan, stash, gain, covers=False):
    rows, width = stash.shape[-2:]
    shape = jax.ShapeDtypeStruct((rows, width), bf16)
    return pl.pallas_call(
        norm_kernel,
        out_shape=[shape, shape],
        in_specs=[anywhere] * 3,
        out_specs=[anywhere] * 2,
        scratch_shapes=[
            pltpu.VMEM(stash.shape[1:], bf16),
            pltpu.VMEM(gain.shape, f32),
            pltpu.SMEM(plan.shape, plan.dtype),
            pltpu.VMEM((2, rows, width), bf16),
            pltpu.SemaphoreType.DMA((3,)),
            pltpu.SemaphoreType.DMA((2,)),
        ],
        compiler_params=params(62.5),
        cost_estimate=cost(covers),
        name="norm_rows",
    )(plan, stash, gain)


def qkv_kernel(which, layout, parts, keep_raw, *refs):
    groups, cores, chips = layout
    count = len(groups) * cores
    pieces, refs = refs[:count], refs[count:]
    (q_gain, k_gain, wk, wv, wq), refs = refs[:5], refs[5:]
    names = [name for name in ("kv", "q") if name in parts] + ["raw"] * keep_raw
    outs, refs = dict(zip(names, refs)), refs[len(names) :]
    results, refs = dict(zip(names, refs)), refs[len(names) :]
    act, gains, wbuf, in_sem, w_sem, out_sem = refs
    leg = own_leg(which)
    head = q_gain.shape[-1]
    rows = pieces[0].shape[0]
    k_heads = wk.shape[-1] // head
    tiles = []
    for kind, weight in (("k", wk), ("v", wv), ("q", wq)):
        if (kind == "q") != ("q" in parts) and len(parts) == 1:
            continue
        for at in range(weight.shape[-1] // head):
            tiles.append((kind, weight, at))
    slots = wbuf.shape[0]
    stream = Stream(
        [
            pltpu.make_async_copy(
                weight.at[0, leg, :, pl.ds(h * head, head)], wbuf.at[at % slots], w_sem.at[at]
            )
            for at, (kind, weight, h) in enumerate(tiles)
        ]
    )
    loads = Loads(in_sem)
    waits = [
        loads.start(piece, act.at[pl.ds(at * rows, rows)]) for at, piece in enumerate(pieces)
    ]
    waits += [loads.start(gain, gains.at[at]) for at, gain in enumerate((q_gain, k_gain))]
    half = head // 2
    bases = piece_bases(groups, cores, chips, rows)
    cos, sin = rotation(row_places(bases, rows, half), head)
    for copy in waits:
        copy.wait()
    row_gains = {
        "q": gains[0, 0, pl.ds(leg, 1), :],
        "k": gains[1, 0, pl.ds(leg, 1), :],
    }
    copies = []

    def send(array, column, at):
        cols = pl.ds(column * head, head)
        copy = pltpu.make_async_copy(
            results[array].at[:, cols], outs[array].at[:, cols], out_sem.at[int(array == "raw"), at]
        )
        copy.start()
        copies.append(copy)

    for at, (kind, weight, h) in enumerate(tiles):
        stream.wait(at)
        raw = jnp.dot(act[...], wbuf[at % slots], preferred_element_type=f32)
        column = h if kind != "v" else k_heads + h
        array = "q" if kind == "q" else "kv"
        begin = column * head
        if kind == "v":
            results[array][:, pl.ds(begin, head)] = raw.astype(bf16)
        else:
            if keep_raw:
                raw_column = h if kind == "k" else k_heads + h
                results["raw"][:, pl.ds(raw_column * head, head)] = raw
                send("raw", raw_column, at)
            normed = raw * mean_square_scale(raw) * row_gains[kind]
            front = normed[:, :half]
            back = normed[:, half:]
            results[array][:, pl.ds(begin, half)] = (front * cos - back * sin).astype(bf16)
            results[array][:, pl.ds(begin + half, half)] = (back * cos + front * sin).astype(bf16)
        send(array, column, at)
    for copy in copies:
        copy.wait()


def project(which, layout, pieces, q_gain, k_gain, wk, wv, wq, keep_raw, covers=False, first=False, parts=("kv", "q")):
    rows, width = pieces[0].shape
    total = rows * len(pieces)
    head = q_gain.shape[-1]
    q_cols, k_cols = wq.shape[-1], wk.shape[-1]
    forms = [((total, 2 * k_cols), bf16)] * ("kv" in parts)
    forms += [((total, q_cols), bf16)] * ("q" in parts)
    tiles = sum(form[0][1] for form in forms) // head
    if keep_raw:
        forms.append(((total, k_cols + q_cols), f32))
    return pl.pallas_call(
        functools.partial(qkv_kernel, which, layout, parts, keep_raw),
        out_shape=[jax.ShapeDtypeStruct(*form) for form in forms],
        in_specs=[anywhere] * (len(pieces) + 5),
        out_specs=[anywhere] * len(forms),
        scratch_shapes=[pltpu.VMEM(*form) for form in forms]
        + [
            pltpu.VMEM((total, width), bf16),
            pltpu.VMEM((2,) + q_gain.shape, f32),
            pltpu.VMEM((3, width, head), bf16),
            pltpu.SemaphoreType.DMA((len(pieces) + 2,)),
            pltpu.SemaphoreType.DMA((tiles,)),
            pltpu.SemaphoreType.DMA((2, tiles)),
        ],
        compiler_params=params(57 if first else 49),
        cost_estimate=cost(covers),
        name="project_heads",
    )(*pieces, q_gain, k_gain, wk, wv, wq)


def visibility(query_place, key_place):
    seen = (
        (key_place >= 0) & (key_place <= query_place) & (key_place > query_place - WINDOW)
    )
    return jnp.where(seen, 0.0, masked_score).astype(f32)


def mask_of(q_groups, key_layout, cores, chips, rows, reaches):
    block = chips * cores * rows
    query_place = row_places(piece_bases(q_groups, cores, chips, rows), rows, 1)
    parts = []
    for distance in range(reaches + 1):
        for groups in key_layout:
            bases = piece_bases(groups, cores, chips, rows)
            parts.append(
                visibility(query_place, lane_places(bases, rows, distance * block))
            )
    return jnp.concatenate(parts, axis=1)


def weights_of(queries, keys, bias):
    scores = lax.dot_general(queries, keys, contract_last, preferred_element_type=f32)
    value = scores * queries.shape[-1] ** (-0.5) + bias
    raised = jnp.exp(value - jnp.max(value, axis=-1, keepdims=True))
    return raised * (1.0 / jnp.sum(raised, axis=-1, keepdims=True))


def load_chunks(loads, sources, held):
    waits = []
    start = 0
    for source in sources:
        size = source.shape[0]
        waits.append(loads.start(source, held.at[pl.ds(start, size)]))
        start += size
    return waits


def split_rows(value, groups, cores, rows):
    parts = []
    for g in range(groups):
        for k in range(cores):
            begin = (g * cores + k) * rows
            parts.append((k, g * rows, value[begin : begin + rows]))
    return parts


class SplitOut:
    def __init__(self, held, outs, sem, groups, cores, rows, tile):
        self.held, self.outs, self.sem = held, outs, sem
        self.groups, self.cores, self.rows, self.tile = groups, cores, rows, tile
        self.copies = []

    def write(self, at, value):
        cols = pl.ds(at * self.tile, self.tile)
        for k, begin, part in split_rows(value, self.groups, self.cores, self.rows):
            self.held[k, pl.ds(begin, self.rows), cols] = part.astype(bf16)
        for k in range(self.cores):
            copy = pltpu.make_async_copy(
                self.held.at[k, :, cols], self.outs[k].at[:, cols], self.sem.at[k, at]
            )
            copy.start()
            self.copies.append(copy)

    def wait(self):
        for copy in self.copies:
            copy.wait()


def attend_kernel(which, layout, key_layout, reaches, rows, head, *refs):
    groups, cores, chips = layout
    count = len(key_layout) * (reaches + 1)
    queries_hbm = refs[0]
    chunks_hbm = refs[1 : 1 + count]
    wo = refs[1 + count]
    outs = refs[2 + count : 2 + count + cores]
    refs = refs[2 + count + cores :]
    if len(wo.shape) == 2:
        queries, keys, context, held, in_sem, out_sem = refs
        wbuf = None
    else:
        queries, keys, context, wbuf, held, in_sem, w_sem, out_sem = refs
    leg = own_leg(which)
    loads = Loads(in_sem)
    waits = [loads.start(queries_hbm, queries)]
    waits += load_chunks(loads, chunks_hbm, keys)
    tile = widest_tile(wo.shape[-1])
    tiles = wo.shape[-1] // tile
    stream = Stream(
        []
        if wbuf is None
        else [
            pltpu.make_async_copy(
                wo.at[0, leg, :, pl.ds(at * tile, tile)], wbuf.at[at], w_sem.at[at]
            )
            for at in range(tiles)
        ]
    )
    k_heads = keys.shape[-1] // (2 * head)
    q_heads = queries.shape[-1] // head
    bias = mask_of(groups, key_layout, cores, chips, rows, reaches)
    for copy in waits:
        copy.wait()
    for h in range(q_heads):
        key_at = h * k_heads // q_heads
        key_cols = pl.ds(key_at * head, head)
        value_cols = pl.ds((k_heads + key_at) * head, head)
        weights = weights_of(queries[:, pl.ds(h * head, head)], keys[:, key_cols], bias)
        context[:, pl.ds(h * head, head)] = jnp.dot(
            weights.astype(bf16), keys[:, value_cols], preferred_element_type=f32
        ).astype(bf16)
        if wbuf is not None:
            stream.wait(h)
    split = SplitOut(held, outs, out_sem, len(groups), cores, rows, tile)
    for at in range(tiles):
        if wbuf is None:
            tile_rows = wo[:, pl.ds(at * tile, tile)]
        else:
            if at >= q_heads:
                stream.wait(at)
            tile_rows = wbuf[at]
        split.write(at, jnp.dot(context[...], tile_rows, preferred_element_type=f32))
    split.wait()


def attend(which, layout, key_layout, reaches, queries, chunks, wo, head, rows, covers=False):
    cores = layout[1]
    total, q_cols = queries.shape
    keys = sum(chunk.shape[0] for chunk in chunks)
    width = wo.shape[-1]
    tile = widest_tile(width)
    resident = wo.ndim == 2
    shape = jax.ShapeDtypeStruct((total // cores, width), bf16)
    return pl.pallas_call(
        functools.partial(attend_kernel, which, layout, key_layout, reaches, rows, head),
        out_shape=[shape] * cores,
        in_specs=[anywhere] * (len(chunks) + 1) + [whole if resident else anywhere],
        out_specs=[anywhere] * cores,
        scratch_shapes=[
            pltpu.VMEM((total, q_cols), bf16),
            pltpu.VMEM((keys, chunks[0].shape[-1]), bf16),
            pltpu.VMEM((total, q_cols), bf16),
        ]
        + [pltpu.VMEM((width // tile, q_cols, tile), bf16)] * (not resident)
        + [
            pltpu.VMEM((cores, total // cores, width), bf16),
            pltpu.SemaphoreType.DMA((len(chunks) + 1,)),
        ]
        + [pltpu.SemaphoreType.DMA((width // tile,))] * (not resident)
        + [pltpu.SemaphoreType.DMA((cores, width // tile))],
        compiler_params=params(36 if resident else 49),
        cost_estimate=cost(covers),
        name="attend_and_project",
    )(queries, *chunks, wo)


def summed(terms, begin, count):
    total = None
    for term in terms:
        at = begin if term.shape[0] > count else 0
        value = term[pl.ds(at, count), :].astype(f32)
        total = value if total is None else total + value
    return total


def row_kernel(kind, which, number, begin, plan, *refs):
    terms = refs[:number]
    stash, grads, gain, out, held, grad_held, gain_held, sem = refs[number:]
    batch = plan[0, which]
    count = out.shape[0]
    here = pl.ds(begin, count)
    loads = Loads(sem)
    waits = [loads.start(gain, gain_held)]
    if kind != "grad":
        waits.append(loads.start(stash.at[0, batch, here], held))
    if kind != "forward":
        waits.append(loads.start(grads.at[0, batch, here], grad_held))
    total = summed(terms, begin, count)
    for copy in waits:
        copy.wait()
    gain_row = gain_held[0, pl.ds(own_leg(which), 1), :]
    if kind == "grad":
        result = norm_back(total, gain_row, grad_held[...].astype(f32))
    elif kind == "forward":
        result = held[...].astype(f32) + total * mean_square_scale(total) * gain_row
    else:
        back = norm_back(held[...].astype(f32), gain_row, total)
        result = grad_held[...].astype(f32) + back
    out[...] = result.astype(bf16)


def finish_rows(kind, which, plan, terms, stash, grads, gain, half=None, covers=False):
    rows, width = stash.shape[-2:]
    begin, count = (0, rows) if half is None else half
    return pl.pallas_call(
        functools.partial(row_kernel, kind, which, len(terms), begin),
        out_shape=jax.ShapeDtypeStruct((count, width), bf16),
        in_specs=[scalars] + [whole] * len(terms) + [anywhere] * 3,
        out_specs=whole,
        scratch_shapes=[
            pltpu.VMEM((count, width), bf16),
            pltpu.VMEM((count, width), bf16),
            pltpu.VMEM(gain.shape, f32),
            pltpu.SemaphoreType.DMA((3,)),
        ],
        compiler_params=params(8),
        cost_estimate=cost(covers),
        name=kind + "_rows",
    )(plan, *terms, stash, grads, gain)


def copy_kernel(source, target, sem):
    copy = pltpu.make_async_copy(source, target, sem)
    copy.start()
    copy.wait()


def copied(value):
    return pl.pallas_call(
        copy_kernel,
        out_shape=jax.ShapeDtypeStruct(value.shape, value.dtype),
        in_specs=[anywhere],
        out_specs=anywhere,
        scratch_shapes=[pltpu.SemaphoreType.DMA],
        compiler_params=params(8),
        cost_estimate=cost(False),
        name="copied",
    )(value)


def head_back(raw, gain_row, cos, sin, grad):
    half = grad.shape[-1] // 2
    front = grad[:, :half]
    back = grad[:, half:]
    turned = jnp.concatenate([front * cos + back * sin, back * cos - front * sin], axis=-1)
    return norm_back(raw, gain_row, turned)


def attend_back_kernel(which, layout, key_layout, reaches, *refs):
    groups, cores, chips = layout
    pieces_count = len(groups) * cores
    halves = len(key_layout)
    count = halves * (reaches + 1)
    pieces, refs = refs[:pieces_count], refs[pieces_count:]
    queries_hbm, refs = refs[:halves], refs[halves:]
    raw_hbm, refs = refs[:halves], refs[halves:]
    chunks_hbm, refs = refs[:count], refs[count:]
    (q_gain, wo, low_hbm), refs = refs[:3], refs[3:]
    grads_hbm, refs = refs[:count], refs[count:]
    (queries, raw, keys, grads, sent), refs = refs[:5], refs[5:]
    resident = len(wo.shape) == 2
    if resident:
        (gain_held, query_low, act, context_grad, in_sem, out_sem) = refs
    else:
        (gain_held, query_low, act, context_grad, wbuf, in_sem, w_sem, out_sem) = refs
    leg = own_leg(which)
    rows = pieces[0].shape[0]
    head = q_gain.shape[-1]
    half = head // 2
    k_heads = keys.shape[-1] // (2 * head)
    q_heads = queries.shape[-1] // head
    q_cols = raw.shape[-1]
    loads = Loads(in_sem)
    early = [
        loads.start(piece, act.at[pl.ds(at * rows, rows)]) for at, piece in enumerate(pieces)
    ]
    stream = Stream(
        []
        if resident
        else [
            pltpu.make_async_copy(
                wo.at[0, leg, pl.ds(at * head, head), :], wbuf.at[at], w_sem.at[at]
            )
            for at in range(q_heads)
        ]
    )
    waits = [loads.start(q_gain, gain_held)]
    waits += load_chunks(loads, queries_hbm, queries)
    waits += load_chunks(loads, chunks_hbm, keys)
    raw_cols = pl.ds(raw_hbm[0].shape[-1] - q_cols, q_cols)
    waits += load_chunks(loads, [part.at[:, raw_cols] for part in raw_hbm], raw)
    cos, sin = rotation(row_places(piece_bases(groups, cores, chips, rows), rows, half), head)
    bias = mask_of(groups, key_layout, cores, chips, rows, reaches)
    for copy in early:
        copy.wait()
    for h in range(q_heads):
        if resident:
            head_rows = wo[pl.ds(h * head, head), :]
        else:
            stream.wait(h)
            head_rows = wbuf[h]
        context_grad[:, pl.ds(h * head, head)] = lax.dot_general(
            act[...], head_rows, contract_last, preferred_element_type=f32
        ).astype(bf16)
    for copy in waits:
        copy.wait()
    gain_row = gain_held[0, pl.ds(leg, 1), :]
    outs = []

    def send(source, target):
        copy = pltpu.make_async_copy(source, target, out_sem.at[len(outs)])
        copy.start()
        outs.append(copy)

    own = grads.shape[0]
    for h in range(q_heads):
        key_at = h * k_heads // q_heads
        first = h == 0 or (h - 1) * k_heads // q_heads != key_at
        last = h == q_heads - 1 or (h + 1) * k_heads // q_heads != key_at
        key_cols = pl.ds(key_at * head, head)
        value_cols = pl.ds((k_heads + key_at) * head, head)
        query_cols = pl.ds(h * head, head)
        query = queries[:, query_cols]
        upper = context_grad[:, query_cols]
        weights = weights_of(query, keys[:, key_cols], bias)
        weight_grad = lax.dot_general(
            upper, keys[:, value_cols], contract_last, preferred_element_type=f32
        )
        inner = jnp.sum(weight_grad * weights, axis=-1, keepdims=True)
        score_grad = (weights * (weight_grad - inner) * head ** (-0.5)).astype(bf16)
        query_grad = jnp.dot(score_grad, keys[:, key_cols], preferred_element_type=f32)
        key_term = lax.dot_general(score_grad, query, contract_first, preferred_element_type=f32)
        value_term = lax.dot_general(
            weights.astype(bf16), upper, contract_first, preferred_element_type=f32
        )
        for cols, term in ((key_cols, key_term), (value_cols, value_term)):
            if not first:
                term = term + grads[:, cols]
            if not last:
                grads[:, cols] = term
                continue
            sent[:, cols] = term.astype(bf16)
            start = 0
            for at, target in enumerate(grads_hbm):
                size = target.shape[0]
                here = pl.ds(start, size)
                if at < halves:
                    grads[here, cols] = term[start : start + size]
                    send(grads.at[here, cols], target.at[:, cols])
                else:
                    send(sent.at[here, cols], target.at[:, cols])
                start += size
        query_low[:, query_cols] = head_back(
            raw[:, query_cols], gain_row, cos, sin, query_grad
        ).astype(bf16)
        send(query_low.at[:, query_cols], low_hbm.at[:, query_cols])
    for copy in outs:
        copy.wait()


def attend_back(which, layout, key_layout, reaches, pieces, queries, raw, chunks, q_gain, wo, covers=False):
    total = sum(part.shape[0] for part in queries)
    q_cols = queries[0].shape[-1]
    head = q_gain.shape[-1]
    keys = sum(chunk.shape[0] for chunk in chunks)
    cols = chunks[0].shape[-1]
    width = wo.shape[-1]
    k_heads = cols // (2 * head)
    q_heads = q_cols // head
    halves = len(key_layout)
    inputs = len(pieces) + 2 * halves + len(chunks) + 1
    resident = wo.ndim == 2
    return pl.pallas_call(
        functools.partial(attend_back_kernel, which, layout, key_layout, reaches),
        out_shape=[jax.ShapeDtypeStruct((total, q_cols), bf16)]
        + [
            jax.ShapeDtypeStruct(chunk.shape, f32 if at < halves else bf16)
            for at, chunk in enumerate(chunks)
        ],
        in_specs=[anywhere] * inputs + [whole if resident else anywhere],
        out_specs=[anywhere] * (1 + len(chunks)),
        scratch_shapes=[
            pltpu.VMEM((total, q_cols), bf16),
            pltpu.VMEM((total, q_cols), f32),
            pltpu.VMEM((keys, cols), bf16),
            pltpu.VMEM((keys, cols), f32),
            pltpu.VMEM((keys, cols), bf16),
            pltpu.VMEM(q_gain.shape, f32),
            pltpu.VMEM((total, q_cols), bf16),
            pltpu.VMEM((total, width), bf16),
            pltpu.VMEM((total, q_cols), bf16),
        ]
        + [pltpu.VMEM((q_heads, head, width), bf16)] * (not resident)
        + [pltpu.SemaphoreType.DMA((inputs,))]
        + [pltpu.SemaphoreType.DMA((q_heads,))] * (not resident)
        + [pltpu.SemaphoreType.DMA((2 * k_heads * len(chunks) + q_heads,))],
        compiler_params=params(36 if resident else 49),
        cost_estimate=cost(covers),
        name="attend_back",
    )(*pieces, *queries, *raw, *chunks, q_gain, wo)


contract_last = (((1,), (1,)), ((), ()))
contract_first = (((0,), (0,)), ((), ()))


def row_streams(leg, weights, buffers, sem):
    slots, tile = buffers[0].shape[:2]
    return [
        Stream(
            [
                pltpu.make_async_copy(
                    weight.at[0, leg, pl.ds(at * tile, tile), :],
                    buffer.at[at % slots],
                    sem.at[j, at],
                )
                for at in range(weight.shape[-2] // tile)
            ]
        )
        for j, (weight, buffer) in enumerate(zip(weights, buffers))
    ]


def query_hidden_kernel(which, parts, query_hbm, wq, *refs):
    outs, refs = refs[: len(parts)], refs[len(parts) :]
    query, buffer, held, in_sem, w_sem, out_sem = refs
    copy = pltpu.make_async_copy(query_hbm, query, in_sem)
    copy.start()
    (stream,) = row_streams(own_leg(which), [wq], [buffer], w_sem)
    slots, tile = buffer.shape[:2]
    copy.wait()
    copies = []
    for at in range(wq.shape[-2] // tile):
        stream.wait(at)
        cols = pl.ds(at * tile, tile)
        held[:, cols] = lax.dot_general(
            query[...], buffer[at % slots], contract_last, preferred_element_type=f32
        )
        start = 0
        for j, size in enumerate(parts):
            copy = pltpu.make_async_copy(
                held.at[pl.ds(start, size), cols], outs[j].at[:, cols], out_sem.at[j, at]
            )
            copy.start()
            copies.append(copy)
            start += size
    for copy in copies:
        copy.wait()


def query_hidden(which, parts, query_low, wq, covers=False):
    total, q_cols = query_low.shape
    width = wq.shape[-2]
    tile = widest_tile(width)
    tiles = width // tile
    return pl.pallas_call(
        functools.partial(query_hidden_kernel, which, parts),
        out_shape=[jax.ShapeDtypeStruct((size, width), f32) for size in parts],
        in_specs=[anywhere] * 2,
        out_specs=[anywhere] * len(parts),
        scratch_shapes=[
            pltpu.VMEM((total, q_cols), bf16),
            pltpu.VMEM((min(3, tiles), tile, q_cols), bf16),
            pltpu.VMEM((total, width), f32),
            pltpu.SemaphoreType.DMA,
            pltpu.SemaphoreType.DMA((1, tiles)),
            pltpu.SemaphoreType.DMA((len(parts), tiles)),
        ],
        compiler_params=params(49),
        cost_estimate=cost(covers),
        name="query_hidden",
    )(query_low, wq)


def hidden_kernel(which, layout, rows, *refs):
    groups, cores, chips = layout
    (part_hbm, own_hbm, received_hbm, raw_hbm, k_gain, wk, wv), refs = refs[:7], refs[7:]
    outs, refs = refs[:cores], refs[cores:]
    (part, own, received, raw, gain_held, key_low, value_low, bk, bv, held), refs = (
        refs[:10],
        refs[10:],
    )
    in_sem, w_sem, out_sem = refs
    leg = own_leg(which)
    slots, tile = bk.shape[:2]
    loads = Loads(in_sem)
    waits = [
        loads.start(received_hbm, received),
        loads.start(own_hbm, own),
        loads.start(raw_hbm.at[:, pl.ds(0, raw.shape[-1])], raw),
        loads.start(k_gain, gain_held),
    ]
    streams = row_streams(leg, (wk, wv), (bk, bv), w_sem)
    part_wait = loads.start(part_hbm, part)
    head = k_gain.shape[-1]
    k_cols = raw.shape[-1]
    cos, sin = rotation(
        row_places(piece_bases(groups, cores, chips, rows), rows, head // 2), head
    )
    for copy in waits:
        copy.wait()
    gain_row = gain_held[0, pl.ds(leg, 1), :]
    for h in range(k_cols // head):
        cols = pl.ds(h * head, head)
        grad = own[:, cols] + received[:, cols].astype(f32)
        key_low[:, cols] = head_back(raw[:, cols], gain_row, cos, sin, grad).astype(bf16)
    value_cols = pl.ds(k_cols, k_cols)
    value_low[...] = (own[:, value_cols] + received[:, value_cols].astype(f32)).astype(bf16)
    split = SplitOut(held, outs, out_sem, len(groups), cores, rows, tile)
    for at in range(wk.shape[-2] // tile):
        for stream in streams:
            stream.wait(at)
        slot = at % slots
        value = lax.dot_general(
            key_low[...], bk[slot], contract_last, preferred_element_type=f32
        )
        value += lax.dot_general(
            value_low[...], bv[slot], contract_last, preferred_element_type=f32
        )
        if at == 0:
            part_wait.wait()
        split.write(at, value + part[:, pl.ds(at * tile, tile)])
    split.wait()


def hidden(which, layout, rows, part, own, received, raw, k_gain, wk, wv, covers=False):
    cores = layout[1]
    count = own.shape[0]
    width = wk.shape[-2]
    k_cols = wk.shape[-1]
    tile = widest_tile(width)
    tiles = width // tile
    slots = min(3, tiles)
    return pl.pallas_call(
        functools.partial(hidden_kernel, which, layout, rows),
        out_shape=[jax.ShapeDtypeStruct((count // cores, width), bf16)] * cores,
        in_specs=[anywhere] * 7,
        out_specs=[anywhere] * cores,
        scratch_shapes=[
            pltpu.VMEM(part.shape, part.dtype),
            pltpu.VMEM(own.shape, own.dtype),
            pltpu.VMEM(received.shape, received.dtype),
            pltpu.VMEM((count, k_cols), f32),
            pltpu.VMEM(k_gain.shape, f32),
            pltpu.VMEM((count, k_cols), bf16),
            pltpu.VMEM((count, k_cols), bf16),
            pltpu.VMEM((slots, tile, k_cols), bf16),
            pltpu.VMEM((slots, tile, k_cols), bf16),
            pltpu.VMEM((cores, count // cores, width), bf16),
            pltpu.SemaphoreType.DMA((5,)),
            pltpu.SemaphoreType.DMA((2, tiles)),
            pltpu.SemaphoreType.DMA((cores, tiles)),
        ],
        compiler_params=params(49),
        cost_estimate=cost(covers),
        name="hidden_grad",
    )(part, own, received, raw, k_gain, wk, wv)


class Group:
    def __init__(self):
        self.size = lax.axis_size("tp")
        self.cores = 2 if self.size % 2 == 0 else 1
        self.chips = self.size // self.cores
        index = lax.axis_index("tp")
        self.chip = index // self.cores
        self.core = index % self.cores

    def place(self, chip, core):
        return (chip % self.chips) * self.cores + core % self.cores

    def to_chip(self, value, ahead):
        pairs = [
            (self.place(chip, core), self.place(chip + ahead, core))
            for chip in range(self.chips)
            for core in range(self.cores)
        ]
        return lax.ppermute(value, "tp", pairs)

    def to_core(self, value, ahead):
        pairs = [
            (self.place(chip, core), self.place(chip, core + ahead))
            for chip in range(self.chips)
            for core in range(self.cores)
        ]
        return lax.ppermute(value, "tp", pairs)

    def spread(self, piece):
        return [piece] + [self.to_core(piece, -k) for k in range(1, self.cores)]

    def positions(self, groups, rows, block):
        inner = jnp.arange(rows, dtype=jnp.int32)
        parts = []
        for g in groups:
            for k in range(self.cores):
                owner = ((self.chip + g) % self.chips) * self.cores + (self.core + k) % self.cores
                parts.append((block * self.size + owner) * rows + inner)
        return jnp.concatenate(parts)


def after(value, *others):
    return lax.optimization_barrier((value,) + others)[0]


def shifted(value, by, first):
    size = lax.axis_size("ctx")
    pairs = [(i, i + by) for i in range(size) if 0 <= i + by < size and i >= first]
    return lax.ppermute(value, "ctx", pairs)


def passed_along(value, by):
    size = lax.axis_size("ctx")
    return lax.ppermute(value, "ctx", [(i, i + by) for i in range(size - by)])


def swapped(value):
    pairs = [(source, source ^ 1) for source in range(lax.axis_size("segment"))]
    return lax.ppermute(value, "segment", pairs)


def per_device(
    stash_inputs,
    stash_grads,
    plan,
    query_weight,
    key_weight,
    value_weight,
    out_weight,
    input_gain,
    output_gain,
    query_gain,
    key_gain,
):
    ahead, behind = 0, 1
    group = Group()
    cores, chips = group.cores, group.chips
    rows = stash_inputs.shape[2]
    head = query_gain.shape[-1]
    block_rows = rows * group.size
    reaches = min(WINDOW // block_rows, lax.axis_size("ctx") - 1)
    near_groups = (0,)
    far_groups = tuple(range(1, chips))
    near = (near_groups, cores, chips)
    far = (far_groups, cores, chips)
    every = (near_groups + far_groups, cores, chips)
    everything = (key_weight, value_weight, query_weight)
    gains = (query_gain, key_gain)

    def chip_pieces(value):
        return [group.to_chip(value, -g) for g in far_groups]

    def all_pieces(pieces):
        spread = []
        for piece in pieces:
            spread += group.spread(piece)
        return spread

    back_normed, ahead_normed = norm_rows(plan, stash_inputs, input_gain)
    back_far = chip_pieces(back_normed)
    back_near = group.spread(back_normed)
    kv_near, q_near, raw_near = project(
        behind, near, back_near, *gains, *everything, True, covers=True, first=True
    )
    near_chain = [kv_near]
    back_far = [after(piece, q_near) for piece in back_far]
    ahead_far = chip_pieces(after(ahead_normed, *back_far))
    far_pieces = all_pieces(back_far)
    if reaches > 0:
        near_chain.append(shifted(kv_near, 1, 0))
    kv_far, q_far, raw_far = project(
        behind, far, far_pieces, *gains, *everything, True, covers=True
    )
    kv_sent = after(kv_far, *near_chain)
    near_chain[-1] = after(near_chain[-1], *ahead_far)
    ahead_far = [after(piece, kv_far) for piece in ahead_far]
    ahead_pieces = group.spread(after(ahead_normed, kv_far)) + all_pieces(ahead_far)
    (kv_ahead,) = project(
        ahead, every, ahead_pieces, *gains, *everything, False, covers=True, parts=("kv",)
    )
    far_chain = [kv_far]
    q_ahead = None
    for step in range(1, reaches + 1):
        far_chain.append(shifted(kv_sent, 1, step - 1))
        if step < reaches:
            near_chain.append(shifted(after(near_chain[-1], kv_far), 1, step))
        if step == 2:
            (q_ahead,) = project(
                ahead,
                every,
                [after(ahead_pieces[0], kv_ahead, kv_sent)] + ahead_pieces[1:],
                *gains,
                *everything,
                False,
                covers=True,
                parts=("q",),
            )
        kv_sent = far_chain[-1]
        if step < reaches:
            beside = kv_ahead if q_ahead is None else q_ahead
            kv_sent = after(kv_sent, beside)
            near_chain[-1] = after(near_chain[-1], beside)
    if q_ahead is None:
        (q_ahead,) = project(
            ahead, every, ahead_pieces, *gains, *everything, False, parts=("q",)
        )
    out_rows = lax.dynamic_index_in_dim(
        after(out_weight, q_ahead, *far_chain[:-1])[0],
        1 - lax.axis_index("segment"),
        0,
        keepdims=False,
    )
    far_chain[-1] = after(far_chain[-1], out_rows)

    back_chunks = []
    for pair in zip(near_chain, far_chain):
        back_chunks += pair
    back_keys = (near_groups, far_groups)
    far_keep, far_send = attend(
        behind,
        far,
        back_keys,
        reaches,
        q_far,
        back_chunks,
        out_rows,
        head,
        rows,
    )
    far_sums = far_parts(group, rows, far_keep, far_send)
    far_terms = [group.to_chip(part, g) for g, part in zip(far_groups, far_sums)]
    near_keep, near_send = attend(
        behind,
        near,
        back_keys,
        reaches,
        after(q_near, far_sums[0]),
        back_chunks,
        out_rows,
        head,
        rows,
        covers=True,
    )
    ahead_chain = [kv_ahead]
    if reaches > 0:
        ahead_chain.append(shifted(after(kv_ahead, far_sums[0]), 1, 0))
    near_keep = after(near_keep, *far_terms, *ahead_chain)
    back_terms = [near_keep, group.to_core(near_send, 1)] + far_terms
    out_grad = finish_rows(
        "grad", behind, plan, back_terms, stash_inputs, stash_grads, output_gain
    )
    grad_far = chip_pieces(out_grad)
    grad_near = group.spread(out_grad)
    if reaches > 1:
        ahead_chain.append(shifted(after(ahead_chain[1], out_grad), 1, 1))
    for step in range(3, reaches + 1):
        ahead_chain.append(shifted(ahead_chain[-1], 1, step - 1))

    results = attend_back(
        behind,
        every,
        back_keys,
        reaches,
        grad_near + all_pieces(grad_far),
        (q_near, q_far),
        (raw_near, raw_far),
        back_chunks,
        query_gain,
        out_rows,
    )
    query_low = results[0]
    near_grads = results[1::2]
    far_grads = results[2::2]
    near_rows = near_grads[0].shape[0]
    near_part, far_part = query_hidden(
        behind, (near_rows, query_low.shape[0] - near_rows), query_low, query_weight, covers=True
    )

    def added(message, grads, distance):
        return (message.astype(f32) + grads[distance].astype(f32)).astype(bf16)

    far_back = after(far_grads[reaches], *ahead_chain[:3])
    near_back = after(near_grads[reaches], *ahead_chain[:3])
    near_sent = near_back
    beside = near_part
    near_hops = {}
    ahead_keep = None
    for distance in range(reaches, 0, -1):
        near_sent = near_back
        far_back = shifted(far_back, -1, distance)
        if distance in near_hops:
            near_back = near_hops[distance]
        else:
            near_back = shifted(near_back, -1, distance)
        if distance == 1:
            break
        far_back = added(after(far_back, beside), far_grads, distance - 1)
        near_back = added(after(near_back, beside), near_grads, distance - 1)
        if ahead_keep is None:
            ahead_keep, ahead_send = attend(
                ahead,
                every,
                (near_groups + far_groups,),
                reaches,
                after(q_ahead, far_back, near_back),
                ahead_chain,
                out_weight,
                head,
                rows,
                covers=True,
            )
            beside = ahead_keep
            late_near = shifted(near_back, -1, distance - 1)
            ahead_send = after(ahead_send, late_near)
            near_hops[distance - 1] = late_near
    if ahead_keep is None:
        ahead_keep, ahead_send = attend(
            ahead,
            every,
            (near_groups + far_groups,),
            reaches,
            after(q_ahead, near_part),
            ahead_chain,
            out_weight,
            head,
            rows,
        )
    ahead_sums = far_parts(group, rows, ahead_keep[rows:], ahead_send[rows:])
    ahead_terms = [ahead_keep[:rows], group.to_core(ahead_send[:rows], 1)] + [
        group.to_chip(part, g) for g, part in zip(far_groups, ahead_sums)
    ]

    kv_weights = (key_weight, value_weight)
    far_back = after(far_back, near_sent, *ahead_sums)
    far_keep, far_send = hidden(
        behind,
        far,
        rows,
        far_part,
        far_grads[0],
        far_back,
        raw_far,
        key_gain,
        *kv_weights,
        covers=True,
    )
    far_send = after(far_send, near_back, *ahead_terms[2:])
    far_sums = far_parts(group, rows, far_keep, far_send)
    halves = ((0, rows // 2), (rows // 2, rows // 2))
    half_terms = [
        [
            group.to_chip(part[begin : begin + count], g)
            for g, part in zip(far_groups, far_sums)
        ]
        for begin, count in halves
    ]
    forward_out = finish_rows(
        "forward",
        ahead,
        plan,
        [after(ahead_terms[0], far_sums[0])] + ahead_terms[1:],
        stash_inputs,
        stash_grads,
        output_gain,
    )
    arrived_act = swapped(forward_out)
    near_keep, near_send = hidden(
        behind,
        near,
        rows,
        after(near_part, forward_out),
        near_grads[0],
        after(near_back, far_sums[0]),
        raw_near,
        key_gain,
        *kv_weights,
        covers=True,
    )
    near_send = after(near_send, arrived_act, *half_terms[0], *half_terms[1])
    near_terms = [near_keep, group.to_core(near_send, 1)]
    arrived_halves = []
    for half, terms in zip(halves, half_terms):
        outgoing = finish_rows(
            "outgoing",
            behind,
            plan,
            near_terms + terms,
            stash_inputs,
            stash_grads,
            input_gain,
            half=half,
        )
        arrived_halves.append(swapped(outgoing))
    arrived_grad = jnp.concatenate(arrived_halves, axis=0)
    arrived_act = copied(arrived_act)
    return (arrived_act[None], arrived_grad[None])


def far_parts(group, rows, far_keep, far_send):
    far = far_keep.astype(f32) + group.to_core(far_send, 1).astype(f32)
    far = far.astype(bf16)
    return [far[(g - 1) * rows : g * rows] for g in range(1, group.chips)]


def solution(mesh):
    return jax.shard_map(
        per_device,
        mesh=mesh,
        in_specs=(
            P("segment", None, ("ctx", "tp"), None),
            P("segment", None, ("ctx", "tp"), None),
            P("segment", None),
            P("segment", None, None, "tp"),
            P("segment", None, None, "tp"),
            P("segment", None, None, "tp"),
            P("segment", None, "tp", None),
            P("segment", None, None),
            P("segment", None, None),
            P("segment", None, None),
            P("segment", None, None),
        ),
        out_specs=(P("segment", ("ctx", "tp"), None), P("segment", ("ctx", "tp"), None)),
        check_vma=False,
    )
```

```python
import functools
import math

import jax
import jax.numpy as jnp
from jax import lax
from jax.experimental import pallas as pl
from jax.experimental.pallas import tpu as pltpu
from jax.sharding import PartitionSpec as P

WINDOW = 1024

epsilon = 1e-06
rope_base = 10000.0
masked_score = -1e30
mebibyte = 1024 * 1024
f32 = jnp.float32
bf16 = jnp.bfloat16

whole = pl.BlockSpec(memory_space=pltpu.VMEM)
scalars = pl.BlockSpec(memory_space=pltpu.SMEM)
anywhere = pl.BlockSpec(memory_space=pl.ANY)


def params(mebibytes):
    return pltpu.CompilerParams(vmem_limit_bytes=int(mebibytes * mebibyte))


class Stream:
    def __init__(self, copies):
        self.copies = copies
        for copy in copies[:2]:
            copy.start()

    def wait(self, at):
        self.copies[at].wait()
        if at + 2 < len(self.copies):
            self.copies[at + 2].start()


def cost(covers):
    size = 64 * mebibyte if covers else 1
    return pl.CostEstimate(flops=1, bytes_accessed=size, transcendentals=0)


def widest_tile(width, limit=1024):
    best = 128
    for tile in range(128, limit + 1, 128):
        if width % tile == 0:
            best = tile
    return best


class Loads:
    def __init__(self, sem):
        self.sem = sem
        self.count = 0

    def start(self, source, target):
        copy = pltpu.make_async_copy(source, target, self.sem.at[self.count])
        copy.start()
        self.count += 1
        return copy


def own_leg(other):
    index = lax.axis_index("segment")
    return 1 - index if other else index


def piece_bases(groups, cores, chips, rows):
    index = lax.axis_index("tp")
    chip = index // cores
    core = index % cores
    begin = lax.axis_index("ctx") * (chips * cores * rows)
    return [
        begin + (((chip + g) % chips) * cores + (core + k) % cores) * rows
        for g in groups
        for k in range(cores)
    ]


def row_places(bases, rows, width):
    return jnp.concatenate(
        [lax.broadcasted_iota(jnp.int32, (rows, width), 0) + base for base in bases], axis=0
    )


def lane_places(bases, rows, back):
    shape = (1, len(bases) * rows)
    lane = lax.broadcasted_iota(jnp.int32, shape, 1)
    place = lane + (bases[0] - back)
    for at in range(1, len(bases)):
        place = jnp.where(lane >= at * rows, lane + (bases[at] - at * rows - back), place)
    return place


def rotation(places, head):
    lane = lax.broadcasted_iota(jnp.int32, places.shape, 1).astype(f32)
    angles = places.astype(f32) * jnp.exp(lane * (-2.0 / head * math.log(rope_base)))
    return jnp.cos(angles), jnp.sin(angles)


def mean_square_scale(value):
    return lax.rsqrt(jnp.mean(value * value, axis=-1, keepdims=True) + epsilon)


def norm_back(value, gain, grad):
    scale = mean_square_scale(value)
    weighted = grad * gain
    inner = jnp.mean(value * weighted, axis=-1, keepdims=True)
    return scale * weighted - value * (scale * scale * scale * inner)


def norm_kernel(plan, stash, gain, first, second, held, gain_held, picks, normed, sem, out_sem):
    loads = Loads(sem)
    waits = [
        loads.start(plan, picks),
        loads.start(stash.at[0], held),
        loads.start(gain, gain_held),
    ]
    for copy in waits:
        copy.wait()
    copies = []
    for which, out in ((1, first), (0, second)):
        value = held[picks[0, which]].astype(f32)
        scaled = value * mean_square_scale(value)
        normed[which] = (scaled * gain_held[0, pl.ds(own_leg(which), 1), :]).astype(bf16)
        copy = pltpu.make_async_copy(normed.at[which], out, out_sem.at[which])
        copy.start()
        copies.append(copy)
    for copy in copies:
        copy.wait()


def norm_rows(plan, stash, gain, covers=False):
    rows, width = stash.shape[-2:]
    shape = jax.ShapeDtypeStruct((rows, width), bf16)
    return pl.pallas_call(
        norm_kernel,
        out_shape=[shape, shape],
        in_specs=[anywhere] * 3,
        out_specs=[anywhere] * 2,
        scratch_shapes=[
            pltpu.VMEM(stash.shape[1:], bf16),
            pltpu.VMEM(gain.shape, f32),
            pltpu.SMEM(plan.shape, plan.dtype),
            pltpu.VMEM((2, rows, width), bf16),
            pltpu.SemaphoreType.DMA((3,)),
            pltpu.SemaphoreType.DMA((2,)),
        ],
        compiler_params=params(62.5),
        cost_estimate=cost(covers),
        name="norm_rows",
    )(plan, stash, gain)


def qkv_kernel(which, layout, parts, keep_raw, *refs):
    groups, cores, chips = layout
    count = len(groups) * cores
    pieces, refs = refs[:count], refs[count:]
    (q_gain, k_gain, wk, wv, wq), refs = refs[:5], refs[5:]
    names = [name for name in ("kv", "q") if name in parts] + ["raw"] * keep_raw
    outs, refs = dict(zip(names, refs)), refs[len(names) :]
    results, refs = dict(zip(names, refs)), refs[len(names) :]
    act, gains, wbuf, in_sem, w_sem, out_sem = refs
    leg = own_leg(which)
    head = q_gain.shape[-1]
    rows = pieces[0].shape[0]
    k_heads = wk.shape[-1] // head
    tiles = []
    for kind, weight in (("k", wk), ("v", wv), ("q", wq)):
        if (kind == "q") != ("q" in parts) and len(parts) == 1:
            continue
        for at in range(weight.shape[-1] // head):
            tiles.append((kind, weight, at))
    slots = wbuf.shape[0]
    stream = Stream(
        [
            pltpu.make_async_copy(
                weight.at[0, leg, :, pl.ds(h * head, head)], wbuf.at[at % slots], w_sem.at[at]
            )
            for at, (kind, weight, h) in enumerate(tiles)
        ]
    )
    loads = Loads(in_sem)
    waits = [
        loads.start(piece, act.at[pl.ds(at * rows, rows)]) for at, piece in enumerate(pieces)
    ]
    waits += [loads.start(gain, gains.at[at]) for at, gain in enumerate((q_gain, k_gain))]
    half = head // 2
    bases = piece_bases(groups, cores, chips, rows)
    cos, sin = rotation(row_places(bases, rows, half), head)
    for copy in waits:
        copy.wait()
    row_gains = {
        "q": gains[0, 0, pl.ds(leg, 1), :],
        "k": gains[1, 0, pl.ds(leg, 1), :],
    }
    copies = []

    def send(array, column, at):
        cols = pl.ds(column * head, head)
        copy = pltpu.make_async_copy(
            results[array].at[:, cols], outs[array].at[:, cols], out_sem.at[int(array == "raw"), at]
        )
        copy.start()
        copies.append(copy)

    for at, (kind, weight, h) in enumerate(tiles):
        stream.wait(at)
        raw = jnp.dot(act[...], wbuf[at % slots], preferred_element_type=f32)
        column = h if kind != "v" else k_heads + h
        array = "q" if kind == "q" else "kv"
        begin = column * head
        if kind == "v":
            results[array][:, pl.ds(begin, head)] = raw.astype(bf16)
        else:
            if keep_raw:
                raw_column = h if kind == "k" else k_heads + h
                results["raw"][:, pl.ds(raw_column * head, head)] = raw
                send("raw", raw_column, at)
            normed = raw * mean_square_scale(raw) * row_gains[kind]
            front = normed[:, :half]
            back = normed[:, half:]
            results[array][:, pl.ds(begin, half)] = (front * cos - back * sin).astype(bf16)
            results[array][:, pl.ds(begin + half, half)] = (back * cos + front * sin).astype(bf16)
        send(array, column, at)
    for copy in copies:
        copy.wait()


def project(which, layout, pieces, q_gain, k_gain, wk, wv, wq, keep_raw, covers=False, first=False, parts=("kv", "q")):
    rows, width = pieces[0].shape
    total = rows * len(pieces)
    head = q_gain.shape[-1]
    q_cols, k_cols = wq.shape[-1], wk.shape[-1]
    forms = [((total, 2 * k_cols), bf16)] * ("kv" in parts)
    forms += [((total, q_cols), bf16)] * ("q" in parts)
    tiles = sum(form[0][1] for form in forms) // head
    if keep_raw:
        forms.append(((total, k_cols + q_cols), f32))
    return pl.pallas_call(
        functools.partial(qkv_kernel, which, layout, parts, keep_raw),
        out_shape=[jax.ShapeDtypeStruct(*form) for form in forms],
        in_specs=[anywhere] * (len(pieces) + 5),
        out_specs=[anywhere] * len(forms),
        scratch_shapes=[pltpu.VMEM(*form) for form in forms]
        + [
            pltpu.VMEM((total, width), bf16),
            pltpu.VMEM((2,) + q_gain.shape, f32),
            pltpu.VMEM((3, width, head), bf16),
            pltpu.SemaphoreType.DMA((len(pieces) + 2,)),
            pltpu.SemaphoreType.DMA((tiles,)),
            pltpu.SemaphoreType.DMA((2, tiles)),
        ],
        compiler_params=params(57 if first else 49),
        cost_estimate=cost(covers),
        name="project_heads",
    )(*pieces, q_gain, k_gain, wk, wv, wq)


def visibility(query_place, key_place):
    seen = (
        (key_place >= 0) & (key_place <= query_place) & (key_place > query_place - WINDOW)
    )
    return jnp.where(seen, 0.0, masked_score).astype(f32)


def mask_of(q_groups, key_layout, cores, chips, rows, reaches):
    block = chips * cores * rows
    query_place = row_places(piece_bases(q_groups, cores, chips, rows), rows, 1)
    parts = []
    for distance in range(reaches + 1):
        for groups in key_layout:
            bases = piece_bases(groups, cores, chips, rows)
            parts.append(
                visibility(query_place, lane_places(bases, rows, distance * block))
            )
    return jnp.concatenate(parts, axis=1)


def weights_of(queries, keys, bias):
    scores = lax.dot_general(queries, keys, contract_last, preferred_element_type=f32)
    value = scores * queries.shape[-1] ** (-0.5) + bias
    raised = jnp.exp(value - jnp.max(value, axis=-1, keepdims=True))
    return raised * (1.0 / jnp.sum(raised, axis=-1, keepdims=True))


def load_chunks(loads, sources, held):
    waits = []
    start = 0
    for source in sources:
        size = source.shape[0]
        waits.append(loads.start(source, held.at[pl.ds(start, size)]))
        start += size
    return waits


def split_rows(value, groups, cores, rows):
    parts = []
    for g in range(groups):
        for k in range(cores):
            begin = (g * cores + k) * rows
            parts.append((k, g * rows, value[begin : begin + rows]))
    return parts


class SplitOut:
    def __init__(self, held, outs, sem, groups, cores, rows, tile):
        self.held, self.outs, self.sem = held, outs, sem
        self.groups, self.cores, self.rows, self.tile = groups, cores, rows, tile
        self.copies = []

    def write(self, at, value):
        cols = pl.ds(at * self.tile, self.tile)
        for k, begin, part in split_rows(value, self.groups, self.cores, self.rows):
            self.held[k, pl.ds(begin, self.rows), cols] = part.astype(bf16)
        for k in range(self.cores):
            copy = pltpu.make_async_copy(
                self.held.at[k, :, cols], self.outs[k].at[:, cols], self.sem.at[k, at]
            )
            copy.start()
            self.copies.append(copy)

    def wait(self):
        for copy in self.copies:
            copy.wait()


def attend_kernel(which, layout, key_layout, reaches, rows, head, *refs):
    groups, cores, chips = layout
    count = len(key_layout) * (reaches + 1)
    queries_hbm = refs[0]
    chunks_hbm = refs[1 : 1 + count]
    wo = refs[1 + count]
    outs = refs[2 + count : 2 + count + cores]
    refs = refs[2 + count + cores :]
    if len(wo.shape) == 2:
        queries, keys, context, held, in_sem, out_sem = refs
        wbuf = None
    else:
        queries, keys, context, wbuf, held, in_sem, w_sem, out_sem = refs
    leg = own_leg(which)
    loads = Loads(in_sem)
    waits = [loads.start(queries_hbm, queries)]
    waits += load_chunks(loads, chunks_hbm, keys)
    tile = widest_tile(wo.shape[-1])
    tiles = wo.shape[-1] // tile
    stream = Stream(
        []
        if wbuf is None
        else [
            pltpu.make_async_copy(
                wo.at[0, leg, :, pl.ds(at * tile, tile)], wbuf.at[at], w_sem.at[at]
            )
            for at in range(tiles)
        ]
    )
    k_heads = keys.shape[-1] // (2 * head)
    q_heads = queries.shape[-1] // head
    bias = mask_of(groups, key_layout, cores, chips, rows, reaches)
    for copy in waits:
        copy.wait()
    for h in range(q_heads):
        key_at = h * k_heads // q_heads
        key_cols = pl.ds(key_at * head, head)
        value_cols = pl.ds((k_heads + key_at) * head, head)
        weights = weights_of(queries[:, pl.ds(h * head, head)], keys[:, key_cols], bias)
        context[:, pl.ds(h * head, head)] = jnp.dot(
            weights.astype(bf16), keys[:, value_cols], preferred_element_type=f32
        ).astype(bf16)
        if wbuf is not None:
            stream.wait(h)
    split = SplitOut(held, outs, out_sem, len(groups), cores, rows, tile)
    for at in range(tiles):
        if wbuf is None:
            tile_rows = wo[:, pl.ds(at * tile, tile)]
        else:
            if at >= q_heads:
                stream.wait(at)
            tile_rows = wbuf[at]
        split.write(at, jnp.dot(context[...], tile_rows, preferred_element_type=f32))
    split.wait()


def attend(which, layout, key_layout, reaches, queries, chunks, wo, head, rows, covers=False):
    cores = layout[1]
    total, q_cols = queries.shape
    keys = sum(chunk.shape[0] for chunk in chunks)
    width = wo.shape[-1]
    tile = widest_tile(width)
    resident = wo.ndim == 2
    shape = jax.ShapeDtypeStruct((total // cores, width), bf16)
    return pl.pallas_call(
        functools.partial(attend_kernel, which, layout, key_layout, reaches, rows, head),
        out_shape=[shape] * cores,
        in_specs=[anywhere] * (len(chunks) + 1) + [whole if resident else anywhere],
        out_specs=[anywhere] * cores,
        scratch_shapes=[
            pltpu.VMEM((total, q_cols), bf16),
            pltpu.VMEM((keys, chunks[0].shape[-1]), bf16),
            pltpu.VMEM((total, q_cols), bf16),
        ]
        + [pltpu.VMEM((width // tile, q_cols, tile), bf16)] * (not resident)
        + [
            pltpu.VMEM((cores, total // cores, width), bf16),
            pltpu.SemaphoreType.DMA((len(chunks) + 1,)),
        ]
        + [pltpu.SemaphoreType.DMA((width // tile,))] * (not resident)
        + [pltpu.SemaphoreType.DMA((cores, width // tile))],
        compiler_params=params(36 if resident else 49),
        cost_estimate=cost(covers),
        name="attend_and_project",
    )(queries, *chunks, wo)


def summed(terms, begin, count):
    total = None
    for term in terms:
        at = begin if term.shape[0] > count else 0
        value = term[pl.ds(at, count), :].astype(f32)
        total = value if total is None else total + value
    return total


def row_kernel(kind, which, number, begin, plan, *refs):
    terms = refs[:number]
    stash, grads, gain, out, held, grad_held, gain_held, sem = refs[number:]
    batch = plan[0, which]
    count = out.shape[0]
    here = pl.ds(begin, count)
    loads = Loads(sem)
    waits = [loads.start(gain, gain_held)]
    if kind != "grad":
        waits.append(loads.start(stash.at[0, batch, here], held))
    if kind != "forward":
        waits.append(loads.start(grads.at[0, batch, here], grad_held))
    total = summed(terms, begin, count)
    for copy in waits:
        copy.wait()
    gain_row = gain_held[0, pl.ds(own_leg(which), 1), :]
    if kind == "grad":
        result = norm_back(total, gain_row, grad_held[...].astype(f32))
    elif kind == "forward":
        result = held[...].astype(f32) + total * mean_square_scale(total) * gain_row
    else:
        back = norm_back(held[...].astype(f32), gain_row, total)
        result = grad_held[...].astype(f32) + back
    out[...] = result.astype(bf16)


def finish_rows(kind, which, plan, terms, stash, grads, gain, half=None, covers=False):
    rows, width = stash.shape[-2:]
    begin, count = (0, rows) if half is None else half
    return pl.pallas_call(
        functools.partial(row_kernel, kind, which, len(terms), begin),
        out_shape=jax.ShapeDtypeStruct((count, width), bf16),
        in_specs=[scalars] + [whole] * len(terms) + [anywhere] * 3,
        out_specs=whole,
        scratch_shapes=[
            pltpu.VMEM((count, width), bf16),
            pltpu.VMEM((count, width), bf16),
            pltpu.VMEM(gain.shape, f32),
            pltpu.SemaphoreType.DMA((3,)),
        ],
        compiler_params=params(8),
        cost_estimate=cost(covers),
        name=kind + "_rows",
    )(plan, *terms, stash, grads, gain)


def copy_kernel(source, target, sem):
    copy = pltpu.make_async_copy(source, target, sem)
    copy.start()
    copy.wait()


def copied(value):
    return pl.pallas_call(
        copy_kernel,
        out_shape=jax.ShapeDtypeStruct(value.shape, value.dtype),
        in_specs=[anywhere],
        out_specs=anywhere,
        scratch_shapes=[pltpu.SemaphoreType.DMA],
        compiler_params=params(8),
        cost_estimate=cost(False),
        name="copied",
    )(value)


def head_back(raw, gain_row, cos, sin, grad):
    half = grad.shape[-1] // 2
    front = grad[:, :half]
    back = grad[:, half:]
    turned = jnp.concatenate([front * cos + back * sin, back * cos - front * sin], axis=-1)
    return norm_back(raw, gain_row, turned)


def attend_back_kernel(which, layout, key_layout, reaches, *refs):
    groups, cores, chips = layout
    pieces_count = len(groups) * cores
    halves = len(key_layout)
    count = halves * (reaches + 1)
    pieces, refs = refs[:pieces_count], refs[pieces_count:]
    queries_hbm, refs = refs[:halves], refs[halves:]
    raw_hbm, refs = refs[:halves], refs[halves:]
    chunks_hbm, refs = refs[:count], refs[count:]
    (q_gain, wo, low_hbm), refs = refs[:3], refs[3:]
    grads_hbm, refs = refs[:count], refs[count:]
    (queries, raw, keys, grads, sent), refs = refs[:5], refs[5:]
    resident = len(wo.shape) == 2
    if resident:
        (gain_held, query_low, act, context_grad, in_sem, out_sem) = refs
    else:
        (gain_held, query_low, act, context_grad, wbuf, in_sem, w_sem, out_sem) = refs
    leg = own_leg(which)
    rows = pieces[0].shape[0]
    head = q_gain.shape[-1]
    half = head // 2
    k_heads = keys.shape[-1] // (2 * head)
    q_heads = queries.shape[-1] // head
    q_cols = raw.shape[-1]
    loads = Loads(in_sem)
    early = [
        loads.start(piece, act.at[pl.ds(at * rows, rows)]) for at, piece in enumerate(pieces)
    ]
    stream = Stream(
        []
        if resident
        else [
            pltpu.make_async_copy(
                wo.at[0, leg, pl.ds(at * head, head), :], wbuf.at[at], w_sem.at[at]
            )
            for at in range(q_heads)
        ]
    )
    waits = [loads.start(q_gain, gain_held)]
    waits += load_chunks(loads, queries_hbm, queries)
    waits += load_chunks(loads, chunks_hbm, keys)
    raw_cols = pl.ds(raw_hbm[0].shape[-1] - q_cols, q_cols)
    waits += load_chunks(loads, [part.at[:, raw_cols] for part in raw_hbm], raw)
    cos, sin = rotation(row_places(piece_bases(groups, cores, chips, rows), rows, half), head)
    bias = mask_of(groups, key_layout, cores, chips, rows, reaches)
    for copy in early:
        copy.wait()
    for h in range(q_heads):
        if resident:
            head_rows = wo[pl.ds(h * head, head), :]
        else:
            stream.wait(h)
            head_rows = wbuf[h]
        context_grad[:, pl.ds(h * head, head)] = lax.dot_general(
            act[...], head_rows, contract_last, preferred_element_type=f32
        ).astype(bf16)
    for copy in waits:
        copy.wait()
    gain_row = gain_held[0, pl.ds(leg, 1), :]
    outs = []

    def send(source, target):
        copy = pltpu.make_async_copy(source, target, out_sem.at[len(outs)])
        copy.start()
        outs.append(copy)

    own = grads.shape[0]
    for h in range(q_heads):
        key_at = h * k_heads // q_heads
        first = h == 0 or (h - 1) * k_heads // q_heads != key_at
        last = h == q_heads - 1 or (h + 1) * k_heads // q_heads != key_at
        key_cols = pl.ds(key_at * head, head)
        value_cols = pl.ds((k_heads + key_at) * head, head)
        query_cols = pl.ds(h * head, head)
        query = queries[:, query_cols]
        upper = context_grad[:, query_cols]
        weights = weights_of(query, keys[:, key_cols], bias)
        weight_grad = lax.dot_general(
            upper, keys[:, value_cols], contract_last, preferred_element_type=f32
        )
        inner = jnp.sum(weight_grad * weights, axis=-1, keepdims=True)
        score_grad = (weights * (weight_grad - inner) * head ** (-0.5)).astype(bf16)
        query_grad = jnp.dot(score_grad, keys[:, key_cols], preferred_element_type=f32)
        key_term = lax.dot_general(score_grad, query, contract_first, preferred_element_type=f32)
        value_term = lax.dot_general(
            weights.astype(bf16), upper, contract_first, preferred_element_type=f32
        )
        for cols, term in ((key_cols, key_term), (value_cols, value_term)):
            if not first:
                term = term + grads[:, cols]
            if not last:
                grads[:, cols] = term
                continue
            sent[:, cols] = term.astype(bf16)
            start = 0
            for at, target in enumerate(grads_hbm):
                size = target.shape[0]
                here = pl.ds(start, size)
                if at < halves:
                    grads[here, cols] = term[start : start + size]
                    send(grads.at[here, cols], target.at[:, cols])
                else:
                    send(sent.at[here, cols], target.at[:, cols])
                start += size
        query_low[:, query_cols] = head_back(
            raw[:, query_cols], gain_row, cos, sin, query_grad
        ).astype(bf16)
        send(query_low.at[:, query_cols], low_hbm.at[:, query_cols])
    for copy in outs:
        copy.wait()


def attend_back(which, layout, key_layout, reaches, pieces, queries, raw, chunks, q_gain, wo, covers=False):
    total = sum(part.shape[0] for part in queries)
    q_cols = queries[0].shape[-1]
    head = q_gain.shape[-1]
    keys = sum(chunk.shape[0] for chunk in chunks)
    cols = chunks[0].shape[-1]
    width = wo.shape[-1]
    k_heads = cols // (2 * head)
    q_heads = q_cols // head
    halves = len(key_layout)
    inputs = len(pieces) + 2 * halves + len(chunks) + 1
    resident = wo.ndim == 2
    return pl.pallas_call(
        functools.partial(attend_back_kernel, which, layout, key_layout, reaches),
        out_shape=[jax.ShapeDtypeStruct((total, q_cols), bf16)]
        + [
            jax.ShapeDtypeStruct(chunk.shape, f32 if at < halves else bf16)
            for at, chunk in enumerate(chunks)
        ],
        in_specs=[anywhere] * inputs + [whole if resident else anywhere],
        out_specs=[anywhere] * (1 + len(chunks)),
        scratch_shapes=[
            pltpu.VMEM((total, q_cols), bf16),
            pltpu.VMEM((total, q_cols), f32),
            pltpu.VMEM((keys, cols), bf16),
            pltpu.VMEM((keys, cols), f32),
            pltpu.VMEM((keys, cols), bf16),
            pltpu.VMEM(q_gain.shape, f32),
            pltpu.VMEM((total, q_cols), bf16),
            pltpu.VMEM((total, width), bf16),
            pltpu.VMEM((total, q_cols), bf16),
        ]
        + [pltpu.VMEM((q_heads, head, width), bf16)] * (not resident)
        + [pltpu.SemaphoreType.DMA((inputs,))]
        + [pltpu.SemaphoreType.DMA((q_heads,))] * (not resident)
        + [pltpu.SemaphoreType.DMA((2 * k_heads * len(chunks) + q_heads,))],
        compiler_params=params(36 if resident else 49),
        cost_estimate=cost(covers),
        name="attend_back",
    )(*pieces, *queries, *raw, *chunks, q_gain, wo)


contract_last = (((1,), (1,)), ((), ()))
contract_first = (((0,), (0,)), ((), ()))


def row_streams(leg, weights, buffers, sem):
    slots, tile = buffers[0].shape[:2]
    return [
        Stream(
            [
                pltpu.make_async_copy(
                    weight.at[0, leg, pl.ds(at * tile, tile), :],
                    buffer.at[at % slots],
                    sem.at[j, at],
                )
                for at in range(weight.shape[-2] // tile)
            ]
        )
        for j, (weight, buffer) in enumerate(zip(weights, buffers))
    ]


def query_hidden_kernel(which, parts, query_hbm, wq, *refs):
    outs, refs = refs[: len(parts)], refs[len(parts) :]
    query, buffer, held, in_sem, w_sem, out_sem = refs
    copy = pltpu.make_async_copy(query_hbm, query, in_sem)
    copy.start()
    (stream,) = row_streams(own_leg(which), [wq], [buffer], w_sem)
    slots, tile = buffer.shape[:2]
    copy.wait()
    copies = []
    for at in range(wq.shape[-2] // tile):
        stream.wait(at)
        cols = pl.ds(at * tile, tile)
        held[:, cols] = lax.dot_general(
            query[...], buffer[at % slots], contract_last, preferred_element_type=f32
        )
        start = 0
        for j, size in enumerate(parts):
            copy = pltpu.make_async_copy(
                held.at[pl.ds(start, size), cols], outs[j].at[:, cols], out_sem.at[j, at]
            )
            copy.start()
            copies.append(copy)
            start += size
    for copy in copies:
        copy.wait()


def query_hidden(which, parts, query_low, wq, covers=False):
    total, q_cols = query_low.shape
    width = wq.shape[-2]
    tile = widest_tile(width)
    tiles = width // tile
    return pl.pallas_call(
        functools.partial(query_hidden_kernel, which, parts),
        out_shape=[jax.ShapeDtypeStruct((size, width), f32) for size in parts],
        in_specs=[anywhere] * 2,
        out_specs=[anywhere] * len(parts),
        scratch_shapes=[
            pltpu.VMEM((total, q_cols), bf16),
            pltpu.VMEM((min(3, tiles), tile, q_cols), bf16),
            pltpu.VMEM((total, width), f32),
            pltpu.SemaphoreType.DMA,
            pltpu.SemaphoreType.DMA((1, tiles)),
            pltpu.SemaphoreType.DMA((len(parts), tiles)),
        ],
        compiler_params=params(49),
        cost_estimate=cost(covers),
        name="query_hidden",
    )(query_low, wq)


def hidden_kernel(which, layout, rows, *refs):
    groups, cores, chips = layout
    (part_hbm, own_hbm, received_hbm, raw_hbm, k_gain, wk, wv), refs = refs[:7], refs[7:]
    outs, refs = refs[:cores], refs[cores:]
    (part, own, received, raw, gain_held, key_low, value_low, bk, bv, held), refs = (
        refs[:10],
        refs[10:],
    )
    in_sem, w_sem, out_sem = refs
    leg = own_leg(which)
    slots, tile = bk.shape[:2]
    loads = Loads(in_sem)
    waits = [
        loads.start(received_hbm, received),
        loads.start(own_hbm, own),
        loads.start(raw_hbm.at[:, pl.ds(0, raw.shape[-1])], raw),
        loads.start(k_gain, gain_held),
    ]
    streams = row_streams(leg, (wk, wv), (bk, bv), w_sem)
    part_wait = loads.start(part_hbm, part)
    head = k_gain.shape[-1]
    k_cols = raw.shape[-1]
    cos, sin = rotation(
        row_places(piece_bases(groups, cores, chips, rows), rows, head // 2), head
    )
    for copy in waits:
        copy.wait()
    gain_row = gain_held[0, pl.ds(leg, 1), :]
    for h in range(k_cols // head):
        cols = pl.ds(h * head, head)
        grad = own[:, cols] + received[:, cols].astype(f32)
        key_low[:, cols] = head_back(raw[:, cols], gain_row, cos, sin, grad).astype(bf16)
    value_cols = pl.ds(k_cols, k_cols)
    value_low[...] = (own[:, value_cols] + received[:, value_cols].astype(f32)).astype(bf16)
    split = SplitOut(held, outs, out_sem, len(groups), cores, rows, tile)
    for at in range(wk.shape[-2] // tile):
        for stream in streams:
            stream.wait(at)
        slot = at % slots
        value = lax.dot_general(
            key_low[...], bk[slot], contract_last, preferred_element_type=f32
        )
        value += lax.dot_general(
            value_low[...], bv[slot], contract_last, preferred_element_type=f32
        )
        if at == 0:
            part_wait.wait()
        split.write(at, value + part[:, pl.ds(at * tile, tile)])
    split.wait()


def hidden(which, layout, rows, part, own, received, raw, k_gain, wk, wv, covers=False):
    cores = layout[1]
    count = own.shape[0]
    width = wk.shape[-2]
    k_cols = wk.shape[-1]
    tile = widest_tile(width)
    tiles = width // tile
    slots = min(3, tiles)
    return pl.pallas_call(
        functools.partial(hidden_kernel, which, layout, rows),
        out_shape=[jax.ShapeDtypeStruct((count // cores, width), bf16)] * cores,
        in_specs=[anywhere] * 7,
        out_specs=[anywhere] * cores,
        scratch_shapes=[
            pltpu.VMEM(part.shape, part.dtype),
            pltpu.VMEM(own.shape, own.dtype),
            pltpu.VMEM(received.shape, received.dtype),
            pltpu.VMEM((count, k_cols), f32),
            pltpu.VMEM(k_gain.shape, f32),
            pltpu.VMEM((count, k_cols), bf16),
            pltpu.VMEM((count, k_cols), bf16),
            pltpu.VMEM((slots, tile, k_cols), bf16),
            pltpu.VMEM((slots, tile, k_cols), bf16),
            pltpu.VMEM((cores, count // cores, width), bf16),
            pltpu.SemaphoreType.DMA((5,)),
            pltpu.SemaphoreType.DMA((2, tiles)),
            pltpu.SemaphoreType.DMA((cores, tiles)),
        ],
        compiler_params=params(49),
        cost_estimate=cost(covers),
        name="hidden_grad",
    )(part, own, received, raw, k_gain, wk, wv)


class Group:
    def __init__(self):
        self.size = lax.axis_size("tp")
        self.cores = 2 if self.size % 2 == 0 else 1
        self.chips = self.size // self.cores
        index = lax.axis_index("tp")
        self.chip = index // self.cores
        self.core = index % self.cores

    def place(self, chip, core):
        return (chip % self.chips) * self.cores + core % self.cores

    def to_chip(self, value, ahead):
        pairs = [
            (self.place(chip, core), self.place(chip + ahead, core))
            for chip in range(self.chips)
            for core in range(self.cores)
        ]
        return lax.ppermute(value, "tp", pairs)

    def to_core(self, value, ahead):
        pairs = [
            (self.place(chip, core), self.place(chip, core + ahead))
            for chip in range(self.chips)
            for core in range(self.cores)
        ]
        return lax.ppermute(value, "tp", pairs)

    def spread(self, piece):
        return [piece] + [self.to_core(piece, -k) for k in range(1, self.cores)]

    def positions(self, groups, rows, block):
        inner = jnp.arange(rows, dtype=jnp.int32)
        parts = []
        for g in groups:
            for k in range(self.cores):
                owner = ((self.chip + g) % self.chips) * self.cores + (self.core + k) % self.cores
                parts.append((block * self.size + owner) * rows + inner)
        return jnp.concatenate(parts)


def after(value, *others):
    return lax.optimization_barrier((value,) + others)[0]


def shifted(value, by, first):
    size = lax.axis_size("ctx")
    pairs = [(i, i + by) for i in range(size) if 0 <= i + by < size and i >= first]
    return lax.ppermute(value, "ctx", pairs)


def passed_along(value, by):
    size = lax.axis_size("ctx")
    return lax.ppermute(value, "ctx", [(i, i + by) for i in range(size - by)])


def swapped(value):
    pairs = [(source, source ^ 1) for source in range(lax.axis_size("segment"))]
    return lax.ppermute(value, "segment", pairs)


def per_device(
    stash_inputs,
    stash_grads,
    plan,
    query_weight,
    key_weight,
    value_weight,
    out_weight,
    input_gain,
    output_gain,
    query_gain,
    key_gain,
):
    ahead, behind = 0, 1
    group = Group()
    cores, chips = group.cores, group.chips
    rows = stash_inputs.shape[2]
    head = query_gain.shape[-1]
    block_rows = rows * group.size
    reaches = min(WINDOW // block_rows, lax.axis_size("ctx") - 1)
    near_groups = (0,)
    far_groups = tuple(range(1, chips))
    near = (near_groups, cores, chips)
    far = (far_groups, cores, chips)
    every = (near_groups + far_groups, cores, chips)
    everything = (key_weight, value_weight, query_weight)
    gains = (query_gain, key_gain)

    def chip_pieces(value):
        return [group.to_chip(value, -g) for g in far_groups]

    def all_pieces(pieces):
        spread = []
        for piece in pieces:
            spread += group.spread(piece)
        return spread

    back_normed, ahead_normed = norm_rows(plan, stash_inputs, input_gain)
    back_far = chip_pieces(back_normed)
    back_near = group.spread(back_normed)
    kv_near, q_near, raw_near = project(
        behind, near, back_near, *gains, *everything, True, covers=True, first=True
    )
    near_chain = [kv_near]
    back_far = [after(piece, q_near) for piece in back_far]
    ahead_far = chip_pieces(after(ahead_normed, *back_far))
    far_pieces = all_pieces(back_far)
    if reaches > 0:
        near_chain.append(shifted(kv_near, 1, 0))
    kv_far, q_far, raw_far = project(
        behind, far, far_pieces, *gains, *everything, True, covers=True
    )
    kv_sent = after(kv_far, *near_chain)
    near_chain[-1] = after(near_chain[-1], *ahead_far)
    ahead_far = [after(piece, kv_far) for piece in ahead_far]
    ahead_pieces = group.spread(after(ahead_normed, kv_far)) + all_pieces(ahead_far)
    (kv_ahead,) = project(
        ahead, every, ahead_pieces, *gains, *everything, False, covers=True, parts=("kv",)
    )
    far_chain = [kv_far]
    q_ahead = None
    for step in range(1, reaches + 1):
        far_chain.append(shifted(kv_sent, 1, step - 1))
        if step < reaches:
            near_chain.append(shifted(after(near_chain[-1], kv_far), 1, step))
        if step == 2:
            (q_ahead,) = project(
                ahead,
                every,
                [after(ahead_pieces[0], kv_ahead, kv_sent)] + ahead_pieces[1:],
                *gains,
                *everything,
                False,
                covers=True,
                parts=("q",),
            )
        kv_sent = far_chain[-1]
        if step < reaches:
            beside = kv_ahead if q_ahead is None else q_ahead
            kv_sent = after(kv_sent, beside)
            near_chain[-1] = after(near_chain[-1], beside)
    if q_ahead is None:
        (q_ahead,) = project(
            ahead, every, ahead_pieces, *gains, *everything, False, parts=("q",)
        )
    out_rows = lax.dynamic_index_in_dim(
        after(out_weight, q_ahead, *far_chain[:-1])[0],
        1 - lax.axis_index("segment"),
        0,
        keepdims=False,
    )
    far_chain[-1] = after(far_chain[-1], out_rows)

    back_chunks = []
    for pair in zip(near_chain, far_chain):
        back_chunks += pair
    back_keys = (near_groups, far_groups)
    far_keep, far_send = attend(
        behind,
        far,
        back_keys,
        reaches,
        q_far,
        back_chunks,
        out_rows,
        head,
        rows,
    )
    far_sums = far_parts(group, rows, far_keep, far_send)
    far_terms = [group.to_chip(part, g) for g, part in zip(far_groups, far_sums)]
    near_keep, near_send = attend(
        behind,
        near,
        back_keys,
        reaches,
        after(q_near, far_sums[0]),
        back_chunks,
        out_rows,
        head,
        rows,
        covers=True,
    )
    ahead_chain = [kv_ahead]
    if reaches > 0:
        ahead_chain.append(shifted(after(kv_ahead, far_sums[0]), 1, 0))
    near_keep = after(near_keep, *far_terms, *ahead_chain)
    back_terms = [near_keep, group.to_core(near_send, 1)] + far_terms
    out_grad = finish_rows(
        "grad", behind, plan, back_terms, stash_inputs, stash_grads, output_gain
    )
    grad_far = chip_pieces(out_grad)
    grad_near = group.spread(out_grad)
    if reaches > 1:
        ahead_chain.append(shifted(after(ahead_chain[1], out_grad), 1, 1))
    for step in range(3, reaches + 1):
        ahead_chain.append(shifted(ahead_chain[-1], 1, step - 1))

    results = attend_back(
        behind,
        every,
        back_keys,
        reaches,
        grad_near + all_pieces(grad_far),
        (q_near, q_far),
        (raw_near, raw_far),
        back_chunks,
        query_gain,
        out_rows,
    )
    query_low = results[0]
    near_grads = results[1::2]
    far_grads = results[2::2]
    near_rows = near_grads[0].shape[0]
    near_part, far_part = query_hidden(
        behind, (near_rows, query_low.shape[0] - near_rows), query_low, query_weight, covers=True
    )

    def added(message, grads, distance):
        return (message.astype(f32) + grads[distance].astype(f32)).astype(bf16)

    far_back = after(far_grads[reaches], *ahead_chain[:3])
    near_back = after(near_grads[reaches], *ahead_chain[:3])
    near_sent = near_back
    beside = near_part
    near_hops = {}
    ahead_keep = None
    for distance in range(reaches, 0, -1):
        near_sent = near_back
        far_back = shifted(far_back, -1, distance)
        if distance in near_hops:
            near_back = near_hops[distance]
        else:
            near_back = shifted(near_back, -1, distance)
        if distance == 1:
            break
        far_back = added(after(far_back, beside), far_grads, distance - 1)
        near_back = added(after(near_back, beside), near_grads, distance - 1)
        if ahead_keep is None:
            ahead_keep, ahead_send = attend(
                ahead,
                every,
                (near_groups + far_groups,),
                reaches,
                after(q_ahead, far_back, near_back),
                ahead_chain,
                out_weight,
                head,
                rows,
                covers=True,
            )
            beside = ahead_keep
            late_near = shifted(near_back, -1, distance - 1)
            ahead_send = after(ahead_send, late_near)
            near_hops[distance - 1] = late_near
    if ahead_keep is None:
        ahead_keep, ahead_send = attend(
            ahead,
            every,
            (near_groups + far_groups,),
            reaches,
            after(q_ahead, near_part),
            ahead_chain,
            out_weight,
            head,
            rows,
        )
    ahead_sums = far_parts(group, rows, ahead_keep[rows:], ahead_send[rows:])
    ahead_terms = [ahead_keep[:rows], group.to_core(ahead_send[:rows], 1)] + [
        group.to_chip(part, g) for g, part in zip(far_groups, ahead_sums)
    ]

    kv_weights = (key_weight, value_weight)
    far_back = after(far_back, near_sent, *ahead_sums)
    far_keep, far_send = hidden(
        behind,
        far,
        rows,
        far_part,
        far_grads[0],
        far_back,
        raw_far,
        key_gain,
        *kv_weights,
        covers=True,
    )
    far_send = after(far_send, near_back, *ahead_terms[2:])
    far_sums = far_parts(group, rows, far_keep, far_send)
    halves = ((0, rows // 2), (rows // 2, rows // 2))
    far_terms = [group.to_chip(part, g) for g, part in zip(far_groups, far_sums)]
    forward_out = finish_rows(
        "forward",
        ahead,
        plan,
        [after(ahead_terms[0], far_sums[0])] + ahead_terms[1:],
        stash_inputs,
        stash_grads,
        output_gain,
    )
    arrived_act = swapped(forward_out)
    near_keep, near_send = hidden(
        behind,
        near,
        rows,
        after(near_part, forward_out),
        near_grads[0],
        after(near_back, far_sums[0]),
        raw_near,
        key_gain,
        *kv_weights,
        covers=True,
    )
    near_keep = after(near_keep, arrived_act, *far_terms)
    near_terms = [near_keep, group.to_core(near_send, 1)]
    arrived_halves = []
    for half in halves:
        outgoing = finish_rows(
            "outgoing",
            behind,
            plan,
            near_terms + far_terms,
            stash_inputs,
            stash_grads,
            input_gain,
            half=half,
        )
        arrived_halves.append(swapped(outgoing))
    arrived_grad = jnp.concatenate(arrived_halves, axis=0)
    arrived_act = copied(arrived_act)
    return (arrived_act[None], arrived_grad[None])


def far_parts(group, rows, far_keep, far_send):
    far = far_keep.astype(f32) + group.to_core(far_send, 1).astype(f32)
    far = far.astype(bf16)
    return [far[(g - 1) * rows : g * rows] for g in range(1, group.chips)]


def solution(mesh):
    return jax.shard_map(
        per_device,
        mesh=mesh,
        in_specs=(
            P("segment", None, ("ctx", "tp"), None),
            P("segment", None, ("ctx", "tp"), None),
            P("segment", None),
            P("segment", None, None, "tp"),
            P("segment", None, None, "tp"),
            P("segment", None, None, "tp"),
            P("segment", None, "tp", None),
            P("segment", None, None),
            P("segment", None, None),
            P("segment", None, None),
            P("segment", None, None),
        ),
        out_specs=(P("segment", ("ctx", "tp"), None), P("segment", ("ctx", "tp"), None)),
        check_vma=False,
    )
```
